32 devices in a mesh: dp: 8 (over z, x), tensor: 4 (over y, core).
Axes of the slice: x: 2, y: 2, z: 4, core: 2. Of those that a mesh axis runs over, the one named last changes fastest.
Arguments:
- tokens: bfloat16 [8192, 1024], P(('dp', 'tensor')), may hold values from -24 to 24
- cotangent: bfloat16 [8192, 1024], P(('dp', 'tensor')), may hold values from -6 to 6
- bucket_start: int32 [32], replicated, may hold values from 0 to 30, as said below
- w_qkv: bfloat16 [1024, 3072], P(('dp', 'tensor')), may hold values from -0.1875 to 0.1875
- w_out: bfloat16 [1024, 1024], P(('dp', 'tensor')), may hold values from -0.1875 to 0.1875
- s_qk: bfloat16 [1024], P(('dp', 'tensor')), may hold values from 0.796875 to 1.59375
- alpha_a: bfloat16 [1024], P(('dp', 'tensor')), may hold values from 0.14941406 to 0.59765625
- alpha_m: bfloat16 [1024], P(('dp', 'tensor')), may hold values from 0.14941406 to 0.59765625
- w_up: bfloat16 [1024, 4096], P('dp', 'tensor'), may hold values from -0.1875 to 0.1875
- w_gate: bfloat16 [1024, 4096], P('dp', 'tensor'), may hold values from -0.1875 to 0.1875
- w_down: bfloat16 [1024, 4096], P('dp', 'tensor'), may hold values from -0.09375 to 0.09375
- s_u: bfloat16 [4096], P('tensor'), may hold values from 0.5 to 2
- s_v: bfloat16 [4096], P('tensor'), may hold values from 0.5 to 2
Outputs:
- layer_out: bfloat16 [8192, 1024], P(('dp', 'tensor'))
- grad_tokens: bfloat16 [8192, 1024], P(('dp', 'tensor'))
- grad_w_qkv: float32 [1024, 3072], P(('dp', 'tensor'))
- grad_w_out: float32 [1024, 1024], P(('dp', 'tensor'))
- grad_s_qk: float32 [1024], P(('dp', 'tensor'))
- grad_alpha_a: float32 [1024], P(('dp', 'tensor'))
- grad_alpha_m: float32 [1024], P(('dp', 'tensor'))
- grad_w_up: float32 [1024, 4096], P('dp', 'tensor')
- grad_w_gate: float32 [1024, 4096], P('dp', 'tensor')
- grad_w_down: float32 [1024, 4096], P('dp', 'tensor')
- grad_s_u: float32 [4096], P('tensor')
- grad_s_v: float32 [4096], P('tensor')
- stream_rms: float32 [3], replicated
The draws below stay inside these ranges and needn't reach their ends.
Inputs may be any that keep to these rules, and one draw needn't show every extreme that they name: Buckets are the aligned runs of 256 token rows, and groups the aligned runs of 4 buckets. A sequence is either all 4 buckets of a group or two buckets 2i and 2i + 1 of one group; bucket_start names the first bucket of the sequence. Half of the 8 groups, rounded up, are each one sequence; the last group is always made of two-bucket sequences, and which of the others are whole changes with the seed.
All inputs are finite; a program needn't handle non-finite values.
Results may differ from the reference program's by a relative error of at most 0.018.
Values may be sent and summed in bfloat16 or wider, within the bound.
A program may use at most 192 MiB of HBM per device.

```python
import math
import jax
import jax.numpy as jnp
from jax import lax

HEADS = 16
HEAD_DIM = 64
D = 1024
FF = 4096
TOK_DEV = 256
GROUPS = 8
SPAN = 4
BUCKETS = 32
GSIZE = 1024
TOKENS = 8192
N_DP = 8


def draw_bucket_start(key, part):
    key = jax.random.fold_in(key, 7)
    order = jax.random.permutation(key, GROUPS - 1)
    long_first = order < (GROUPS + 1) // 2
    long_group = jnp.concatenate([long_first, jnp.zeros((1,), dtype=bool)])
    bucket = jnp.arange(BUCKETS, dtype=jnp.int32)
    group_of = bucket // SPAN
    whole = group_of * SPAN
    paired = bucket - bucket % 2
    return jnp.where(long_group[group_of], whole, paired).astype(jnp.int32)


def rising_rows(key, entries, top_factor):
    place = jnp.arange(TOKENS, dtype=jnp.float32) / (TOKENS - 1)
    jitter = jax.random.uniform(jax.random.fold_in(key, 5), (TOKENS,), jnp.float32, 0.85, 1.15)
    scale = jnp.exp(math.log(top_factor) * place) * jitter
    return entries * scale[:, None]


def draw_tokens(key, part):
    key = jax.random.fold_in(key, 11)
    base = jnp.clip(jax.random.normal(key, (TOKENS, D), jnp.float32), -3.4, 3.4)
    values = rising_rows(key, base, 6.0)
    return values.astype(jnp.bfloat16)


def block_scale(rng, extent, cuts, least, largest):
    factor_of, own = 1.0, jax.random.fold_in(rng, 6)
    for axis_at, blocks in cuts:
        draws = jnp.exp(jax.random.uniform(jax.random.fold_in(own, axis_at), (blocks,), jnp.float32, least / len(cuts), largest / len(cuts)))
        factor_of = factor_of * jnp.repeat(draws, extent[axis_at] // blocks).reshape([-1 if axis == axis_at else 1 for axis in range(len(extent))])
    return factor_of


def scatter_about(own_key, shape, scale, limit, pieces=(), kind=jnp.bfloat16):
    factor_of = block_scale(own_key, shape, pieces, -0.22, 0.18) if pieces else 1.0
    array = jax.random.normal(own_key, shape, jnp.float32) * scale * factor_of
    return jnp.minimum(jnp.maximum(array, -limit), limit).astype(kind)


def setup_inputs(seed: int = 0) -> dict:
    key_of = jax.random.split(jax.random.key(seed), 14)
    return {
        "tokens": draw_tokens(jax.random.fold_in(key_of[13], 71), 0),
        "cotangent": scatter_about(key_of[1], (TOKENS, D), 1.0, 6.0, ((0, 32),)),
        "bucket_start": draw_bucket_start(jax.random.fold_in(key_of[13], 71), 0),
        "w_qkv": scatter_about(key_of[3], (D, 3 * D), D ** -0.5, 0.1875, ((0, 32),)),
        "w_out": scatter_about(key_of[4], (D, D), D ** -0.5, 0.1875, ((0, 32),)),
        "s_qk": jnp.clip(jnp.exp(math.log(1.59375) - 0.6931472 * jax.random.uniform(key_of[5], (D,), jnp.float32) ** block_scale(key_of[5], (D,), ((0, 32),), -0.2, 0.2)), 0.796875, 1.59375).astype(jnp.bfloat16),
        "alpha_a": jnp.clip(0.14941406 + 0.4482422 * jax.random.uniform(key_of[6], (D,), jnp.float32) ** block_scale(key_of[6], (D,), ((0, 32),), -0.2, 0.2), 0.14941406, 0.59765625).astype(jnp.bfloat16),
        "alpha_m": jnp.clip(0.14941406 + 0.4482422 * jax.random.uniform(key_of[7], (D,), jnp.float32) ** block_scale(key_of[7], (D,), ((0, 32),), -0.2, 0.2), 0.14941406, 0.59765625).astype(jnp.bfloat16),
        "w_up": scatter_about(key_of[8], (D, FF), D ** -0.5, 0.1875, ((0, 8), (1, 4))),
        "w_gate": scatter_about(key_of[9], (D, FF), D ** -0.5, 0.1875, ((0, 8), (1, 4))),
        "w_down": scatter_about(key_of[10], (D, FF), FF ** -0.5, 0.09375, ((0, 8), (1, 4))),
        "s_u": jnp.clip(jnp.exp(math.log(2.0) - 1.3862944 * jax.random.uniform(key_of[11], (FF,), jnp.float32) ** block_scale(key_of[11], (FF,), ((0, 4),), -0.2, 0.2)), 0.5, 2.0).astype(jnp.bfloat16),
        "s_v": jnp.clip(jnp.exp(math.log(2.0) - 1.3862944 * jax.random.uniform(key_of[12], (FF,), jnp.float32) ** block_scale(key_of[12], (FF,), ((0, 4),), -0.2, 0.2)), 0.5, 2.0).astype(jnp.bfloat16),
    }


@jax.custom_vjp
def low(v):
    return lax.optimization_barrier(v.astype(jnp.bfloat16)).astype(jnp.float32)

@jax.custom_vjp
def low_back(v):
    return v

def low_keep(v):
    return (low(v), None)

def low_pass(kept, grad):
    return (grad,)

def back_keep(v):
    return (v, None)

def back_low(kept, grad):
    return (low(grad),)
low.defvjp(low_keep, low_pass)
low_back.defvjp(back_keep, back_low)
EPSILON = 1e-06
MASKED_SCORE = -1e+30
HIGHEST = lax.Precision.HIGHEST

def rms_rows(value):
    return value * lax.rsqrt(lax.optimization_barrier(jnp.mean(value * value, axis=-1, keepdims=True)) + EPSILON)

def unit_heads(value):
    shaped = value.reshape(value.shape[0], HEADS, HEAD_DIM)
    factor = lax.rsqrt(lax.optimization_barrier(jnp.sum(shaped * shaped, axis=-1, keepdims=True)) + EPSILON)
    return (shaped * factor).reshape(value.shape)

def attend_group(packed):
    query, keys, values, seq_ids = packed
    block_rows = min(512, GSIZE)
    blocks = GSIZE // block_rows
    key_heads = keys.reshape(GSIZE, HEADS, HEAD_DIM)
    value_heads = values.reshape(GSIZE, HEADS, HEAD_DIM)
    positions = jnp.arange(GSIZE, dtype=jnp.int32)

    def one_block(inner):
        query_block, id_block, pos_block = inner
        scores = jnp.einsum('qhd,khd->hqk', query_block, key_heads, precision=HIGHEST) * math.sqrt(HEAD_DIM)
        scores = low_back(scores)
        allowed = (positions[None, :] <= pos_block[:, None]) & (seq_ids[None, :] == id_block[:, None])
        masked = jnp.where(allowed[None], scores, MASKED_SCORE)
        row_top = lax.optimization_barrier(jnp.max(masked, axis=-1, keepdims=True))
        expo = jnp.where(allowed[None], jnp.exp(masked - row_top), 0.0)
        probs = low(expo / lax.optimization_barrier(jnp.sum(expo, axis=-1, keepdims=True)))
        return jnp.einsum('hqk,khd->qhd', probs, value_heads, precision=HIGHEST)
    result = lax.map(jax.checkpoint(one_block), (query.reshape(blocks, block_rows, HEADS, HEAD_DIM), seq_ids.reshape(blocks, block_rows), positions.reshape(blocks, block_rows)))
    return result.reshape(GSIZE, HEADS * HEAD_DIM)

def reference(tokens, cotangent, bucket_start, w_qkv, w_out, s_qk, alpha_a, alpha_m, w_up, w_gate, w_down, s_u, s_v):
    width = HEADS * HEAD_DIM
    seq_ids = jnp.repeat(bucket_start.astype(jnp.int32), TOK_DEV).astype(jnp.int32)

    def forward_pass(inputs, qkv_weight, out_weight, gain_qk, mix_attn, mix_mlp, up_weight, gate_weight, down_weight, scale_up, scale_gate):
        qkv = low_back(jnp.dot(inputs, qkv_weight, precision=HIGHEST))
        query = low(unit_heads(qkv[:, :width]) * gain_qk)
        keys = low(unit_heads(qkv[:, width:2 * width]) * gain_qk)
        values = low(qkv[:, 2 * width:])
        attended = lax.map(jax.checkpoint(attend_group), (query.reshape(N_DP, GSIZE, width), keys.reshape(N_DP, GSIZE, width), values.reshape(N_DP, GSIZE, width), seq_ids.reshape(N_DP, GSIZE)))
        attended = low(low_back(attended.reshape(TOKENS, width)))
        branch_a = low_back(jnp.dot(attended, out_weight, precision=HIGHEST))
        h_attn = rms_rows(branch_a)
        resid_one = inputs + mix_attn * (h_attn - inputs)
        hidden_one = rms_rows(resid_one)
        rows_low = low(hidden_one)
        up_raw = low_back(jnp.dot(rows_low, up_weight, precision=HIGHEST))
        gate_raw = low_back(jnp.dot(rows_low, gate_weight, precision=HIGHEST))
        inner = low(up_raw * scale_up * jax.nn.silu(gate_raw * scale_gate))
        branch_m = low_back(jnp.dot(inner, down_weight.T, precision=HIGHEST))
        h_mlp = rms_rows(branch_m)
        resid_two = hidden_one + mix_mlp * (h_mlp - hidden_one)
        result = rms_rows(resid_two)
        sums = jnp.stack([jnp.sum(branch_a * branch_a), jnp.sum(branch_m * branch_m), jnp.sum(resid_two * resid_two)])
        return (result, sums)
    floats = tuple((arr.astype(jnp.float32) for arr in (tokens, w_qkv, w_out, s_qk, alpha_a, alpha_m, w_up, w_gate, w_down, s_u, s_v)))
    result, pull_back, sums = jax.vjp(forward_pass, *floats, has_aux=True)
    grads = pull_back(cotangent.astype(jnp.float32))
    stream_rms = jnp.sqrt(sums / (TOKENS * width))
    return (result.astype(jnp.bfloat16), grads[0].astype(jnp.bfloat16), grads[1], grads[2], grads[3], grads[4], grads[5], grads[6], grads[7], grads[8], grads[9], grads[10], stream_rms)
```

```python
import functools
import math

import jax
import jax.numpy as jnp
from jax import lax
from jax.experimental import pallas as pl
from jax.experimental.pallas import tpu as pltpu
from jax.sharding import PartitionSpec as P

HEAD_DIM = 64


EPSILON = 1e-06
MASKED_SCORE = -1e30


def rms_rows(value):
    return value * lax.rsqrt(jnp.mean(value * value, axis=-1, keepdims=True) + EPSILON)


def rms_back(upstream, normed, source):
    factor = lax.rsqrt(jnp.mean(source * source, axis=-1, keepdims=True) + EPSILON)
    return factor * (upstream - normed * jnp.mean(upstream * normed, axis=-1, keepdims=True))


def unit_heads(value):
    shaped = value.reshape(value.shape[0], -1, HEAD_DIM)
    factor = lax.rsqrt(jnp.sum(shaped * shaped, axis=-1, keepdims=True) + EPSILON)
    return ((shaped * factor).reshape(value.shape), factor)


def unit_back(upstream, normed, factor):
    upper_grad = upstream.reshape(normed.shape[0], -1, HEAD_DIM)
    normed_heads = normed.reshape(normed.shape[0], -1, HEAD_DIM)
    result = factor * (
        upper_grad - normed_heads * jnp.sum(upper_grad * normed_heads, axis=-1, keepdims=True)
    )
    return result.reshape(upstream.shape)


def block_span(total_rows, row_count):
    units = total_rows // row_count
    block_units = max(1, min(units, 512 // row_count))
    while units % block_units:
        block_units -= 1
    return row_count * block_units


def local(
    tokens,
    cotangent,
    bucket_start,
    w_qkv,
    w_out,
    s_qk,
    alpha_a,
    alpha_m,
    w_up,
    w_gate,
    w_down,
    s_u,
    s_v,
):
    row_count, model_width = tokens.shape
    head_count = model_width // HEAD_DIM
    score_scale = math.sqrt(HEAD_DIM)
    spread = lax.axis_size("tensor")
    group_rows = spread * row_count
    tensor_slot = lax.axis_index("tensor")
    qkv_full, out_full, gain_qk, mix_attn, mix_mlp = (
        lax.all_gather(w_qkv, ("dp", "tensor"), axis=0, tiled=True),
        lax.all_gather(w_out, ("dp", "tensor"), axis=0, tiled=True),
        lax.all_gather(s_qk, ("dp", "tensor"), axis=0, tiled=True),
        lax.all_gather(alpha_a, ("dp", "tensor"), axis=0, tiled=True),
        lax.all_gather(alpha_m, ("dp", "tensor"), axis=0, tiled=True),
    )
    up_full, gate_full, down_full = (
        lax.all_gather(w_up, "dp", axis=0, tiled=True),
        lax.all_gather(w_gate, "dp", axis=0, tiled=True),
        lax.all_gather(w_down, "dp", axis=0, tiled=True),
    )
    gain_qk = gain_qk.astype(jnp.float32)
    mix_attn = mix_attn.astype(jnp.float32)
    mix_mlp = mix_mlp.astype(jnp.float32)
    scale_up = s_u.astype(jnp.float32)
    scale_gate = s_v.astype(jnp.float32)
    starts = lax.dynamic_slice_in_dim(bucket_start, lax.axis_index("dp") * spread, spread)
    key_seq = jnp.repeat(starts, row_count)
    own_seq = starts[tensor_slot]
    query_pos = tensor_slot * row_count + jnp.arange(row_count, dtype=jnp.int32)

    def allowed(key_start, key_count):
        key_pos = key_start + jnp.arange(key_count, dtype=jnp.int32)
        seq_part = lax.dynamic_slice_in_dim(key_seq, key_start, key_count)
        return (key_pos[None, :] <= query_pos[:, None]) & (seq_part[None, :] == own_seq)

    inputs = tokens.astype(jnp.float32)
    qkv = jnp.dot(tokens, qkv_full, preferred_element_type=jnp.float32)
    q_unit, q_factor = unit_heads(qkv[:, :model_width])
    k_unit, k_factor = unit_heads(qkv[:, model_width : 2 * model_width])
    query_low = (q_unit * gain_qk).astype(jnp.bfloat16)
    keys_low = (k_unit * gain_qk).astype(jnp.bfloat16)
    values_low = qkv[:, 2 * model_width :].astype(jnp.bfloat16)
    query_heads = query_low.reshape(row_count, head_count, HEAD_DIM)
    key_all, value_all = (
        lax.all_gather(keys_low, "tensor", axis=0, tiled=True),
        lax.all_gather(values_low, "tensor", axis=0, tiled=True),
    )
    key_block = block_span(group_rows, row_count)
    blocks = group_rows // key_block

    def block_scores(key_source, key_start, key_count):
        key_part = lax.dynamic_slice_in_dim(key_source, key_start, key_count).reshape(
            key_count, head_count, HEAD_DIM
        )
        return (
            jnp.einsum("qhd,khd->hqk", query_heads, key_part, preferred_element_type=jnp.float32)
            * score_scale
        )

    def stat_step(state_pair, block_index):
        row_top, row_total = state_pair
        key_start = block_index * key_block
        allowed_keys = allowed(key_start, key_block)[None]
        masked = jnp.where(allowed_keys, block_scores(key_all, key_start, key_block), MASKED_SCORE)
        new_top = jnp.maximum(row_top, jnp.max(masked, axis=-1))
        fresh = jnp.where(allowed_keys, jnp.exp(masked - new_top[..., None]), 0.0)
        row_total = row_total * jnp.exp(row_top - new_top) + jnp.sum(fresh, axis=-1)
        return ((new_top, row_total), None)

    start_state = (
        jnp.full((head_count, row_count), MASKED_SCORE, jnp.float32),
        jnp.zeros((head_count, row_count), jnp.float32),
    )
    (row_top, row_total), _ = lax.scan(stat_step, start_state, jnp.arange(blocks))
    log_total = row_top + jnp.log(row_total)

    def probs_for(key_source, key_start, key_count):
        scores = block_scores(key_source, key_start, key_count)
        allowed_keys = allowed(key_start, key_count)[None]
        return jnp.where(allowed_keys, jnp.exp(scores - log_total[..., None]), 0.0)

    def value_part(value_source, key_start, key_count):
        return lax.dynamic_slice_in_dim(value_source, key_start, key_count).reshape(
            key_count, head_count, HEAD_DIM
        )

    def out_step(carry_sum, block_index):
        key_start = block_index * key_block
        attn_probs = probs_for(key_all, key_start, key_block).astype(jnp.bfloat16)
        term = jnp.einsum(
            "hqk,khd->qhd",
            attn_probs,
            value_part(value_all, key_start, key_block),
            preferred_element_type=jnp.float32,
        )
        return (carry_sum + term, None)

    attended, _ = lax.scan(
        out_step, jnp.zeros((row_count, head_count, HEAD_DIM), jnp.float32), jnp.arange(blocks)
    )
    attended_low = attended.reshape(row_count, model_width).astype(jnp.bfloat16)
    branch_a = jnp.dot(attended_low, out_full, preferred_element_type=jnp.float32)
    h_attn = rms_rows(branch_a)
    resid_one = inputs + mix_attn * (h_attn - inputs)
    hidden_one = rms_rows(resid_one)
    hidden_low = hidden_one.astype(jnp.bfloat16)
    rows_all = lax.all_gather(hidden_low, "tensor", axis=0, tiled=True)
    up_raw = jnp.dot(rows_all, up_full, preferred_element_type=jnp.float32)
    gate_raw = jnp.dot(rows_all, gate_full, preferred_element_type=jnp.float32)
    up_scaled = up_raw * scale_up
    gate_scaled = gate_raw * scale_gate
    gate_sigmoid = jax.nn.sigmoid(gate_scaled)
    silu_gate = gate_scaled * gate_sigmoid
    inner_low = (up_scaled * silu_gate).astype(jnp.bfloat16)
    branch_m = lax.psum_scatter(
        jnp.einsum("tf,df->td", inner_low, down_full, preferred_element_type=jnp.float32).astype(
            jnp.bfloat16
        ),
        "tensor",
        scatter_dimension=0,
        tiled=True,
    ).astype(jnp.float32)
    h_mlp = rms_rows(branch_m)
    resid_two = hidden_one + mix_mlp * (h_mlp - hidden_one)
    result = rms_rows(resid_two)
    partial_stats = jnp.stack(
        [jnp.sum(branch_a * branch_a), jnp.sum(branch_m * branch_m), jnp.sum(resid_two * resid_two)]
    )
    upstream = cotangent.astype(jnp.float32)
    d_resid_two = rms_back(upstream, result, resid_two)
    grad_mix_mlp = jnp.sum(d_resid_two * (h_mlp - hidden_one), axis=0)
    d_branch_m = rms_back(mix_mlp * d_resid_two, h_mlp, branch_m).astype(jnp.bfloat16)
    grads_all = lax.all_gather(d_branch_m, "tensor", axis=0, tiled=True)
    d_inner = jnp.dot(grads_all, down_full, preferred_element_type=jnp.float32)
    grad_up_scaled = d_inner * silu_gate
    grad_gate_scaled = (
        d_inner * up_scaled * gate_sigmoid * (1.0 + gate_scaled * (1.0 - gate_sigmoid))
    )
    grad_scale_up = jnp.sum(grad_up_scaled * up_raw, axis=0)
    grad_scale_gate = jnp.sum(grad_gate_scaled * gate_raw, axis=0)
    up_grad_low = (grad_up_scaled * scale_up).astype(jnp.bfloat16)
    gate_grad_low = (grad_gate_scaled * scale_gate).astype(jnp.bfloat16)
    grad_down = jnp.einsum("td,tf->df", grads_all, inner_low, preferred_element_type=jnp.float32)
    grad_up = jnp.einsum("td,tf->df", rows_all, up_grad_low, preferred_element_type=jnp.float32)
    grad_gate = jnp.einsum("td,tf->df", rows_all, gate_grad_low, preferred_element_type=jnp.float32)
    first = jnp.einsum("tf,df->td", up_grad_low, up_full, preferred_element_type=jnp.float32)
    d_hidden_one = (1.0 - mix_mlp) * d_resid_two + lax.psum_scatter(
        (
            first
            + jnp.einsum("tf,df->td", gate_grad_low, gate_full, preferred_element_type=jnp.float32)
        ).astype(jnp.bfloat16),
        "tensor",
        scatter_dimension=0,
        tiled=True,
    ).astype(jnp.float32)
    d_resid_one = rms_back(d_hidden_one, hidden_one, resid_one)
    grad_mix_attn = jnp.sum(d_resid_one * (h_attn - inputs), axis=0)
    d_branch_a = rms_back(mix_attn * d_resid_one, h_attn, branch_a).astype(jnp.bfloat16)
    grad_out = jnp.einsum("tc,td->cd", attended_low, d_branch_a, preferred_element_type=jnp.float32)
    d_attended = jnp.einsum(
        "td,cd->tc", d_branch_a, out_full, preferred_element_type=jnp.float32
    ).astype(jnp.bfloat16)
    d_heads = d_attended.reshape(row_count, head_count, HEAD_DIM)
    row_delta = jnp.sum(d_heads.astype(jnp.float32) * attended, axis=-1).T
    key_back, value_back = (
        lax.all_gather(keys_low, "tensor", axis=0, tiled=True),
        lax.all_gather(values_low, "tensor", axis=0, tiled=True),
    )

    def score_grads(key_start, key_count):
        attn_probs = probs_for(key_back, key_start, key_count)
        d_probs = jnp.einsum(
            "qhd,khd->hqk",
            d_heads,
            value_part(value_back, key_start, key_count),
            preferred_element_type=jnp.float32,
        )
        d_scores = (attn_probs * (d_probs - row_delta[..., None])).astype(jnp.bfloat16)
        return (attn_probs, d_scores)

    def query_step(carry_sum, block_index):
        key_start = block_index * key_block
        attn_probs, d_scores = score_grads(key_start, key_block)
        key_part = lax.dynamic_slice_in_dim(key_back, key_start, key_block).reshape(
            key_block, head_count, HEAD_DIM
        )
        return (
            carry_sum
            + jnp.einsum("hqk,khd->qhd", d_scores, key_part, preferred_element_type=jnp.float32),
            None,
        )

    d_query, _ = lax.scan(
        query_step, jnp.zeros((row_count, head_count, HEAD_DIM), jnp.float32), jnp.arange(blocks)
    )
    d_query = d_query.reshape(row_count, model_width) * score_scale
    part_rows = lax.axis_size("tensor") * row_count
    sub_block = block_span(part_rows, row_count)

    def one_block(block_index):
        begin = block_index * sub_block
        attn_probs, d_scores = score_grads(begin, sub_block)
        d_keys = (
            jnp.einsum("hqk,qhd->khd", d_scores, query_heads, preferred_element_type=jnp.float32)
            * score_scale
        )
        d_values = jnp.einsum(
            "hqk,qhd->khd",
            attn_probs.astype(jnp.bfloat16),
            d_heads,
            preferred_element_type=jnp.float32,
        )
        return jnp.concatenate(
            [d_keys.reshape(sub_block, model_width), d_values.reshape(sub_block, model_width)],
            axis=1,
        )

    block_terms = lax.map(one_block, jnp.arange(part_rows // sub_block))
    key_grads = lax.psum_scatter(
        block_terms.reshape(part_rows, 2 * model_width).astype(jnp.bfloat16),
        "tensor",
        scatter_dimension=0,
        tiled=True,
    ).astype(jnp.float32)
    d_keys_own = key_grads[:, :model_width]
    d_values_own = key_grads[:, model_width:]
    grad_gain = jnp.sum(d_query * q_unit + d_keys_own * k_unit, axis=0)
    d_qkv = jnp.concatenate(
        [
            unit_back(d_query * gain_qk, q_unit, q_factor),
            unit_back(d_keys_own * gain_qk, k_unit, k_factor),
            d_values_own,
        ],
        axis=1,
    ).astype(jnp.bfloat16)
    grad_qkv = jnp.einsum("tc,tf->cf", tokens, d_qkv, preferred_element_type=jnp.float32)
    d_tokens = (1.0 - mix_attn) * d_resid_one + jnp.einsum(
        "tf,cf->tc", d_qkv, qkv_full, preferred_element_type=jnp.float32
    )
    sum_qkv, sum_out, sum_gain, sum_mix_attn, sum_mix_mlp = (
        lax.psum_scatter(grad_qkv, ("dp", "tensor"), scatter_dimension=0, tiled=True),
        lax.psum_scatter(grad_out, ("dp", "tensor"), scatter_dimension=0, tiled=True),
        lax.psum_scatter(grad_gain, ("dp", "tensor"), scatter_dimension=0, tiled=True),
        lax.psum_scatter(grad_mix_attn, ("dp", "tensor"), scatter_dimension=0, tiled=True),
        lax.psum_scatter(grad_mix_mlp, ("dp", "tensor"), scatter_dimension=0, tiled=True),
    )
    sum_up, sum_gate, sum_down = (
        lax.psum_scatter(
            grad_up.astype(jnp.bfloat16), "dp", scatter_dimension=0, tiled=True
        ).astype(jnp.float32),
        lax.psum_scatter(
            grad_gate.astype(jnp.bfloat16), "dp", scatter_dimension=0, tiled=True
        ).astype(jnp.float32),
        lax.psum_scatter(
            grad_down.astype(jnp.bfloat16), "dp", scatter_dimension=0, tiled=True
        ).astype(jnp.float32),
    )
    sum_scale_up, sum_scale_gate = lax.psum((grad_scale_up, grad_scale_gate), "dp")
    stat_sums = lax.psum(partial_stats, ("dp", "tensor"))
    entry_count = row_count * model_width * lax.axis_size("dp") * spread
    stream_rms = jnp.sqrt(stat_sums / entry_count)
    return (
        result.astype(jnp.bfloat16),
        d_tokens.astype(jnp.bfloat16),
        sum_qkv,
        sum_out,
        sum_gain,
        sum_mix_attn,
        sum_mix_mlp,
        sum_up,
        sum_gate,
        sum_down,
        sum_scale_up,
        sum_scale_gate,
        stream_rms,
    )


MESH = pl.DeviceIdType.MESH
BF16 = jnp.bfloat16
F32 = jnp.float32
LOG2E = 1.4426950408889634
COPIES = 192
VMEM_BYTES = 63 * 2**20


def nn(left, right):
    return lax.dot_general(left, right, (((1,), (0,)), ((), ())), preferred_element_type=F32)


def nt(left, right):
    return lax.dot_general(left, right, (((1,), (1,)), ((), ())), preferred_element_type=F32)


def tn(left, right):
    return lax.dot_general(left, right, (((0,), (0,)), ((), ())), preferred_element_type=F32)


def flip(index, bits):
    bit = 1
    while bit <= bits:
        if bits & bit:
            index = index + bit - 2 * bit * lax.rem(lax.div(index, bit), 2)
        bit *= 2
    return index


def mean_rows(value):
    return jnp.mean(value, axis=-1, keepdims=True)


def fused_kernel(
    tokens, cotangent, whole_row, w_qkv, w_out, small, w_up, w_gate, w_down, scale_u, scale_v,
    layer_out, grad_tokens, grad_qkv, grad_out, grad_up, grad_gate, grad_down, stats_out,
    tok, wq, wo, wu, wg, wd, small_t, small_d, gains,
    raw, qkv, linv, att, ato, branch, hid, h1, ur, gr, inn,
    part, from_core3, from_core1, from_y,
    dr2, dr1, db, dba, dat, dao, dqkv, delta,
    gd, x_down, x_up, x_gate, x_qkv, x_out, z_down, z_up, z_gate, z_qkv, z_out,
    o_core3, o_core1, o_y, osum, q_sum, q_piece, stats, s_tensor, s_x, s_z,
    send_sem, recv_sem,
):
    d = lax.axis_index("dp")
    t = lax.axis_index("tensor")
    core, ynb, diag = (d, flip(t, 1)), (d, flip(t, 2)), (d, flip(t, 3))
    tensor_peer = {1: core, 2: ynb, 3: diag}
    xnb = (flip(d, 1), t)
    z_peer = {m: (flip(d, m), t) for m in (2, 4, 6)}

    barrier = pltpu.get_barrier_semaphore()
    peers = [core, ynb, diag, xnb] + [z_peer[m] for m in (2, 4, 6)]
    for peer in peers:
        pl.semaphore_signal(barrier, inc=1, device_id=peer, device_id_type=MESH)
    pl.semaphore_wait(barrier, len(peers))

    issued = []

    def send(src, dst, peer):
        index = len(issued)
        copy = pltpu.make_async_remote_copy(
            src_ref=src,
            dst_ref=dst,
            send_sem=send_sem.at[index],
            recv_sem=recv_sem.at[index],
            device_id=peer,
            device_id_type=MESH,
        )
        copy.start()
        issued.append(copy)
        return copy

    waited = set()

    def sent(copy):
        if id(copy) not in waited:
            waited.add(id(copy))
            copy.wait_send()

    def rows(start, count=256):
        return pl.ds(pl.multiple_of(start * count, count), count)

    def block(r):
        return pl.ds(r * 256, 256)

    class Gather:
        def __init__(self, src, view):
            self.src, self.view = src, view

        def start(self):
            own = self.view(d)
            self.z = {m: send(self.src, own, z_peer[m]) for m in (2, 4, 6)}
            self.x = [send(self.src, own, xnb)]

        def forward(self):
            for m in (2, 4, 6):
                self.z[m].wait_recv()
                part_ref = self.view(flip(d, m))
                self.x.append(send(part_ref, part_ref, xnb))

        def finish(self):
            for copy in self.x:
                copy.wait_recv()

    def rows_of(ref):
        return lambda index: ref.at[pl.ds(pl.multiple_of(index * 128, 128), 128)]

    take_qkv = Gather(
        wq.at[:, pl.ds(pl.multiple_of(d * 128, 128), 128), :],
        lambda index: wq.at[:, pl.ds(pl.multiple_of(index * 128, 128), 128), :],
    )
    take_small = Gather(small_d.at[d], lambda index: small_d.at[index])
    take_out = Gather(w_out, lambda index: wo.at[index, t])
    take_up = Gather(w_up, rows_of(wu))
    take_gate = Gather(w_gate, rows_of(wg))
    take_down = Gather(w_down, rows_of(wd))

    qkv_own = pl.ds(pl.multiple_of(d * 128 + t * 32, 32), 32)
    qkv_sends = [
        send(
            w_qkv.at[:, :, pl.ds(pl.multiple_of(flip(t, r) * 256, 256), 256)],
            wq.at[:, qkv_own, :],
            tensor_peer[r],
        )
        for r in (1, 2, 3)
    ]
    small_sends = [send(small, small_t.at[r - 1], tensor_peer[r]) for r in (1, 2, 3)]
    tok_y = send(tokens, tok.at[block(2)], ynb)
    tok_core = send(tokens, tok.at[block(1)], core)
    tok[0:256, :] = tokens[...]
    wq[:, qkv_own, :] = w_qkv[:, :, pl.ds(pl.multiple_of(t * 256, 256), 256)]
    wo[d, t] = w_out[...]
    wu[pl.ds(pl.multiple_of(d * 128, 128), 128), :] = w_up[...]
    wg[pl.ds(pl.multiple_of(d * 128, 128), 128), :] = w_gate[...]
    wd[pl.ds(pl.multiple_of(d * 128, 128), 128), :] = w_down[...]
    stats[...] = jnp.zeros_like(stats)
    for copy in small_sends:
        copy.wait_recv()
    small_d[d] = small[...] + small_t[0] + small_t[1] + small_t[2]
    take_small.start()
    for copy in qkv_sends:
        copy.wait_recv()
    take_qkv.start()

    take_small.forward()
    take_qkv.forward()
    take_out.start()
    take_up.start()
    tok_y.wait_recv()
    tok_diag = send(tok.at[block(2)], tok.at[block(3)], core)
    take_small.finish()
    total = small_d[0].astype(F32)
    for index in range(1, 8):
        total = total + small_d[index].astype(F32)
    gains[...] = total
    take_qkv.finish()
    tok_core.wait_recv()
    tok_diag.wait_recv()

    head_col = pl.ds(pl.multiple_of(t * 256, 256), 256)
    gain_qk = gains[0:1, head_col]
    lane = lax.broadcasted_iota(jnp.int32, (1, 256), 1)
    lane_head = lax.div(lane, HEAD_DIM)
    same_head = jnp.where(
        lax.div(lax.broadcasted_iota(jnp.int32, (256, 256), 0), HEAD_DIM)
        == lax.div(lax.broadcasted_iota(jnp.int32, (256, 256), 1), HEAD_DIM),
        1.0,
        0.0,
    ).astype(BF16)

    def head_sum(value):
        high = value.astype(BF16)
        low = (value - high.astype(F32)).astype(BF16)
        return nn(high, same_head) + nn(low, same_head)

    def qkv_step(r, carry):
        at = rows(r)
        x = tok[at, :]
        for j in range(3):
            y = nn(x, wq[j])
            if j < 2:
                raw[j, at, :] = y
                factor = lax.rsqrt(head_sum(y * y) + EPSILON)
                qkv[j, at, :] = (y * factor * gain_qk).astype(BF16)
            else:
                qkv[j, at, :] = y.astype(BF16)
        return carry

    lax.fori_loop(0, 4, qkv_step, 0)
    take_out.forward()
    take_gate.start()

    def true_rows(i):
        return rows(flip(t, i))

    whole = whole_row[...]
    row_id = lax.broadcasted_iota(jnp.int32, (256, 256), 0)
    col_id = lax.broadcasted_iota(jnp.int32, (256, 256), 1)
    exp_scale = math.sqrt(HEAD_DIM) * LOG2E

    def attend(i):
        at = true_rows(i)

        def head_step(h, carry):
            mask = lane_head == h
            q = jnp.where(mask, qkv[0, at, :], 0).astype(BF16)
            acc = jnp.zeros((256, 256), F32)
            weight = jnp.zeros((256, 1), F32)
            for j in range(i + 1):
                key_at = true_rows(j)
                e = jnp.exp2(nt(q, qkv[1, key_at, :]) * exp_scale)
                if j == i:
                    e = jnp.where(col_id <= row_id, e, 0.0)
                elif j // 2 != i // 2:
                    e = e * whole
                weight = weight + jnp.sum(e, axis=1, keepdims=True)
                acc = acc + nn(e.astype(BF16), qkv[2, key_at, :])
            inverse = 1.0 / weight
            linv[at, :] = jnp.where(mask, inverse, linv[at, :])
            att[at, :] = jnp.where(mask, (acc * inverse).astype(BF16), att[at, :])
            return carry

        linv[at, :] = jnp.zeros((256, 256), F32)
        att[at, :] = jnp.zeros((256, 256), BF16)
        lax.fori_loop(0, 4, head_step, 0)

    attend(0)
    attend(1)
    attend(2)
    take_up.forward()
    take_down.start()
    attend(3)

    att_sends = [send(att.at[block(r)], ato.at[t], tensor_peer[r]) for r in (2, 3, 1)]
    ato[t] = att[block(0), :]
    take_out.finish()
    wo_y = send(wo.at[:, t], wo.at[:, t], ynb)
    wo_core = send(wo.at[:, t], wo.at[:, t], core)
    wo_y.wait_recv()
    wo_far = send(wo.at[:, flip(t, 2)], wo.at[:, flip(t, 2)], core)
    for copy in att_sends:
        copy.wait_recv()
    wo_core.wait_recv()
    wo_far.wait_recv()

    def out_rows(slot, columns):
        return wo[2 * slot : 2 * slot + 2, :, :, columns].reshape(256, 256)

    def out_step(n, carry):
        at = rows(n)
        acc = nn(ato[0], out_rows(0, at))
        for slot in range(1, 4):
            acc = acc + nn(ato[slot], out_rows(slot, at))
        branch[:, at] = acc
        return carry

    lax.fori_loop(0, 4, out_step, 0)

    mix_a = gains[1:2, :]
    mix_m = gains[2:3, :]
    CH = 32

    def add_stat(row, value):
        stats[row : row + 1, :] = stats[row : row + 1, :] + jnp.sum(value, axis=0, keepdims=True)

    def first_norm(at):
        x = tokens[at, :].astype(F32)
        ba = branch[at, :]
        fa = lax.rsqrt(mean_rows(ba * ba) + EPSILON)
        ha = ba * fa
        r1 = x + mix_a * (ha - x)
        f1 = lax.rsqrt(mean_rows(r1 * r1) + EPSILON)
        return x, ba, fa, ha, f1, r1 * f1

    def norm_step(c, carry):
        at = rows(c, CH)
        _, ba, _, _, _, hidden = first_norm(at)
        add_stat(3, ba * ba)
        hid[at, :] = hidden
        h1[at, :] = hidden.astype(BF16)
        return carry

    lax.fori_loop(0, 256 // CH, norm_step, 0)

    def spread(ref):
        return send(ref.at[block(0)], ref.at[block(2)], ynb), send(
            ref.at[block(0)], ref.at[block(1)], core
        )

    def relay(ref, from_ynb):
        from_ynb.wait_recv()
        return send(ref.at[block(2)], ref.at[block(3)], core)

    h1_y, h1_core = spread(h1)
    h1_far = relay(h1, h1_y)
    take_gate.forward()
    take_down.forward()
    take_up.finish()
    take_gate.finish()
    h1_core.wait_recv()
    h1_far.wait_recv()

    def up_step(index, carry):
        f = lax.rem(index, 4)
        at, cols = rows(lax.div(index, 4)), rows(f)
        hidden = h1[at, :]
        u_raw = nn(hidden, wu[:, cols])
        g_raw = nn(hidden, wg[:, cols])
        gate = g_raw * scale_v[:, cols]
        silu = gate / (1.0 + jnp.exp(-gate))
        ur[at, cols] = u_raw.astype(BF16)
        gr[at, cols] = g_raw.astype(BF16)
        inn[at, cols] = (u_raw * scale_u[:, cols] * silu).astype(BF16)
        return carry

    lax.fori_loop(0, 16, up_step, 0)
    take_down.finish()

    class Reduce:
        def __init__(self, which, before, make):
            self.which, self.before, self.make = which, before, make

        def run(self):
            k = self.which
            waits = self.before.copies if self.before else {}
            self.copies = {}
            for r in (3, 2, 1, 0):
                if r in waits:
                    sent(waits[r])
                self.make(r)
                if r == 3:
                    self.copies[3] = send(part.at[block(3)], from_core3.at[k], core)
                elif r == 2:
                    self.copies[3].wait_recv()
                    part[block(2), :] = (
                        part[block(2), :].astype(F32) + from_core3[k].astype(F32)
                    ).astype(BF16)
                    self.copies[2] = send(part.at[block(2)], from_y.at[k], ynb)
                elif r == 1:
                    self.copies[1] = send(part.at[block(1)], from_core1.at[k], core)

        def finish(self):
            self.copies[1].wait_recv()
            self.copies[2].wait_recv()

        def at(self, where):
            k = self.which
            return (
                part[where, :].astype(F32)
                + from_core1[k, where, :].astype(F32)
                + from_y[k, where, :].astype(F32)
            )

    def make_down(r):
        def step(n, carry):
            cols = rows(n)
            part[block(r), cols] = nt(inn[block(r), :], wd[cols, :]).astype(BF16)
            return carry

        lax.fori_loop(0, 4, step, 0)

    sum_m = Reduce(0, None, make_down)
    sum_m.run()
    sum_m.finish()

    def loss_step(c, carry):
        at = rows(c, CH)
        bm = sum_m.at(at)
        hidden = hid[at, :]
        fm = lax.rsqrt(mean_rows(bm * bm) + EPSILON)
        hm = bm * fm
        r2 = hidden + mix_m * (hm - hidden)
        f2 = lax.rsqrt(mean_rows(r2 * r2) + EPSILON)
        result = r2 * f2
        layer_out[at, :] = result.astype(BF16)
        up = cotangent[at, :].astype(F32)
        grad = f2 * (up - result * mean_rows(up * result))
        dr2[at, :] = grad
        add_stat(1, grad * (hm - hidden))
        add_stat(4, bm * bm)
        add_stat(5, r2 * r2)
        c_m = mix_m * grad
        db[at, :] = (fm * (c_m - hm * mean_rows(c_m * hm))).astype(BF16)
        return carry

    lax.fori_loop(0, 256 // CH, loss_step, 0)

    class Scatter:
        def __init__(self, view, from_x, from_z):
            self.view, self.from_x, self.from_z = view, from_x, from_z
            self.x, self.z = {}, {}

        def ship(self, k):
            self.x[k] = send(self.view(flip(d, 2 * k + 1)), self.from_x.at[k], xnb)

        def fold(self, k):
            self.x[k].wait_recv()
            own = self.view(flip(d, 2 * k))
            own[...] = (own[...].astype(F32) + self.from_x[k].astype(F32)).astype(BF16)
            if k:
                self.z[k] = send(own, self.from_z.at[k - 1], z_peer[2 * k])

        def total(self):
            for k in (3, 2, 1):
                self.z[k].wait_recv()
            own = self.view(d)[...].astype(F32)
            for k in range(3):
                own = own + self.from_z[k].astype(F32)
            return own

    def release(gather):
        for copy in [*gather.z.values(), *gather.x]:
            sent(copy)

    def weight_grad(left, right, out, scatter):
        for k in (3, 2, 1, 0):
            at = rows(lax.div(flip(d, 2 * k), 2))

            def step(n, carry):
                cols = rows(n)
                out[at, cols] = tn(left[:, at], right[:, cols]).astype(BF16)
                return carry

            lax.fori_loop(0, 4, step, 0)
            scatter.ship(k)

    db_y, db_core = spread(db)
    db_far = relay(db, db_y)
    db_core.wait_recv()
    db_far.wait_recv()

    sum_down = Scatter(rows_of(gd), x_down, z_down)
    weight_grad(db, inn, gd, sum_down)

    def make_hidden(r):
        at = block(r)

        def inner_step(f, carry):
            cols = rows(f)
            d_inner = nn(db[at, :], wd[:, cols])
            u_raw = ur[at, cols].astype(F32)
            g_raw = gr[at, cols].astype(F32)
            gate = g_raw * scale_v[:, cols]
            sig = 1.0 / (1.0 + jnp.exp(-gate))
            up = u_raw * scale_u[:, cols]
            d_up = d_inner * (gate * sig)
            d_gate = d_inner * up * (sig * (1.0 + gate * (1.0 - sig)))
            stats[6:7, cols] = stats[6:7, cols] + jnp.sum(d_up * u_raw, axis=0, keepdims=True)
            stats[7:8, cols] = stats[7:8, cols] + jnp.sum(d_gate * g_raw, axis=0, keepdims=True)
            ur[at, cols] = (d_up * scale_u[:, cols]).astype(BF16)
            gr[at, cols] = (d_gate * scale_v[:, cols]).astype(BF16)
            return carry

        def back_step(n, carry):
            cols = rows(n)
            part[at, cols] = (nt(ur[at, :], wu[cols, :]) + nt(gr[at, :], wg[cols, :])).astype(BF16)
            return carry

        lax.fori_loop(0, 4, inner_step, 0)
        lax.fori_loop(0, 4, back_step, 0)

    sum_h = Reduce(1, sum_m, make_hidden)
    sum_h.run()

    gu, gg, go = wd, wu, wg
    for gather in (take_down, take_up, take_gate):
        release(gather)
    sum_up = Scatter(rows_of(gu), x_up, z_up)
    sum_gate = Scatter(rows_of(gg), x_gate, z_gate)
    weight_grad(h1, ur, gu, sum_up)
    sum_down.fold(3)
    sum_down.fold(2)
    weight_grad(h1, gr, gg, sum_gate)
    sum_down.fold(1)
    sum_down.fold(0)
    sum_h.finish()

    def mid_step(c, carry):
        at = rows(c, CH)
        x, _, fa, ha, f1, hidden = first_norm(at)
        d_hidden = (1.0 - mix_m) * dr2[at, :] + sum_h.at(at)
        grad = f1 * (d_hidden - hidden * mean_rows(d_hidden * hidden))
        dr1[at, :] = grad
        add_stat(0, grad * (ha - x))
        c_a = mix_a * grad
        dba[at, :] = (fa * (c_a - ha * mean_rows(c_a * ha))).astype(BF16)
        return carry

    lax.fori_loop(0, 256 // CH, mid_step, 0)

    dat_sends = []
    for r in (2, 3, 1, 0):
        slot = flip(t, r)
        weight = wo[pl.ds(2 * slot, 2)].reshape(256, 1024)
        piece = nt(dba[...], weight).astype(BF16)
        if r:
            dat[r - 1] = piece
            dat_sends.append(send(dat.at[r - 1], dao.at[block(r)], tensor_peer[r]))
        else:
            dao[block(0), :] = piece

    def out_grad_step(n, carry):
        cols = rows(n)
        for slot in range(4):
            g = tn(ato[slot], dba[:, cols]).astype(BF16)
            for q in range(8):
                start = (q % 4) * 256 + (2 * slot + q // 4) * 32
                go[start : start + 32, cols] = g[q * 32 : (q + 1) * 32, :]
        return carry

    lax.fori_loop(0, 4, out_grad_step, 0)

    def go_rows(r):
        return rows(flip(t, r))

    go_core3 = send(go.at[go_rows(3)], o_core3, core)
    go_core1 = send(go.at[go_rows(1)], o_core1, core)
    sum_up.fold(3)
    sum_up.fold(2)
    go_core3.wait_recv()
    go[go_rows(2), :] = (go[go_rows(2), :].astype(F32) + o_core3[...].astype(F32)).astype(BF16)
    go_y = send(go.at[go_rows(2)], o_y, ynb)
    for copy in dat_sends:
        copy.wait_recv()

    head_rows = jnp.where(
        lax.broadcasted_iota(jnp.int32, (8, 256), 0)
        == lax.div(lax.broadcasted_iota(jnp.int32, (8, 256), 1), HEAD_DIM),
        1.0,
        0.0,
    ).astype(BF16)
    for copy in att_sends:
        sent(copy)

    def ready_step(r, carry):
        at = rows(r)
        scaled = (dao[at, :].astype(F32) * linv[at, :]).astype(BF16)
        dao[at, :] = scaled
        product = scaled.astype(F32) * att[at, :].astype(F32)
        high = product.astype(BF16)
        low = (product - high.astype(F32)).astype(BF16)
        delta[r] = nt(head_rows, high) + nt(head_rows, low)
        att[at, :] = qkv[1, at, :].T
        return carry

    lax.fori_loop(0, 4, ready_step, 0)
    d_key, d_value, d_query_t = branch, hid, dr2
    d_key[...] = jnp.zeros_like(d_key)
    d_value[...] = jnp.zeros_like(d_value)
    d_query_t[...] = jnp.zeros_like(d_query_t)

    def attend_back(j, i):
        key_at, query_at = true_rows(j), true_rows(i)
        key_cols, query_cols = slice(j * 256, j * 256 + 256), slice(i * 256, i * 256 + 256)

        def head_step(h, carry):
            mask = lane_head == h
            q = jnp.where(mask, qkv[0, query_at, :], 0).astype(BF16)
            do = jnp.where(mask, dao[query_at, :], 0).astype(BF16)
            e = jnp.exp2(nt(qkv[1, key_at, :], q) * exp_scale)
            if i == j:
                e = jnp.where(row_id <= col_id, e, 0.0)
            elif j // 2 != i // 2:
                e = e * whole
            d_prob = nt(qkv[2, key_at, :], do)
            d_score = (e * (d_prob - delta[flip(t, i), pl.ds(h, 1), :])).astype(BF16)
            d_key[:, key_cols] += nn(d_score, q)
            d_value[:, key_cols] += nn(e.astype(BF16), do)
            part_rows = pl.ds(pl.multiple_of(h * HEAD_DIM, HEAD_DIM), HEAD_DIM)
            key_t = att[pl.ds(pl.multiple_of(flip(t, j) * 256 + h * HEAD_DIM, HEAD_DIM), HEAD_DIM), :]
            d_query_t[part_rows, query_cols] += nn(key_t, d_score)
            return carry

        lax.fori_loop(0, 4, head_step, 0)

    attend_back(0, 0)
    attend_back(0, 1)
    sum_up.fold(1)
    sum_up.fold(0)
    attend_back(0, 2)
    attend_back(0, 3)
    sum_gate.fold(3)
    sum_gate.fold(2)
    attend_back(1, 1)
    attend_back(1, 2)
    attend_back(1, 3)
    sum_gate.fold(1)
    sum_gate.fold(0)
    go_core1.wait_recv()
    go_y.wait_recv()
    osum[...] = (
        go[go_rows(0), :].astype(F32) + o_core1[...].astype(F32) + o_y[...].astype(F32)
    ).astype(BF16)
    sum_out = Scatter(
        lambda index: osum.at[pl.ds(pl.multiple_of(index * 32, 32), 32)], x_out, z_out
    )
    for k in (3, 2, 1, 0):
        sum_out.ship(k)
    attend_back(2, 2)
    attend_back(2, 3)
    attend_back(3, 3)

    def qkv_back(i):
        at = true_rows(i)
        cols = slice(i * 256, i * 256 + 256)
        scale = math.sqrt(HEAD_DIM)
        for j, grad in ((0, d_query_t[:, cols].T * scale), (1, d_key[:, cols] * scale)):
            y = raw[j, at, :]
            factor = lax.rsqrt(head_sum(y * y) + EPSILON)
            w = y * factor
            stats[2:3, head_col] = stats[2:3, head_col] + jnp.sum(grad * w, axis=0, keepdims=True)
            c = grad * gain_qk
            dqkv[j, at, :] = (factor * (c - w * head_sum(c * w))).astype(BF16)
        dqkv[2, at, :] = d_value[:, cols].astype(BF16)

    for i in range(4):
        qkv_back(i)

    gq = qkv
    sum_qkv = Scatter(
        lambda index: gq.at[:, pl.ds(pl.multiple_of(index * 128, 128), 128), :], x_qkv, z_qkv
    )
    for k in (3, 2, 1, 0):
        zz = lax.div(flip(d, 2 * k), 2)
        for j in range(3):
            gq[j, rows(zz), :] = tn(tok[:, rows(zz)], dqkv[j]).astype(BF16)
        sum_qkv.ship(k)

    small_sends = [send(stats, s_tensor.at[r - 1], tensor_peer[r]) for r in (1, 2, 3)]

    def make_tokens(r):
        def step(n, carry):
            cols = rows(n)
            acc = nt(dqkv[0, block(r), :], wq[0, cols, :])
            for j in (1, 2):
                acc = acc + nt(dqkv[j, block(r), :], wq[j, cols, :])
            part[block(r), cols] = acc.astype(BF16)
            return carry

        lax.fori_loop(0, 4, step, 0)

    sum_t = Reduce(2, sum_h, make_tokens)
    sum_t.run()

    for k in (3, 2, 1, 0):
        sum_out.fold(k)
    for copy in small_sends:
        copy.wait_recv()
    over_tensor = s_tensor[0] + s_tensor[1] + s_tensor[2]
    shared = lax.broadcasted_iota(jnp.int32, (8, 1024), 0) < 6
    s_x[0] = stats[...] + jnp.where(shared, over_tensor, 0.0)
    stat_x = send(s_x.at[0], s_x.at[1], xnb)
    for k in (3, 2, 1, 0):
        sum_qkv.fold(k)
    stat_x.wait_recv()
    s_z[0] = s_x[0] + s_x[1]
    stat_z = [send(s_z.at[0], s_z.at[k], z_peer[2 * k]) for k in (1, 2, 3)]

    grad_down[...] = sum_down.total()
    grad_up[...] = sum_up.total()
    grad_gate[...] = sum_gate.total()
    grad_out[...] = sum_out.total()
    q_sum[...] = sum_qkv.total()
    q_sends = [
        send(
            q_sum.at[:, pl.ds(pl.multiple_of(flip(t, r) * 32, 32), 32), :],
            q_piece.at[t],
            tensor_peer[r],
        )
        for r in (1, 2, 3)
    ]
    q_piece[t] = q_sum[:, pl.ds(pl.multiple_of(t * 32, 32), 32), :]
    sum_t.finish()

    def last_step(c, carry):
        at = rows(c, CH)
        grad_tokens[at, :] = ((1.0 - mix_a) * dr1[at, :] + sum_t.at(at)).astype(BF16)
        return carry

    lax.fori_loop(0, 256 // CH, last_step, 0)
    for copy in stat_z:
        copy.wait_recv()
    stats_out[...] = s_z[0] + s_z[1] + s_z[2] + s_z[3]
    for copy in q_sends:
        copy.wait_recv()
    for slot in range(4):
        for j in range(3):
            grad_qkv[:, j * 1024 + slot * 256 : j * 1024 + slot * 256 + 256] = q_piece[slot, j]
    for copy in issued:
        sent(copy)


def fits(mesh):
    return dict(mesh.shape) == {"dp": 8, "tensor": 4}


def fused(
    tokens, cotangent, bucket_start, w_qkv, w_out, s_qk, alpha_a, alpha_m, w_up, w_gate, w_down, s_u, s_v
):
    n_rows, width = tokens.shape
    d, t = lax.axis_index("dp"), lax.axis_index("tensor")
    index = d * lax.axis_size("tensor") + t
    piece = s_qk.shape[0]
    starts = lax.dynamic_slice_in_dim(bucket_start, d * 4, 4)
    whole = jnp.where(starts[0] == starts[2], 1.0, 0.0)
    whole_row = jnp.full((1, 256), whole, F32)
    vectors = jnp.stack([s_qk, alpha_a, alpha_m]).astype(F32)
    mine = lax.div(jnp.arange(width, dtype=jnp.int32), piece) == index
    small = jnp.where(mine[None, :], jnp.tile(vectors, (1, width // piece)), 0.0)
    small = jnp.pad(small, ((0, 13), (0, 0))).astype(BF16)
    vmem = pl.BlockSpec(memory_space=pltpu.VMEM)
    bf = lambda *shape: pltpu.VMEM(shape, BF16)
    fl = lambda *shape: pltpu.VMEM(shape, F32)
    out_shapes = [
        ((256, 1024), BF16), ((256, 1024), BF16), ((32, 3072), F32), ((32, 1024), F32),
        ((128, 1024), F32), ((128, 1024), F32), ((128, 1024), F32), ((8, 1024), F32),
    ]
    scratch = [
        bf(1024, 1024), bf(3, 1024, 256), bf(8, 4, 32, 1024), bf(1024, 1024), bf(1024, 1024),
        bf(1024, 1024), bf(3, 16, 1024), bf(8, 16, 1024), fl(16, 1024),
        fl(2, 1024, 256), bf(3, 1024, 256), fl(1024, 256), bf(1024, 256), bf(4, 256, 256),
        fl(256, 1024), fl(256, 1024), bf(1024, 1024), bf(1024, 1024), bf(1024, 1024), bf(1024, 1024),
        bf(1024, 1024), bf(3, 256, 1024), bf(3, 256, 1024), bf(3, 256, 1024),
        fl(256, 1024), fl(256, 1024), bf(1024, 1024), bf(256, 1024), bf(3, 256, 256),
        bf(1024, 256), bf(3, 1024, 256), fl(4, 8, 256),
        bf(1024, 1024), bf(4, 128, 1024), bf(4, 128, 1024), bf(4, 128, 1024), bf(4, 3, 128, 256),
        bf(4, 32, 1024), bf(3, 128, 1024), bf(3, 128, 1024), bf(3, 128, 1024), bf(3, 3, 128, 256),
        bf(3, 32, 1024), bf(256, 1024), bf(256, 1024), bf(256, 1024), bf(256, 1024),
        fl(3, 128, 256), fl(4, 3, 32, 256), fl(8, 1024), fl(3, 8, 1024), fl(2, 8, 1024), fl(4, 8, 1024),
        pltpu.SemaphoreType.DMA((COPIES,)), pltpu.SemaphoreType.DMA((COPIES,)),
    ]
    outs = pl.pallas_call(
        fused_kernel,
        out_shape=[jax.ShapeDtypeStruct(shape, kind) for shape, kind in out_shapes],
        in_specs=[vmem] * 11,
        out_specs=[vmem] * 8,
        scratch_shapes=scratch,
        compiler_params=pltpu.CompilerParams(
            collective_id=0, has_side_effects=True, vmem_limit_bytes=VMEM_BYTES
        ),
        cost_estimate=pl.CostEstimate(
            flops=27_000_000_000, bytes_accessed=8_000_000, transcendentals=10_000_000
        ),
    )(
        tokens, cotangent, whole_row,
        w_qkv.reshape(piece, 3, width).transpose(1, 0, 2), w_out, small, w_up, w_gate, w_down,
        s_u.astype(F32)[None, :], s_v.astype(F32)[None, :],
    )
    result, d_tokens, g_qkv, g_out, g_up, g_gate, g_down, stats = outs
    own = lax.dynamic_slice(stats, (0, index * piece), (3, piece))
    entries = n_rows * width * lax.axis_size("dp") * lax.axis_size("tensor")
    stream_rms = jnp.sqrt(jnp.sum(stats[3:6], axis=1) / entries)
    return (
        result, d_tokens, g_qkv, g_out, own[2], own[0], own[1], g_up, g_gate, g_down,
        stats[6], stats[7], stream_rms,
    )


def solution(mesh):
    body = fused if fits(mesh) else local
    return jax.shard_map(
        body,
        mesh=mesh,
        in_specs=(
            P(("dp", "tensor"), None),
            P(("dp", "tensor"), None),
            P(),
            P(("dp", "tensor"), None),
            P(("dp", "tensor"), None),
            P(("dp", "tensor")),
            P(("dp", "tensor")),
            P(("dp", "tensor")),
            P("dp", "tensor"),
            P("dp", "tensor"),
            P("dp", "tensor"),
            P("tensor"),
            P("tensor"),
        ),
        out_specs=(
            P(("dp", "tensor"), None),
            P(("dp", "tensor"), None),
            P(("dp", "tensor"), None),
            P(("dp", "tensor"), None),
            P(("dp", "tensor")),
            P(("dp", "tensor")),
            P(("dp", "tensor")),
            P("dp", "tensor"),
            P("dp", "tensor"),
            P("dp", "tensor"),
            P("tensor"),
            P("tensor"),
            P(),
        ),
        check_vma=False,
    )
```

```python
import functools
import math

import jax
import jax.numpy as jnp
from jax import lax
from jax.experimental import pallas as pl
from jax.experimental.pallas import tpu as pltpu
from jax.sharding import PartitionSpec as P

HEAD_DIM = 64


EPSILON = 1e-06
MASKED_SCORE = -1e30


def rms_rows(value):
    return value * lax.rsqrt(jnp.mean(value * value, axis=-1, keepdims=True) + EPSILON)


def rms_back(upstream, normed, source):
    factor = lax.rsqrt(jnp.mean(source * source, axis=-1, keepdims=True) + EPSILON)
    return factor * (upstream - normed * jnp.mean(upstream * normed, axis=-1, keepdims=True))


def unit_heads(value):
    shaped = value.reshape(value.shape[0], -1, HEAD_DIM)
    factor = lax.rsqrt(jnp.sum(shaped * shaped, axis=-1, keepdims=True) + EPSILON)
    return ((shaped * factor).reshape(value.shape), factor)


def unit_back(upstream, normed, factor):
    upper_grad = upstream.reshape(normed.shape[0], -1, HEAD_DIM)
    normed_heads = normed.reshape(normed.shape[0], -1, HEAD_DIM)
    result = factor * (
        upper_grad - normed_heads * jnp.sum(upper_grad * normed_heads, axis=-1, keepdims=True)
    )
    return result.reshape(upstream.shape)


def block_span(total_rows, row_count):
    units = total_rows // row_count
    block_units = max(1, min(units, 512 // row_count))
    while units % block_units:
        block_units -= 1
    return row_count * block_units


def local(
    tokens,
    cotangent,
    bucket_start,
    w_qkv,
    w_out,
    s_qk,
    alpha_a,
    alpha_m,
    w_up,
    w_gate,
    w_down,
    s_u,
    s_v,
):
    row_count, model_width = tokens.shape
    head_count = model_width // HEAD_DIM
    score_scale = math.sqrt(HEAD_DIM)
    spread = lax.axis_size("tensor")
    group_rows = spread * row_count
    tensor_slot = lax.axis_index("tensor")
    qkv_full, out_full, gain_qk, mix_attn, mix_mlp = (
        lax.all_gather(w_qkv, ("dp", "tensor"), axis=0, tiled=True),
        lax.all_gather(w_out, ("dp", "tensor"), axis=0, tiled=True),
        lax.all_gather(s_qk, ("dp", "tensor"), axis=0, tiled=True),
        lax.all_gather(alpha_a, ("dp", "tensor"), axis=0, tiled=True),
        lax.all_gather(alpha_m, ("dp", "tensor"), axis=0, tiled=True),
    )
    up_full, gate_full, down_full = (
        lax.all_gather(w_up, "dp", axis=0, tiled=True),
        lax.all_gather(w_gate, "dp", axis=0, tiled=True),
        lax.all_gather(w_down, "dp", axis=0, tiled=True),
    )
    gain_qk = gain_qk.astype(jnp.float32)
    mix_attn = mix_attn.astype(jnp.float32)
    mix_mlp = mix_mlp.astype(jnp.float32)
    scale_up = s_u.astype(jnp.float32)
    scale_gate = s_v.astype(jnp.float32)
    starts = lax.dynamic_slice_in_dim(bucket_start, lax.axis_index("dp") * spread, spread)
    key_seq = jnp.repeat(starts, row_count)
    own_seq = starts[tensor_slot]
    query_pos = tensor_slot * row_count + jnp.arange(row_count, dtype=jnp.int32)

    def allowed(key_start, key_count):
        key_pos = key_start + jnp.arange(key_count, dtype=jnp.int32)
        seq_part = lax.dynamic_slice_in_dim(key_seq, key_start, key_count)
        return (key_pos[None, :] <= query_pos[:, None]) & (seq_part[None, :] == own_seq)

    inputs = tokens.astype(jnp.float32)
    qkv = jnp.dot(tokens, qkv_full, preferred_element_type=jnp.float32)
    q_unit, q_factor = unit_heads(qkv[:, :model_width])
    k_unit, k_factor = unit_heads(qkv[:, model_width : 2 * model_width])
    query_low = (q_unit * gain_qk).astype(jnp.bfloat16)
    keys_low = (k_unit * gain_qk).astype(jnp.bfloat16)
    values_low = qkv[:, 2 * model_width :].astype(jnp.bfloat16)
    query_heads = query_low.reshape(row_count, head_count, HEAD_DIM)
    key_all, value_all = (
        lax.all_gather(keys_low, "tensor", axis=0, tiled=True),
        lax.all_gather(values_low, "tensor", axis=0, tiled=True),
    )
    key_block = block_span(group_rows, row_count)
    blocks = group_rows // key_block

    def block_scores(key_source, key_start, key_count):
        key_part = lax.dynamic_slice_in_dim(key_source, key_start, key_count).reshape(
            key_count, head_count, HEAD_DIM
        )
        return (
            jnp.einsum("qhd,khd->hqk", query_heads, key_part, preferred_element_type=jnp.float32)
            * score_scale
        )

    def stat_step(state_pair, block_index):
        row_top, row_total = state_pair
        key_start = block_index * key_block
        allowed_keys = allowed(key_start, key_block)[None]
        masked = jnp.where(allowed_keys, block_scores(key_all, key_start, key_block), MASKED_SCORE)
        new_top = jnp.maximum(row_top, jnp.max(masked, axis=-1))
        fresh = jnp.where(allowed_keys, jnp.exp(masked - new_top[..., None]), 0.0)
        row_total = row_total * jnp.exp(row_top - new_top) + jnp.sum(fresh, axis=-1)
        return ((new_top, row_total), None)

    start_state = (
        jnp.full((head_count, row_count), MASKED_SCORE, jnp.float32),
        jnp.zeros((head_count, row_count), jnp.float32),
    )
    (row_top, row_total), _ = lax.scan(stat_step, start_state, jnp.arange(blocks))
    log_total = row_top + jnp.log(row_total)

    def probs_for(key_source, key_start, key_count):
        scores = block_scores(key_source, key_start, key_count)
        allowed_keys = allowed(key_start, key_count)[None]
        return jnp.where(allowed_keys, jnp.exp(scores - log_total[..., None]), 0.0)

    def value_part(value_source, key_start, key_count):
        return lax.dynamic_slice_in_dim(value_source, key_start, key_count).reshape(
            key_count, head_count, HEAD_DIM
        )

    def out_step(carry_sum, block_index):
        key_start = block_index * key_block
        attn_probs = probs_for(key_all, key_start, key_block).astype(jnp.bfloat16)
        term = jnp.einsum(
            "hqk,khd->qhd",
            attn_probs,
            value_part(value_all, key_start, key_block),
            preferred_element_type=jnp.float32,
        )
        return (carry_sum + term, None)

    attended, _ = lax.scan(
        out_step, jnp.zeros((row_count, head_count, HEAD_DIM), jnp.float32), jnp.arange(blocks)
    )
    attended_low = attended.reshape(row_count, model_width).astype(jnp.bfloat16)
    branch_a = jnp.dot(attended_low, out_full, preferred_element_type=jnp.float32)
    h_attn = rms_rows(branch_a)
    resid_one = inputs + mix_attn * (h_attn - inputs)
    hidden_one = rms_rows(resid_one)
    hidden_low = hidden_one.astype(jnp.bfloat16)
    rows_all = lax.all_gather(hidden_low, "tensor", axis=0, tiled=True)
    up_raw = jnp.dot(rows_all, up_full, preferred_element_type=jnp.float32)
    gate_raw = jnp.dot(rows_all, gate_full, preferred_element_type=jnp.float32)
    up_scaled = up_raw * scale_up
    gate_scaled = gate_raw * scale_gate
    gate_sigmoid = jax.nn.sigmoid(gate_scaled)
    silu_gate = gate_scaled * gate_sigmoid
    inner_low = (up_scaled * silu_gate).astype(jnp.bfloat16)
    branch_m = lax.psum_scatter(
        jnp.einsum("tf,df->td", inner_low, down_full, preferred_element_type=jnp.float32).astype(
            jnp.bfloat16
        ),
        "tensor",
        scatter_dimension=0,
        tiled=True,
    ).astype(jnp.float32)
    h_mlp = rms_rows(branch_m)
    resid_two = hidden_one + mix_mlp * (h_mlp - hidden_one)
    result = rms_rows(resid_two)
    partial_stats = jnp.stack(
        [jnp.sum(branch_a * branch_a), jnp.sum(branch_m * branch_m), jnp.sum(resid_two * resid_two)]
    )
    upstream = cotangent.astype(jnp.float32)
    d_resid_two = rms_back(upstream, result, resid_two)
    grad_mix_mlp = jnp.sum(d_resid_two * (h_mlp - hidden_one), axis=0)
    d_branch_m = rms_back(mix_mlp * d_resid_two, h_mlp, branch_m).astype(jnp.bfloat16)
    grads_all = lax.all_gather(d_branch_m, "tensor", axis=0, tiled=True)
    d_inner = jnp.dot(grads_all, down_full, preferred_element_type=jnp.float32)
    grad_up_scaled = d_inner * silu_gate
    grad_gate_scaled = (
        d_inner * up_scaled * gate_sigmoid * (1.0 + gate_scaled * (1.0 - gate_sigmoid))
    )
    grad_scale_up = jnp.sum(grad_up_scaled * up_raw, axis=0)
    grad_scale_gate = jnp.sum(grad_gate_scaled * gate_raw, axis=0)
    up_grad_low = (grad_up_scaled * scale_up).astype(jnp.bfloat16)
    gate_grad_low = (grad_gate_scaled * scale_gate).astype(jnp.bfloat16)
    grad_down = jnp.einsum("td,tf->df", grads_all, inner_low, preferred_element_type=jnp.float32)
    grad_up = jnp.einsum("td,tf->df", rows_all, up_grad_low, preferred_element_type=jnp.float32)
    grad_gate = jnp.einsum("td,tf->df", rows_all, gate_grad_low, preferred_element_type=jnp.float32)
    first = jnp.einsum("tf,df->td", up_grad_low, up_full, preferred_element_type=jnp.float32)
    d_hidden_one = (1.0 - mix_mlp) * d_resid_two + lax.psum_scatter(
        (
            first
            + jnp.einsum("tf,df->td", gate_grad_low, gate_full, preferred_element_type=jnp.float32)
        ).astype(jnp.bfloat16),
        "tensor",
        scatter_dimension=0,
        tiled=True,
    ).astype(jnp.float32)
    d_resid_one = rms_back(d_hidden_one, hidden_one, resid_one)
    grad_mix_attn = jnp.sum(d_resid_one * (h_attn - inputs), axis=0)
    d_branch_a = rms_back(mix_attn * d_resid_one, h_attn, branch_a).astype(jnp.bfloat16)
    grad_out = jnp.einsum("tc,td->cd", attended_low, d_branch_a, preferred_element_type=jnp.float32)
    d_attended = jnp.einsum(
        "td,cd->tc", d_branch_a, out_full, preferred_element_type=jnp.float32
    ).astype(jnp.bfloat16)
    d_heads = d_attended.reshape(row_count, head_count, HEAD_DIM)
    row_delta = jnp.sum(d_heads.astype(jnp.float32) * attended, axis=-1).T
    key_back, value_back = (
        lax.all_gather(keys_low, "tensor", axis=0, tiled=True),
        lax.all_gather(values_low, "tensor", axis=0, tiled=True),
    )

    def score_grads(key_start, key_count):
        attn_probs = probs_for(key_back, key_start, key_count)
        d_probs = jnp.einsum(
            "qhd,khd->hqk",
            d_heads,
            value_part(value_back, key_start, key_count),
            preferred_element_type=jnp.float32,
        )
        d_scores = (attn_probs * (d_probs - row_delta[..., None])).astype(jnp.bfloat16)
        return (attn_probs, d_scores)

    def query_step(carry_sum, block_index):
        key_start = block_index * key_block
        attn_probs, d_scores = score_grads(key_start, key_block)
        key_part = lax.dynamic_slice_in_dim(key_back, key_start, key_block).reshape(
            key_block, head_count, HEAD_DIM
        )
        return (
            carry_sum
            + jnp.einsum("hqk,khd->qhd", d_scores, key_part, preferred_element_type=jnp.float32),
            None,
        )

    d_query, _ = lax.scan(
        query_step, jnp.zeros((row_count, head_count, HEAD_DIM), jnp.float32), jnp.arange(blocks)
    )
    d_query = d_query.reshape(row_count, model_width) * score_scale
    part_rows = lax.axis_size("tensor") * row_count
    sub_block = block_span(part_rows, row_count)

    def one_block(block_index):
        begin = block_index * sub_block
        attn_probs, d_scores = score_grads(begin, sub_block)
        d_keys = (
            jnp.einsum("hqk,qhd->khd", d_scores, query_heads, preferred_element_type=jnp.float32)
            * score_scale
        )
        d_values = jnp.einsum(
            "hqk,qhd->khd",
            attn_probs.astype(jnp.bfloat16),
            d_heads,
            preferred_element_type=jnp.float32,
        )
        return jnp.concatenate(
            [d_keys.reshape(sub_block, model_width), d_values.reshape(sub_block, model_width)],
            axis=1,
        )

    block_terms = lax.map(one_block, jnp.arange(part_rows // sub_block))
    key_grads = lax.psum_scatter(
        block_terms.reshape(part_rows, 2 * model_width).astype(jnp.bfloat16),
        "tensor",
        scatter_dimension=0,
        tiled=True,
    ).astype(jnp.float32)
    d_keys_own = key_grads[:, :model_width]
    d_values_own = key_grads[:, model_width:]
    grad_gain = jnp.sum(d_query * q_unit + d_keys_own * k_unit, axis=0)
    d_qkv = jnp.concatenate(
        [
            unit_back(d_query * gain_qk, q_unit, q_factor),
            unit_back(d_keys_own * gain_qk, k_unit, k_factor),
            d_values_own,
        ],
        axis=1,
    ).astype(jnp.bfloat16)
    grad_qkv = jnp.einsum("tc,tf->cf", tokens, d_qkv, preferred_element_type=jnp.float32)
    d_tokens = (1.0 - mix_attn) * d_resid_one + jnp.einsum(
        "tf,cf->tc", d_qkv, qkv_full, preferred_element_type=jnp.float32
    )
    sum_qkv, sum_out, sum_gain, sum_mix_attn, sum_mix_mlp = (
        lax.psum_scatter(grad_qkv, ("dp", "tensor"), scatter_dimension=0, tiled=True),
        lax.psum_scatter(grad_out, ("dp", "tensor"), scatter_dimension=0, tiled=True),
        lax.psum_scatter(grad_gain, ("dp", "tensor"), scatter_dimension=0, tiled=True),
        lax.psum_scatter(grad_mix_attn, ("dp", "tensor"), scatter_dimension=0, tiled=True),
        lax.psum_scatter(grad_mix_mlp, ("dp", "tensor"), scatter_dimension=0, tiled=True),
    )
    sum_up, sum_gate, sum_down = (
        lax.psum_scatter(
            grad_up.astype(jnp.bfloat16), "dp", scatter_dimension=0, tiled=True
        ).astype(jnp.float32),
        lax.psum_scatter(
            grad_gate.astype(jnp.bfloat16), "dp", scatter_dimension=0, tiled=True
        ).astype(jnp.float32),
        lax.psum_scatter(
            grad_down.astype(jnp.bfloat16), "dp", scatter_dimension=0, tiled=True
        ).astype(jnp.float32),
    )
    sum_scale_up, sum_scale_gate = lax.psum((grad_scale_up, grad_scale_gate), "dp")
    stat_sums = lax.psum(partial_stats, ("dp", "tensor"))
    entry_count = row_count * model_width * lax.axis_size("dp") * spread
    stream_rms = jnp.sqrt(stat_sums / entry_count)
    return (
        result.astype(jnp.bfloat16),
        d_tokens.astype(jnp.bfloat16),
        sum_qkv,
        sum_out,
        sum_gain,
        sum_mix_attn,
        sum_mix_mlp,
        sum_up,
        sum_gate,
        sum_down,
        sum_scale_up,
        sum_scale_gate,
        stream_rms,
    )


MESH = pl.DeviceIdType.MESH
BF16 = jnp.bfloat16
F32 = jnp.float32
LOG2E = 1.4426950408889634
COPIES = 224
VMEM_BYTES = 63 * 2**20
CH = 32


def nn(left, right):
    return lax.dot_general(left, right, (((1,), (0,)), ((), ())), preferred_element_type=F32)


def nt(left, right):
    return lax.dot_general(left, right, (((1,), (1,)), ((), ())), preferred_element_type=F32)


def tn(left, right):
    return lax.dot_general(left, right, (((0,), (0,)), ((), ())), preferred_element_type=F32)


def flip(index, bits):
    bit = 1
    while bit <= bits:
        if bits & bit:
            index = index + bit - 2 * bit * lax.rem(lax.div(index, bit), 2)
        bit *= 2
    return index


def mean_rows(value):
    return jnp.mean(value, axis=-1, keepdims=True)


def rows(start, count=256):
    return pl.ds(pl.multiple_of(start * count, count), count)


def block(r):
    return pl.ds(r * 256, 256)


def fused_kernel(
    tokens, cotangent, bucket_start, w_qkv, w_out, s_qk, alpha_a, alpha_m, w_up, w_gate, w_down, scale_u,
    scale_v,
    layer_hbm, tokens_hbm, qkv_hbm, out_hbm, up_hbm, gate_hbm, down_hbm, stats_out,
    layer_out, grad_tokens, grad_qkv, grad_out, grad_up, grad_gate, grad_down,
    tok, cot, wq, wo, wu, wg, wd, small, small_t, small_d, gains,
    raw, qkv, linv, att, ato, branch, hid, h1, ur, gr, inn,
    part, from_core3, from_core1, from_y,
    dr2, dr1, d_inner_f32, db, dba, dat, dao, dqkv, delta,
    gd, x_down, x_up, x_gate, x_qkv, x_out, z_down, z_up, z_gate, z_qkv, z_out,
    o_core3, o_core1, o_y, osum, q_sum, q_piece, stats, s_tensor, s_x, s_z,
    send_sem, recv_sem, local_sem,
):
    d = lax.axis_index("dp")
    t = lax.axis_index("tensor")
    z = lax.div(d, 2)
    inner = lax.rem(lax.div(z + 1, 2), 2) == 1
    core, ynb, diag = (d, flip(t, 1)), (d, flip(t, 2)), (d, flip(t, 3))
    tensor_peer = {1: core, 2: ynb, 3: diag}
    xnb = (flip(d, 1), t)
    z_peer = {m: (flip(d, m), t) for m in (2, 4, 6)}

    barrier = pltpu.get_barrier_semaphore()
    peers = [core, ynb, diag, xnb] + [z_peer[m] for m in (2, 4, 6)]
    for peer in peers:
        pl.semaphore_signal(barrier, inc=1, device_id=peer, device_id_type=MESH)

    issued = []
    used = [0]

    def number():
        used[0] += 1
        return used[0] - 1

    def describe(src, dst, peer, at, to):
        return pltpu.make_async_remote_copy(
            src_ref=src,
            dst_ref=dst,
            send_sem=send_sem.at[at],
            recv_sem=recv_sem.at[to],
            device_id=peer,
            device_id_type=MESH,
        )

    def send(src, dst, peer):
        at = number()
        copy = describe(src, dst, peer, at, at)
        copy.start()
        issued.append(copy)
        return copy

    waited = set()

    def sent(copy):
        if id(copy) not in waited:
            waited.add(id(copy))
            copy.wait_send()

    locals_ = []

    def bring(src, dst):
        copy = pltpu.make_async_copy(src, dst, local_sem.at[len(locals_)])
        copy.start()
        locals_.append(copy)
        return copy

    outer = jnp.logical_not(inner)

    class Gather:
        def __init__(self, src, view):
            self.src, self.view = src, view
            self.at6, self.relay_at = number(), number()

        def start_x(self):
            self.x = [send(self.src, self.view(d), xnb)]

        def start_far(self):
            self.z = {4: send(self.src, self.view(d), z_peer[4])}
            self.straight = describe(self.src, self.view(d), z_peer[6], self.at6, self.at6)
            pl.when(inner)(self.straight.start)

        def start_near(self):
            self.z[2] = send(self.src, self.view(d), z_peer[2])

        def start_z(self):
            self.start_far()
            self.start_near()

        def hop(self):
            self.z[4].wait_recv()
            shard = self.view(flip(d, 4))
            self.relay = describe(shard, shard, z_peer[2], self.relay_at, self.at6)
            pl.when(inner)(self.relay.start)

        def forward_one(self, m):
            if m == 2:
                self.z[2].wait_recv()
            if m == 6:
                self.straight.wait_recv()
            shard = self.view(flip(d, m))
            self.x.append(send(shard, shard, xnb))

        def forward(self):
            self.forward_one(2)
            self.hop()
            self.forward_one(4)
            self.forward_one(6)

        def finish(self):
            for copy in self.x:
                copy.wait_recv()

        def release(self):
            for copy in [*self.z.values(), *self.x]:
                sent(copy)
            for copy in (self.straight, self.relay):
                pl.when(inner)(copy.wait_send)

    class GatherPairs(Gather):
        def __init__(self, src, shard, pair):
            super().__init__(src, pair)
            self.shard = shard

        def start_x(self):
            self.x = [send(self.src, self.shard(d), xnb)]

        def start_far(self):
            self.x[0].wait_recv()
            self.src = self.view(d)
            super().start_far()

    def rows_of(ref, count=128):
        return lambda index: ref.at[rows(index, count)]

    def pair_of(ref):
        return lambda index: ref.at[rows(lax.div(index, 2))]

    take_qkv = Gather(wq.at[:, rows(d, 128), :], lambda index: wq.at[:, rows(index, 128), :])
    take_small = Gather(small_d.at[:, rows(d, 128)], lambda index: small_d.at[:, rows(index, 128)])
    take_out = Gather(w_out, lambda index: wo.at[index, t])
    take_up = Gather(w_up, rows_of(wu))
    take_gate = Gather(w_gate, rows_of(wg))
    take_down = GatherPairs(w_down, rows_of(wd), pair_of(wd))

    piece = s_qk.shape[1]
    own_qkv = pl.ds(pl.multiple_of(d * 128 + t * 32, 32), 32)

    def qkv_cols(slot, pair, j):
        return pl.ds(pl.multiple_of(j * 1024 + slot * 256 + pair * 128, 128), 128)

    def qkv_place(pair, j):
        return wq.at[pair, own_qkv, j * 128 : j * 128 + 128]

    parts_of_qkv = [(pair, j) for pair in range(2) for j in range(3)]
    local_qkv = [
        bring(w_qkv.at[:, qkv_cols(t, pair, j)], qkv_place(pair, j)) for pair, j in parts_of_qkv
    ]
    local_tok = bring(tokens, tok.at[block(0)])
    local_rest = [
        bring(w_out, wo.at[d, t]),
        bring(w_up, wu.at[rows(d, 128)]),
        bring(w_gate, wg.at[rows(d, 128)]),
        bring(w_down, wd.at[rows(d, 128)]),
        bring(cotangent, cot),
    ]
    place = jnp.where(
        lax.broadcasted_iota(jnp.int32, (piece, 128), 1)
        == lax.broadcasted_iota(jnp.int32, (piece, 128), 0) + t * piece,
        1.0,
        0.0,
    ).astype(BF16)
    small_row = lax.broadcasted_iota(jnp.int32, (16, 128), 0)
    placed = jnp.zeros((16, 128), F32)
    for index, vector in enumerate((s_qk, alpha_a, alpha_m)):
        placed = jnp.where(small_row == index, nn(vector[...], place), placed)
    small[...] = placed.astype(BF16)
    stats[...] = jnp.zeros_like(stats)
    pl.semaphore_wait(barrier, len(peers))

    small_sends = [send(small, small_t.at[r - 1], tensor_peer[r]) for r in (2, 3, 1)]
    qkv_sends = [
        send(w_qkv.at[:, qkv_cols(flip(t, r), pair, j)], qkv_place(pair, j), tensor_peer[r])
        for r in (2, 3, 1)
        for pair, j in parts_of_qkv
    ]
    take_out.start_z()
    take_down.start_x()
    take_out.start_x()
    for copy in small_sends:
        copy.wait_recv()
    small_d[:, rows(d, 128)] = small[...] + small_t[0] + small_t[1] + small_t[2]
    take_small.start_z()
    take_small.start_x()
    for copy in local_qkv:
        copy.wait()
    for copy in qkv_sends:
        copy.wait_recv()
    take_qkv.start_z()
    take_qkv.start_x()
    tok_y = send(tokens, tok.at[block(2)], ynb)
    tok_core = send(tokens, tok.at[block(1)], core)
    take_up.start_far()

    take_out.forward()
    take_small.forward()
    take_qkv.hop()
    take_qkv.forward_one(4)
    take_up.start_near()
    take_up.start_x()
    take_qkv.forward_one(2)
    take_qkv.forward_one(6)
    take_gate.start_far()
    tok_y.wait_recv()
    tok_diag = send(tok.at[block(2)], tok.at[block(3)], core)
    take_small.finish()
    gains[...] = small_d[...].astype(F32)
    take_qkv.finish()
    local_tok.wait()
    tok_core.wait_recv()
    tok_diag.wait_recv()

    def gain_pair(pair):
        gain = gains[0:1, pl.ds(pl.multiple_of(t * 256 + pair * 128, 128), 128)]
        return jnp.concatenate([gain, gain], axis=1)

    first_head = lax.broadcasted_iota(jnp.int32, (256, 128), 1) < HEAD_DIM
    same_head = jnp.where(
        lax.div(lax.broadcasted_iota(jnp.int32, (256, 256), 0), HEAD_DIM)
        == lax.div(lax.broadcasted_iota(jnp.int32, (256, 256), 1), HEAD_DIM),
        1.0,
        0.0,
    ).astype(BF16)

    def head_sum(value):
        high = value.astype(BF16)
        low = (value - high.astype(F32)).astype(BF16)
        return nn(high, same_head) + nn(low, same_head)

    def qkv_step(r, carry):
        at = rows(r)
        x = tok[at, :]
        for pair in range(2):
            y = nn(x, wq[pair])
            qk = y[:, :256]
            raw[pair, at, :] = qk
            factor = lax.rsqrt(head_sum(qk * qk) + EPSILON)
            qkv[pair, at, :256] = (qk * factor * gain_pair(pair)).astype(BF16)
            qkv[pair, at, 256:] = y[:, 256:].astype(BF16)
        return carry

    lax.fori_loop(0, 4, qkv_step, 0)

    def true_rows(i):
        return rows(flip(t, i))

    whole = jnp.where(bucket_start[d * 4] == bucket_start[d * 4 + 2], 1.0, 0.0)
    row_id = lax.broadcasted_iota(jnp.int32, (256, 256), 0)
    col_id = lax.broadcasted_iota(jnp.int32, (256, 256), 1)
    exp_scale = math.sqrt(HEAD_DIM) * LOG2E

    def two_heads(value):
        zero = jnp.zeros_like(value)
        return jnp.concatenate(
            [jnp.where(first_head, value, zero), jnp.where(first_head, zero, value)], axis=0
        )

    def one_of_two(value):
        return jnp.where(first_head, value[:256], value[256:])

    causal = jnp.concatenate([col_id <= row_id] * 2, axis=0)

    def attend(i):
        at = true_rows(i)

        def head_step(pair, carry):
            q = two_heads(qkv[pair, at, 0:128])
            acc = jnp.zeros((512, 128), F32)
            weight = jnp.zeros((512, 1), F32)
            for j in range(i + 1):
                key_at = true_rows(j)
                e = jnp.exp2(nt(q, qkv[pair, key_at, 128:256]) * exp_scale)
                if j == i:
                    e = jnp.where(causal, e, 0.0)
                elif j // 2 != i // 2:
                    e = e * whole
                weight = weight + jnp.sum(e, axis=1, keepdims=True)
                acc = acc + nn(e.astype(BF16), qkv[pair, key_at, 256:384])
            inverse = 1.0 / weight
            lanes = rows(pair, 128)
            linv[at, lanes] = one_of_two(jnp.broadcast_to(inverse, (512, 128)))
            att[at, lanes] = one_of_two(acc * inverse).astype(BF16)
            return carry

        lax.fori_loop(0, 2, head_step, 0)

    attend(0)
    attend(1)
    take_up.hop()
    take_up.forward_one(4)
    take_gate.start_near()
    take_gate.start_x()
    take_up.forward_one(2)
    take_up.forward_one(6)
    for copy in local_rest[1:]:
        copy.wait()
    take_down.start_far()
    attend(2)
    attend(3)

    att_sends = [send(att.at[block(r)], ato.at[t], tensor_peer[r]) for r in (2, 3, 1)]
    ato[t] = att[block(0), :]
    take_out.finish()
    local_rest[0].wait()
    wo_y = send(wo.at[:, t], wo.at[:, t], ynb)
    wo_core = send(wo.at[:, t], wo.at[:, t], core)
    wo_y.wait_recv()
    wo_far = send(wo.at[:, flip(t, 2)], wo.at[:, flip(t, 2)], core)
    for copy in att_sends:
        copy.wait_recv()
    wo_core.wait_recv()
    wo_far.wait_recv()

    def out_rows(slot, columns):
        return wo[2 * slot : 2 * slot + 2, :, :, columns].reshape(256, 256)

    def out_step(n, carry):
        at = rows(n)
        acc = nn(ato[0], out_rows(0, at))
        for slot in range(1, 4):
            acc = acc + nn(ato[slot], out_rows(slot, at))
        branch[:, at] = acc
        return carry

    lax.fori_loop(0, 4, out_step, 0)

    mix_a = gains[1:2, :]
    mix_m = gains[2:3, :]

    def add_stat(row, value):
        stats[row : row + 1, :] = stats[row : row + 1, :] + jnp.sum(value, axis=0, keepdims=True)

    def first_norm(at):
        x = tok[at, :].astype(F32)
        ba = branch[at, :]
        fa = lax.rsqrt(mean_rows(ba * ba) + EPSILON)
        ha = ba * fa
        r1 = x + mix_a * (ha - x)
        f1 = lax.rsqrt(mean_rows(r1 * r1) + EPSILON)
        return x, ba, fa, ha, f1, r1 * f1

    def norm_step(c, carry):
        at = rows(c, CH)
        _, ba, _, _, _, hidden = first_norm(at)
        add_stat(3, ba * ba)
        hid[at, :] = hidden
        h1[at, :] = hidden.astype(BF16)
        return carry

    lax.fori_loop(0, 256 // CH, norm_step, 0)

    def spread(ref):
        return send(ref.at[block(0)], ref.at[block(2)], ynb), send(
            ref.at[block(0)], ref.at[block(1)], core
        )

    def relay(ref, from_ynb):
        from_ynb.wait_recv()
        return send(ref.at[block(2)], ref.at[block(3)], core)

    h1_y, h1_core = spread(h1)
    take_gate.hop()
    take_gate.forward_one(4)
    take_down.start_near()
    take_gate.forward_one(2)
    take_gate.forward_one(6)
    h1_far = relay(h1, h1_y)
    take_up.finish()
    h1_core.wait_recv()
    h1_far.wait_recv()
    take_gate.finish()

    def up_step(r, carry):
        at = rows(r)
        hidden = h1[at, :]
        u_raw = nn(hidden, wu[...])
        g_raw = nn(hidden, wg[...])
        gate = g_raw * scale_v[...].astype(F32)
        silu = gate / (1.0 + jnp.exp(-gate))
        ur[at, :] = u_raw.astype(BF16)
        gr[at, :] = g_raw.astype(BF16)
        inn[at, :] = (u_raw * scale_u[...].astype(F32) * silu).astype(BF16)
        return carry

    lax.fori_loop(0, 4, up_step, 0)

    class Reduce:
        def __init__(self, which, before, make):
            self.which, self.before, self.make = which, before, make
            self.copies = {}

        def run(self, order):
            for r in order:
                self.step(r)

        def step(self, r):
            k = self.which
            if r in self.before.copies:
                before = self.before.copies[r]
                for copy in before if isinstance(before, list) else [before]:
                    sent(copy)
            self.make(r)
            if r == 3:
                self.copies[3] = send(part.at[block(3)], from_core3.at[k], core)
            elif r == 2:
                self.copies[3].wait_recv()
                part[block(2), :] = (
                    part[block(2), :].astype(F32) + from_core3[k].astype(F32)
                ).astype(BF16)
                self.copies[2] = send(part.at[block(2)], from_y.at[k], ynb)
            elif r == 1:
                self.copies[1] = send(part.at[block(1)], from_core1.at[k], core)

        def finish(self):
            self.copies[1].wait_recv()
            self.copies[2].wait_recv()

        def at(self, where):
            k = self.which
            return (
                part[where, :].astype(F32)
                + from_core1[k, where, :].astype(F32)
                + from_y[k, where, :].astype(F32)
            )

    class ReduceColumns:
        def __init__(self):
            self.copies = {r: [] for r in (1, 2, 3)}
            self.columns = []

        def step(self, k):
            cols = rows(lax.div(flip(d, 2 * k), 2))
            part[:, cols] = nt(inn[...], wd[cols, :]).astype(BF16)
            self.columns.append(cols)
            self.copies[3].append(send(part.at[block(3), cols], from_core3.at[0, :, cols], core))
            self.copies[1].append(send(part.at[block(1), cols], from_core1.at[0, :, cols], core))

        def pass_on(self):
            done = len(self.copies[2])
            cols = self.columns[done]
            self.copies[3][done].wait_recv()
            part[block(2), cols] = (
                part[block(2), cols].astype(F32) + from_core3[0, :, cols].astype(F32)
            ).astype(BF16)
            self.copies[2].append(send(part.at[block(2), cols], from_y.at[0, :, cols], ynb))

        def finish(self):
            for r in (1, 2):
                for copy in self.copies[r]:
                    copy.wait_recv()

        at = Reduce.at
        which = 0

    sum_m = ReduceColumns()
    sum_m.step(0)
    take_down.z[2].wait_recv()
    take_down.hop()
    sum_m.pass_on()
    sum_m.step(1)
    sum_m.pass_on()
    sum_m.step(2)
    sum_m.pass_on()
    take_down.straight.wait_recv()
    sum_m.step(3)
    sum_m.pass_on()
    sum_m.finish()

    def loss_step(c, carry):
        at = rows(c, CH)
        bm = sum_m.at(at)
        hidden = hid[at, :]
        fm = lax.rsqrt(mean_rows(bm * bm) + EPSILON)
        hm = bm * fm
        r2 = hidden + mix_m * (hm - hidden)
        f2 = lax.rsqrt(mean_rows(r2 * r2) + EPSILON)
        result = r2 * f2
        layer_out[at, :] = result.astype(BF16)
        up = cot[at, :].astype(F32)
        grad = f2 * (up - result * mean_rows(up * result))
        dr2[at, :] = grad
        add_stat(1, grad * (hm - hidden))
        add_stat(4, bm * bm)
        add_stat(5, r2 * r2)
        c_m = mix_m * grad
        db[at, :] = (fm * (c_m - hm * mean_rows(c_m * hm))).astype(BF16)
        return carry

    lax.fori_loop(0, 256 // CH, loss_step, 0)

    db_y, db_core = spread(db)

    class AlongZ:
        def __init__(self, view, landing):
            self.view, self.landing = view, landing
            self.at6, self.relay_at = number(), number()
            self.z = {}

        def push(self, k):
            shard = self.view(flip(d, 2 * k))
            if k == 3:
                self.straight = describe(
                    shard, self.landing.at[2], z_peer[6], self.at6, self.at6
                )
                self.relay = describe(
                    shard, self.landing.at[3], z_peer[2], self.relay_at, self.relay_at
                )
                pl.when(inner)(self.straight.start)
                pl.when(outer)(self.relay.start)
            elif k == 2:

                @pl.when(inner)
                def _():
                    self.relay.wait_recv()
                    shard[...] = (shard[...].astype(F32) + self.landing[3].astype(F32)).astype(BF16)

                self.z[2] = send(shard, self.landing.at[1], z_peer[4])
            else:
                self.z[1] = send(shard, self.landing.at[0], z_peer[2])

        def total_into(self, out):
            self.z[1].wait_recv()
            self.z[2].wait_recv()
            out[...] = (
                self.view(d)[...].astype(F32)
                + self.landing[0].astype(F32)
                + self.landing[1].astype(F32)
            ).astype(out.dtype)

            @pl.when(inner)
            def _():
                self.straight.wait_recv()
                out[...] = (out[...].astype(F32) + self.landing[2].astype(F32)).astype(out.dtype)

        def settle(self):
            pl.when(inner)(self.straight.wait_send)
            pl.when(outer)(self.relay.wait_send)

    class Scatter(AlongZ):
        def __init__(self, view, from_x, landing):
            super().__init__(view, landing)
            self.from_x = from_x
            self.x = {}

        def ship(self, k):
            self.x[k] = send(self.view(flip(d, 2 * k + 1)), self.from_x.at[k], xnb)

        def fold(self, k):
            self.x[k].wait_recv()
            own = self.view(flip(d, 2 * k))
            own[...] = (own[...].astype(F32) + self.from_x[k].astype(F32)).astype(BF16)
            if k in (1, 3):
                self.push(k)

    def weight_grad(left, right, out, ship):
        for k in (3, 1, 2, 0):
            at = rows(lax.div(flip(d, 2 * k), 2))

            out[at, :] = tn(left[:, at], right[...]).astype(BF16)
            ship(k)

    def make_hidden(r):
        at = block(r)
        d_inner_f32[...] = nn(db[at, :], wd[...])

        def inner_step(c, carry):
            here = rows(c, CH)
            where = pl.ds(pl.multiple_of(r * 256 + c * CH, CH), CH)
            d_inner = d_inner_f32[here, :]
            u_raw = ur[where, :].astype(F32)
            g_raw = gr[where, :].astype(F32)
            gain_u = scale_u[...].astype(F32)
            gain_v = scale_v[...].astype(F32)
            gate = g_raw * gain_v
            sig = 1.0 / (1.0 + jnp.exp(-gate))
            up = u_raw * gain_u
            d_up = d_inner * (gate * sig)
            d_gate = d_inner * up * (sig * (1.0 + gate * (1.0 - sig)))
            add_stat(6, d_up * u_raw)
            add_stat(7, d_gate * g_raw)
            ur[where, :] = (d_up * gain_u).astype(BF16)
            gr[where, :] = (d_gate * gain_v).astype(BF16)
            return carry

        lax.fori_loop(0, 256 // CH, inner_step, 0)
        part[at, :] = (nt(ur[at, :], wu[...]) + nt(gr[at, :], wg[...])).astype(BF16)

    sum_h = Reduce(1, sum_m, make_hidden)
    db_core.wait_recv()
    sum_h.run((1, 0))
    db_far = relay(db, db_y)
    db_far.wait_recv()
    sum_down = AlongZ(pair_of(gd), z_down)
    weight_grad(db, inn, gd, lambda k: sum_down.push(k) if k in (1, 3) else None)
    sum_h.run((3, 2))
    sum_down.push(2)

    gu, gg, go = wd, wu, wg
    for gather in (take_down, take_up, take_gate):
        gather.release()
    sum_up = Scatter(rows_of(gu), x_up, z_up)
    sum_gate = Scatter(rows_of(gg), x_gate, z_gate)
    weight_grad(h1, ur, gu, sum_up.ship)
    weight_grad(h1, gr, gg, sum_gate.ship)
    sum_h.finish()

    def mid_step(c, carry):
        at = rows(c, CH)
        x, _, fa, ha, f1, hidden = first_norm(at)
        d_hidden = (1.0 - mix_m) * dr2[at, :] + sum_h.at(at)
        grad = f1 * (d_hidden - hidden * mean_rows(d_hidden * hidden))
        dr1[at, :] = grad
        add_stat(0, grad * (ha - x))
        c_a = mix_a * grad
        dba[at, :] = (fa * (c_a - ha * mean_rows(c_a * ha))).astype(BF16)
        return carry

    lax.fori_loop(0, 256 // CH, mid_step, 0)

    dat_sends = []
    for r in (2, 3, 1, 0):
        slot = flip(t, r)
        weight = wo[pl.ds(2 * slot, 2)].reshape(256, 1024)
        value = nt(dba[...], weight).astype(BF16)
        if r:
            dat[r - 1] = value
            dat_sends.append(send(dat.at[r - 1], dao.at[block(r)], tensor_peer[r]))
        else:
            dao[block(0), :] = value
    for slot in range(4):
        g = tn(ato[slot], dba[...]).astype(BF16)
        for q in range(8):
            start = (q % 4) * 256 + (2 * slot + q // 4) * 32
            go[start : start + 32, :] = g[q * 32 : (q + 1) * 32, :]

    def go_rows(r):
        return rows(flip(t, r))

    go_core3 = send(go.at[go_rows(3)], o_core3, core)
    go_core1 = send(go.at[go_rows(1)], o_core1, core)
    go_core3.wait_recv()
    go[go_rows(2), :] = (go[go_rows(2), :].astype(F32) + o_core3[...].astype(F32)).astype(BF16)
    go_y = send(go.at[go_rows(2)], o_y, ynb)
    sum_up.fold(3)
    sum_up.fold(1)

    head_rows = jnp.where(
        lax.broadcasted_iota(jnp.int32, (8, 256), 0)
        == lax.div(lax.broadcasted_iota(jnp.int32, (8, 256), 1), HEAD_DIM),
        1.0,
        0.0,
    ).astype(BF16)
    for copy in att_sends:
        sent(copy)

    def ready_step(r, carry):
        at = rows(r)
        scaled = (dao[at, :].astype(F32) * linv[at, :]).astype(BF16)
        dao[at, :] = scaled
        product = scaled.astype(F32) * att[at, :].astype(F32)
        high = product.astype(BF16)
        low = (product - high.astype(F32)).astype(BF16)
        delta[r] = nt(head_rows, high) + nt(head_rows, low)
        return carry

    key_grads, query_grads = branch, hid
    seen = jnp.concatenate([row_id <= col_id] * 2, axis=1)

    def lanes_of(r, half=0):
        return pl.ds(pl.multiple_of(r * 128 + half * 512, 128), 128)

    def attend_back(pair, query_r, key_r, visible):
        query_at, key_at = rows(query_r), rows(key_r)
        q = two_heads(qkv[pair, query_at, 0:128])
        do = two_heads(dao[query_at, pair * 128 : pair * 128 + 128])
        keys = qkv[pair, key_at, 128:256]
        e = visible(jnp.exp2(nt(keys, q) * exp_scale))
        d_prob = nt(qkv[pair, key_at, 256:384], do)
        shift = jnp.concatenate(
            [delta[query_r, 2 * pair + h : 2 * pair + h + 1, :] for h in range(2)], axis=1
        )
        d_score = (e * (d_prob - shift)).astype(BF16)
        key_grads[:, lanes_of(key_r)] += nn(d_score, q)
        key_grads[:, lanes_of(key_r, 1)] += nn(e.astype(BF16), do)
        query_grads[:, lanes_of(query_r)] += one_of_two(tn(d_score, keys))

    def diagonal(pair):
        def diagonal_step(r, carry):
            attend_back(pair, r, r, lambda e: jnp.where(seen, e, 0.0))
            return carry

        return diagonal_step

    def mixed(a, b):
        low = lax.rem(a, 2) + lax.rem(b, 2) - 2 * lax.rem(a, 2) * lax.rem(b, 2)
        high_a, high_b = lax.div(a, 2), lax.div(b, 2)
        return low + 2 * (high_a + high_b - 2 * high_a * high_b)

    def below(pair):
        def below_step(n, carry):
            i = 1 + lax.div(n, 3) + lax.div(n + 4, 5)
            j = n - lax.div(i * (i - 1), 2)
            apart = (lax.div(i, 2) - lax.div(j, 2)).astype(F32)
            factor = 1.0 - apart + apart * whole
            attend_back(pair, mixed(i, t), mixed(j, t), lambda e: e * factor)
            return carry

        return below_step

    def clear():
        key_grads[...] = jnp.zeros_like(key_grads)
        query_grads[...] = jnp.zeros_like(query_grads)

    def qkv_back(pair):
        scale = math.sqrt(HEAD_DIM)
        gain = gain_pair(pair)
        column = pl.ds(pl.multiple_of(t * 256 + pair * 128, 128), 128)

        def back_qkv_step(r, carry):
            at = rows(r)
            y = raw[pair, at, :]
            factor = lax.rsqrt(head_sum(y * y) + EPSILON)
            w = y * factor
            grad = (
                jnp.concatenate([query_grads[:, lanes_of(r)], key_grads[:, lanes_of(r)]], axis=1)
                * scale
            )
            both = jnp.sum(grad * w, axis=0, keepdims=True)
            stats[2:3, column] = stats[2:3, column] + both[:, :128] + both[:, 128:]
            c = grad * gain
            dqkv[pair, at, :256] = (factor * (c - w * head_sum(c * w))).astype(BF16)
            dqkv[pair, at, 256:] = key_grads[:, lanes_of(r, 1)].astype(BF16)
            return carry

        lax.fori_loop(0, 4, back_qkv_step, 0)

    gq = qkv

    def qkv_shard(pair):
        return lambda index: gq.at[pair, rows(index, 128), :]

    sum_qkv = [Scatter(qkv_shard(pair), x_qkv.at[pair], z_qkv.at[pair]) for pair in range(2)]

    def qkv_weight(pair):
        for k in (3, 1, 2, 0):
            at = rows(lax.div(flip(d, 2 * k), 2))
            gq[pair, at, :] = tn(tok[:, at], dqkv[pair]).astype(BF16)
            sum_qkv[pair].ship(k)

    clear()
    dat_sends[2].wait_recv()
    lax.fori_loop(0, 2, ready_step, 0)
    lax.fori_loop(0, 2, diagonal(0), 0)
    sum_up.fold(2)
    sum_up.push(2)
    sum_up.fold(0)
    dat_sends[0].wait_recv()
    dat_sends[1].wait_recv()
    lax.fori_loop(2, 4, ready_step, 0)
    lax.fori_loop(2, 4, diagonal(0), 0)
    go_core1.wait_recv()
    go_y.wait_recv()
    osum[...] = (
        go[go_rows(0), :].astype(F32) + o_core1[...].astype(F32) + o_y[...].astype(F32)
    ).astype(BF16)
    sum_out = Scatter(rows_of(osum, 32), x_out, z_out)
    for k in (3, 1, 2, 0):
        sum_out.ship(k)
    lax.fori_loop(0, 6, below(0), 0)
    qkv_back(0)
    qkv_weight(0)
    clear()
    sum_gate.fold(3)
    sum_gate.fold(1)
    lax.fori_loop(0, 4, diagonal(1), 0)
    sum_gate.fold(2)
    sum_gate.push(2)
    sum_gate.fold(0)
    down_pair = pair_of(gd)(d)
    sum_down.total_into(down_pair)
    down_x = send(gd.at[rows(flip(d, 1), 128)], x_down, xnb)
    lax.fori_loop(0, 6, below(1), 0)
    qkv_back(1)
    qkv_weight(1)
    for k in (3, 1, 2, 0):
        sum_out.fold(k)
    sum_out.push(2)

    small_back = [send(stats, s_tensor.at[r - 1], tensor_peer[r]) for r in (1, 2, 3)]

    def make_tokens(r):
        part[block(r), :] = (
            nt(dqkv[0, block(r), :], wq[0]) + nt(dqkv[1, block(r), :], wq[1])
        ).astype(BF16)

    sum_t = Reduce(2, sum_h, make_tokens)
    sum_t.run((3, 2))
    for k in (3, 1, 2, 0):
        sum_qkv[0].fold(k)
    sum_qkv[0].push(2)
    sum_t.run((1, 0))
    for copy in small_back:
        copy.wait_recv()
    over_tensor = s_tensor[0] + s_tensor[1] + s_tensor[2]
    shared = lax.broadcasted_iota(jnp.int32, (8, 1024), 0) < 6
    s_x[0] = stats[...] + jnp.where(shared, over_tensor, 0.0)
    stat_x = send(s_x.at[0], s_x.at[1], xnb)
    for k in (3, 1, 2, 0):
        sum_qkv[1].fold(k)
    sum_qkv[1].push(2)

    outgoing = []

    def put(src, dst):
        outgoing.append(bring(src, dst))

    put(layer_out, layer_hbm)
    down_x.wait_recv()
    grad_down[...] = gd[rows(d, 128), :].astype(F32) + x_down[...].astype(F32)
    put(grad_down, down_hbm)
    sum_up.total_into(grad_up)
    put(grad_up, up_hbm)
    sum_gate.total_into(grad_gate)
    put(grad_gate, gate_hbm)
    sum_out.total_into(grad_out)
    put(grad_out, out_hbm)
    stat_x.wait_recv()
    s_z[0] = s_x[0] + s_x[1]
    stat_z = [send(s_z.at[0], s_z.at[k], z_peer[2 * k]) for k in (1, 2, 3)]
    for pair in range(2):
        sum_qkv[pair].total_into(q_sum.at[pair])
    q_sends = [
        send(q_sum.at[:, rows(flip(t, r), 32), :], q_piece.at[t], tensor_peer[r]) for r in (2, 3, 1)
    ]
    q_piece[t] = q_sum[:, rows(t, 32), :]
    sum_t.finish()

    def last_step(c, carry):
        at = rows(c, CH)
        grad_tokens[at, :] = ((1.0 - mix_a) * dr1[at, :] + sum_t.at(at)).astype(BF16)
        return carry

    lax.fori_loop(0, 256 // CH, last_step, 0)
    put(grad_tokens, tokens_hbm)
    for copy in stat_z:
        copy.wait_recv()
    stats_out[...] = s_z[0] + s_z[1] + s_z[2] + s_z[3]
    for copy in q_sends:
        copy.wait_recv()
    for slot in range(4):
        for pair, j in parts_of_qkv:
            start = j * 1024 + slot * 256 + pair * 128
            grad_qkv[:, start : start + 128] = q_piece[slot, pair, :, j * 128 : j * 128 + 128]
    put(grad_qkv, qkv_hbm)
    for gather in (take_qkv, take_small, take_out):
        gather.release()
    for scatter in (sum_down, sum_up, sum_gate, sum_out, *sum_qkv):
        scatter.settle()
    for copy in issued:
        sent(copy)
    for copy in outgoing:
        copy.wait()


def finish_kernel(entries, *refs):
    large, stats, outs, held, sems = refs[:7], refs[7], refs[8:18], refs[18:25], refs[25]
    taken = [pltpu.make_async_copy(large[i], held[i], sems.at[0, i]) for i in range(7)]
    given = [pltpu.make_async_copy(held[i], outs[i], sems.at[1, i]) for i in range(7)]
    for copy in taken:
        copy.start()
    own, scales, stream = outs[7:]
    index = lax.axis_index("dp") * lax.axis_size("tensor") + lax.axis_index("tensor")
    piece = own.shape[1]
    pick = lax.broadcasted_iota(jnp.int32, (1024, piece), 0) == (
        lax.broadcasted_iota(jnp.int32, (1024, piece), 1) + index * piece
    )
    own[...] = lax.dot_general(
        stats[0:3, :],
        jnp.where(pick, 1.0, 0.0),
        (((1,), (0,)), ((), ())),
        precision=lax.Precision.HIGHEST,
        preferred_element_type=F32,
    )
    scales[...] = stats[6:8, :]
    sums = jnp.sum(stats[3:6, :], axis=1, keepdims=True)
    stream[...] = jnp.broadcast_to(jnp.sqrt(sums / entries), stream.shape)
    for i in range(7):
        taken[i].wait()
        given[i].start()
    for copy in given:
        copy.wait()


def fits(mesh):
    return dict(mesh.shape) == {"dp": 8, "tensor": 4}


def fused(
    tokens, cotangent, bucket_start, w_qkv, w_out, s_qk, alpha_a, alpha_m, w_up, w_gate, w_down, s_u, s_v
):
    n_rows, width = tokens.shape
    piece = s_qk.shape[0]
    vmem = pl.BlockSpec(memory_space=pltpu.VMEM)
    smem = pl.BlockSpec(memory_space=pltpu.SMEM)
    hbm = pl.BlockSpec(memory_space=pl.ANY)
    bf = lambda *shape: pltpu.VMEM(shape, BF16)
    fl = lambda *shape: pltpu.VMEM(shape, F32)
    large = [
        jax.ShapeDtypeStruct(shape, kind)
        for shape, kind in (
            ((256, 1024), BF16), ((256, 1024), BF16), ((32, 3072), F32), ((32, 1024), F32),
            ((128, 1024), F32), ((128, 1024), F32), ((128, 1024), F32),
        )
    ]
    scratch = [
        *[pltpu.VMEM(leaf.shape, leaf.dtype) for leaf in large],
        bf(1024, 1024), bf(256, 1024), bf(2, 1024, 384), bf(8, 4, 32, 1024), bf(1024, 1024),
        bf(1024, 1024), bf(1024, 1024), bf(16, 128), bf(3, 16, 128), bf(16, 1024), fl(16, 1024),
        fl(2, 1024, 256), bf(2, 1024, 384), fl(1024, 256), bf(1024, 256), bf(4, 256, 256),
        fl(256, 1024), fl(256, 1024), bf(1024, 1024), bf(1024, 1024), bf(1024, 1024), bf(1024, 1024),
        bf(1024, 1024), bf(3, 256, 1024), bf(3, 256, 1024), bf(3, 256, 1024),
        fl(256, 1024), fl(256, 1024), fl(256, 1024), bf(1024, 1024), bf(256, 1024), bf(3, 256, 256),
        bf(1024, 256), bf(2, 1024, 384), fl(4, 8, 256),
        bf(1024, 1024), bf(128, 1024), bf(4, 128, 1024), bf(4, 128, 1024), bf(2, 4, 128, 384),
        bf(4, 32, 1024), bf(4, 256, 1024), bf(4, 128, 1024), bf(4, 128, 1024), bf(2, 4, 128, 384),
        bf(4, 32, 1024), bf(256, 1024), bf(256, 1024), bf(256, 1024), bf(256, 1024),
        fl(2, 128, 384), fl(4, 2, 32, 384), fl(8, 1024), fl(3, 8, 1024), fl(2, 8, 1024), fl(4, 8, 1024),
        pltpu.SemaphoreType.DMA((COPIES,)), pltpu.SemaphoreType.DMA((COPIES,)),
        pltpu.SemaphoreType.DMA((32,)),
    ]
    *big, stats = pl.pallas_call(
        fused_kernel,
        out_shape=[*large, jax.ShapeDtypeStruct((8, 1024), F32)],
        in_specs=[hbm, hbm, smem, hbm, hbm, vmem, vmem, vmem, hbm, hbm, hbm, vmem, vmem],
        out_specs=[*[hbm] * 7, vmem],
        scratch_shapes=scratch,
        compiler_params=pltpu.CompilerParams(
            collective_id=0, has_side_effects=True, vmem_limit_bytes=VMEM_BYTES
        ),
        cost_estimate=pl.CostEstimate(
            flops=27_000_000_000, bytes_accessed=8_000_000, transcendentals=10_000_000
        ),
    )(
        tokens, cotangent, bucket_start, w_qkv, w_out, s_qk[None, :], alpha_a[None, :],
        alpha_m[None, :], w_up, w_gate, w_down, s_u[None, :], s_v[None, :],
    )
    entries = n_rows * width * lax.axis_size("dp") * lax.axis_size("tensor")
    *big, own, scales, stream = pl.pallas_call(
        functools.partial(finish_kernel, float(entries)),
        out_shape=[
            *large,
            jax.ShapeDtypeStruct((3, piece), F32),
            jax.ShapeDtypeStruct((2, 1024), F32),
            jax.ShapeDtypeStruct((3, 128), F32),
        ],
        in_specs=[hbm] * 7 + [vmem],
        out_specs=[hbm] * 7 + [vmem] * 3,
        scratch_shapes=[*[pltpu.VMEM(leaf.shape, leaf.dtype) for leaf in large], pltpu.SemaphoreType.DMA((2, 7))],
    )(*big, stats)
    return (
        *big[:4], own[2], own[0], own[1], *big[4:], scales[0], scales[1], stream[:, 0],
    )


def solution(mesh):
    body = fused if fits(mesh) else local
    return jax.shard_map(
        body,
        mesh=mesh,
        in_specs=(
            P(("dp", "tensor"), None),
            P(("dp", "tensor"), None),
            P(),
            P(("dp", "tensor"), None),
            P(("dp", "tensor"), None),
            P(("dp", "tensor")),
            P(("dp", "tensor")),
            P(("dp", "tensor")),
            P("dp", "tensor"),
            P("dp", "tensor"),
            P("dp", "tensor"),
            P("tensor"),
            P("tensor"),
        ),
        out_specs=(
            P(("dp", "tensor"), None),
            P(("dp", "tensor"), None),
            P(("dp", "tensor"), None),
            P(("dp", "tensor"), None),
            P(("dp", "tensor")),
            P(("dp", "tensor")),
            P(("dp", "tensor")),
            P("dp", "tensor"),
            P("dp", "tensor"),
            P("dp", "tensor"),
            P("tensor"),
            P("tensor"),
            P(),
        ),
        check_vma=False,
    )
```

```python
import functools
import math

import jax
import jax.numpy as jnp
from jax import lax
from jax.experimental import pallas as pl
from jax.experimental.pallas import tpu as pltpu
from jax.sharding import PartitionSpec as P

HEAD_DIM = 64


EPSILON = 1e-06
MASKED_SCORE = -1e30


def rms_rows(value):
    return value * lax.rsqrt(jnp.mean(value * value, axis=-1, keepdims=True) + EPSILON)


def rms_back(upstream, normed, source):
    factor = lax.rsqrt(jnp.mean(source * source, axis=-1, keepdims=True) + EPSILON)
    return factor * (upstream - normed * jnp.mean(upstream * normed, axis=-1, keepdims=True))


def unit_heads(value):
    shaped = value.reshape(value.shape[0], -1, HEAD_DIM)
    factor = lax.rsqrt(jnp.sum(shaped * shaped, axis=-1, keepdims=True) + EPSILON)
    return ((shaped * factor).reshape(value.shape), factor)


def unit_back(upstream, normed, factor):
    upper_grad = upstream.reshape(normed.shape[0], -1, HEAD_DIM)
    normed_heads = normed.reshape(normed.shape[0], -1, HEAD_DIM)
    result = factor * (
        upper_grad - normed_heads * jnp.sum(upper_grad * normed_heads, axis=-1, keepdims=True)
    )
    return result.reshape(upstream.shape)


def block_span(total_rows, row_count):
    units = total_rows // row_count
    block_units = max(1, min(units, 512 // row_count))
    while units % block_units:
        block_units -= 1
    return row_count * block_units


def local(
    tokens,
    cotangent,
    bucket_start,
    w_qkv,
    w_out,
    s_qk,
    alpha_a,
    alpha_m,
    w_up,
    w_gate,
    w_down,
    s_u,
    s_v,
):
    row_count, model_width = tokens.shape
    head_count = model_width // HEAD_DIM
    score_scale = math.sqrt(HEAD_DIM)
    spread = lax.axis_size("tensor")
    group_rows = spread * row_count
    tensor_slot = lax.axis_index("tensor")
    qkv_full, out_full, gain_qk, mix_attn, mix_mlp = (
        lax.all_gather(w_qkv, ("dp", "tensor"), axis=0, tiled=True),
        lax.all_gather(w_out, ("dp", "tensor"), axis=0, tiled=True),
        lax.all_gather(s_qk, ("dp", "tensor"), axis=0, tiled=True),
        lax.all_gather(alpha_a, ("dp", "tensor"), axis=0, tiled=True),
        lax.all_gather(alpha_m, ("dp", "tensor"), axis=0, tiled=True),
    )
    up_full, gate_full, down_full = (
        lax.all_gather(w_up, "dp", axis=0, tiled=True),
        lax.all_gather(w_gate, "dp", axis=0, tiled=True),
        lax.all_gather(w_down, "dp", axis=0, tiled=True),
    )
    gain_qk = gain_qk.astype(jnp.float32)
    mix_attn = mix_attn.astype(jnp.float32)
    mix_mlp = mix_mlp.astype(jnp.float32)
    scale_up = s_u.astype(jnp.float32)
    scale_gate = s_v.astype(jnp.float32)
    starts = lax.dynamic_slice_in_dim(bucket_start, lax.axis_index("dp") * spread, spread)
    key_seq = jnp.repeat(starts, row_count)
    own_seq = starts[tensor_slot]
    query_pos = tensor_slot * row_count + jnp.arange(row_count, dtype=jnp.int32)

    def allowed(key_start, key_count):
        key_pos = key_start + jnp.arange(key_count, dtype=jnp.int32)
        seq_part = lax.dynamic_slice_in_dim(key_seq, key_start, key_count)
        return (key_pos[None, :] <= query_pos[:, None]) & (seq_part[None, :] == own_seq)

    inputs = tokens.astype(jnp.float32)
    qkv = jnp.dot(tokens, qkv_full, preferred_element_type=jnp.float32)
    q_unit, q_factor = unit_heads(qkv[:, :model_width])
    k_unit, k_factor = unit_heads(qkv[:, model_width : 2 * model_width])
    query_low = (q_unit * gain_qk).astype(jnp.bfloat16)
    keys_low = (k_unit * gain_qk).astype(jnp.bfloat16)
    values_low = qkv[:, 2 * model_width :].astype(jnp.bfloat16)
    query_heads = query_low.reshape(row_count, head_count, HEAD_DIM)
    key_all, value_all = (
        lax.all_gather(keys_low, "tensor", axis=0, tiled=True),
        lax.all_gather(values_low, "tensor", axis=0, tiled=True),
    )
    key_block = block_span(group_rows, row_count)
    blocks = group_rows // key_block

    def block_scores(key_source, key_start, key_count):
        key_part = lax.dynamic_slice_in_dim(key_source, key_start, key_count).reshape(
            key_count, head_count, HEAD_DIM
        )
        return (
            jnp.einsum("qhd,khd->hqk", query_heads, key_part, preferred_element_type=jnp.float32)
            * score_scale
        )

    def stat_step(state_pair, block_index):
        row_top, row_total = state_pair
        key_start = block_index * key_block
        allowed_keys = allowed(key_start, key_block)[None]
        masked = jnp.where(allowed_keys, block_scores(key_all, key_start, key_block), MASKED_SCORE)
        new_top = jnp.maximum(row_top, jnp.max(masked, axis=-1))
        fresh = jnp.where(allowed_keys, jnp.exp(masked - new_top[..., None]), 0.0)
        row_total = row_total * jnp.exp(row_top - new_top) + jnp.sum(fresh, axis=-1)
        return ((new_top, row_total), None)

    start_state = (
        jnp.full((head_count, row_count), MASKED_SCORE, jnp.float32),
        jnp.zeros((head_count, row_count), jnp.float32),
    )
    (row_top, row_total), _ = lax.scan(stat_step, start_state, jnp.arange(blocks))
    log_total = row_top + jnp.log(row_total)

    def probs_for(key_source, key_start, key_count):
        scores = block_scores(key_source, key_start, key_count)
        allowed_keys = allowed(key_start, key_count)[None]
        return jnp.where(allowed_keys, jnp.exp(scores - log_total[..., None]), 0.0)

    def value_part(value_source, key_start, key_count):
        return lax.dynamic_slice_in_dim(value_source, key_start, key_count).reshape(
            key_count, head_count, HEAD_DIM
        )

    def out_step(carry_sum, block_index):
        key_start = block_index * key_block
        attn_probs = probs_for(key_all, key_start, key_block).astype(jnp.bfloat16)
        term = jnp.einsum(
            "hqk,khd->qhd",
            attn_probs,
            value_part(value_all, key_start, key_block),
            preferred_element_type=jnp.float32,
        )
        return (carry_sum + term, None)

    attended, _ = lax.scan(
        out_step, jnp.zeros((row_count, head_count, HEAD_DIM), jnp.float32), jnp.arange(blocks)
    )
    attended_low = attended.reshape(row_count, model_width).astype(jnp.bfloat16)
    branch_a = jnp.dot(attended_low, out_full, preferred_element_type=jnp.float32)
    h_attn = rms_rows(branch_a)
    resid_one = inputs + mix_attn * (h_attn - inputs)
    hidden_one = rms_rows(resid_one)
    hidden_low = hidden_one.astype(jnp.bfloat16)
    rows_all = lax.all_gather(hidden_low, "tensor", axis=0, tiled=True)
    up_raw = jnp.dot(rows_all, up_full, preferred_element_type=jnp.float32)
    gate_raw = jnp.dot(rows_all, gate_full, preferred_element_type=jnp.float32)
    up_scaled = up_raw * scale_up
    gate_scaled = gate_raw * scale_gate
    gate_sigmoid = jax.nn.sigmoid(gate_scaled)
    silu_gate = gate_scaled * gate_sigmoid
    inner_low = (up_scaled * silu_gate).astype(jnp.bfloat16)
    branch_m = lax.psum_scatter(
        jnp.einsum("tf,df->td", inner_low, down_full, preferred_element_type=jnp.float32).astype(
            jnp.bfloat16
        ),
        "tensor",
        scatter_dimension=0,
        tiled=True,
    ).astype(jnp.float32)
    h_mlp = rms_rows(branch_m)
    resid_two = hidden_one + mix_mlp * (h_mlp - hidden_one)
    result = rms_rows(resid_two)
    partial_stats = jnp.stack(
        [jnp.sum(branch_a * branch_a), jnp.sum(branch_m * branch_m), jnp.sum(resid_two * resid_two)]
    )
    upstream = cotangent.astype(jnp.float32)
    d_resid_two = rms_back(upstream, result, resid_two)
    grad_mix_mlp = jnp.sum(d_resid_two * (h_mlp - hidden_one), axis=0)
    d_branch_m = rms_back(mix_mlp * d_resid_two, h_mlp, branch_m).astype(jnp.bfloat16)
    grads_all = lax.all_gather(d_branch_m, "tensor", axis=0, tiled=True)
    d_inner = jnp.dot(grads_all, down_full, preferred_element_type=jnp.float32)
    grad_up_scaled = d_inner * silu_gate
    grad_gate_scaled = (
        d_inner * up_scaled * gate_sigmoid * (1.0 + gate_scaled * (1.0 - gate_sigmoid))
    )
    grad_scale_up = jnp.sum(grad_up_scaled * up_raw, axis=0)
    grad_scale_gate = jnp.sum(grad_gate_scaled * gate_raw, axis=0)
    up_grad_low = (grad_up_scaled * scale_up).astype(jnp.bfloat16)
    gate_grad_low = (grad_gate_scaled * scale_gate).astype(jnp.bfloat16)
    grad_down = jnp.einsum("td,tf->df", grads_all, inner_low, preferred_element_type=jnp.float32)
    grad_up = jnp.einsum("td,tf->df", rows_all, up_grad_low, preferred_element_type=jnp.float32)
    grad_gate = jnp.einsum("td,tf->df", rows_all, gate_grad_low, preferred_element_type=jnp.float32)
    first = jnp.einsum("tf,df->td", up_grad_low, up_full, preferred_element_type=jnp.float32)
    d_hidden_one = (1.0 - mix_mlp) * d_resid_two + lax.psum_scatter(
        (
            first
            + jnp.einsum("tf,df->td", gate_grad_low, gate_full, preferred_element_type=jnp.float32)
        ).astype(jnp.bfloat16),
        "tensor",
        scatter_dimension=0,
        tiled=True,
    ).astype(jnp.float32)
    d_resid_one = rms_back(d_hidden_one, hidden_one, resid_one)
    grad_mix_attn = jnp.sum(d_resid_one * (h_attn - inputs), axis=0)
    d_branch_a = rms_back(mix_attn * d_resid_one, h_attn, branch_a).astype(jnp.bfloat16)
    grad_out = jnp.einsum("tc,td->cd", attended_low, d_branch_a, preferred_element_type=jnp.float32)
    d_attended = jnp.einsum(
        "td,cd->tc", d_branch_a, out_full, preferred_element_type=jnp.float32
    ).astype(jnp.bfloat16)
    d_heads = d_attended.reshape(row_count, head_count, HEAD_DIM)
    row_delta = jnp.sum(d_heads.astype(jnp.float32) * attended, axis=-1).T
    key_back, value_back = (
        lax.all_gather(keys_low, "tensor", axis=0, tiled=True),
        lax.all_gather(values_low, "tensor", axis=0, tiled=True),
    )

    def score_grads(key_start, key_count):
        attn_probs = probs_for(key_back, key_start, key_count)
        d_probs = jnp.einsum(
            "qhd,khd->hqk",
            d_heads,
            value_part(value_back, key_start, key_count),
            preferred_element_type=jnp.float32,
        )
        d_scores = (attn_probs * (d_probs - row_delta[..., None])).astype(jnp.bfloat16)
        return (attn_probs, d_scores)

    def query_step(carry_sum, block_index):
        key_start = block_index * key_block
        attn_probs, d_scores = score_grads(key_start, key_block)
        key_part = lax.dynamic_slice_in_dim(key_back, key_start, key_block).reshape(
            key_block, head_count, HEAD_DIM
        )
        return (
            carry_sum
            + jnp.einsum("hqk,khd->qhd", d_scores, key_part, preferred_element_type=jnp.float32),
            None,
        )

    d_query, _ = lax.scan(
        query_step, jnp.zeros((row_count, head_count, HEAD_DIM), jnp.float32), jnp.arange(blocks)
    )
    d_query = d_query.reshape(row_count, model_width) * score_scale
    part_rows = lax.axis_size("tensor") * row_count
    sub_block = block_span(part_rows, row_count)

    def one_block(block_index):
        begin = block_index * sub_block
        attn_probs, d_scores = score_grads(begin, sub_block)
        d_keys = (
            jnp.einsum("hqk,qhd->khd", d_scores, query_heads, preferred_element_type=jnp.float32)
            * score_scale
        )
        d_values = jnp.einsum(
            "hqk,qhd->khd",
            attn_probs.astype(jnp.bfloat16),
            d_heads,
            preferred_element_type=jnp.float32,
        )
        return jnp.concatenate(
            [d_keys.reshape(sub_block, model_width), d_values.reshape(sub_block, model_width)],
            axis=1,
        )

    block_terms = lax.map(one_block, jnp.arange(part_rows // sub_block))
    key_grads = lax.psum_scatter(
        block_terms.reshape(part_rows, 2 * model_width).astype(jnp.bfloat16),
        "tensor",
        scatter_dimension=0,
        tiled=True,
    ).astype(jnp.float32)
    d_keys_own = key_grads[:, :model_width]
    d_values_own = key_grads[:, model_width:]
    grad_gain = jnp.sum(d_query * q_unit + d_keys_own * k_unit, axis=0)
    d_qkv = jnp.concatenate(
        [
            unit_back(d_query * gain_qk, q_unit, q_factor),
            unit_back(d_keys_own * gain_qk, k_unit, k_factor),
            d_values_own,
        ],
        axis=1,
    ).astype(jnp.bfloat16)
    grad_qkv = jnp.einsum("tc,tf->cf", tokens, d_qkv, preferred_element_type=jnp.float32)
    d_tokens = (1.0 - mix_attn) * d_resid_one + jnp.einsum(
        "tf,cf->tc", d_qkv, qkv_full, preferred_element_type=jnp.float32
    )
    sum_qkv, sum_out, sum_gain, sum_mix_attn, sum_mix_mlp = (
        lax.psum_scatter(grad_qkv, ("dp", "tensor"), scatter_dimension=0, tiled=True),
        lax.psum_scatter(grad_out, ("dp", "tensor"), scatter_dimension=0, tiled=True),
        lax.psum_scatter(grad_gain, ("dp", "tensor"), scatter_dimension=0, tiled=True),
        lax.psum_scatter(grad_mix_attn, ("dp", "tensor"), scatter_dimension=0, tiled=True),
        lax.psum_scatter(grad_mix_mlp, ("dp", "tensor"), scatter_dimension=0, tiled=True),
    )
    sum_up, sum_gate, sum_down = (
        lax.psum_scatter(
            grad_up.astype(jnp.bfloat16), "dp", scatter_dimension=0, tiled=True
        ).astype(jnp.float32),
        lax.psum_scatter(
            grad_gate.astype(jnp.bfloat16), "dp", scatter_dimension=0, tiled=True
        ).astype(jnp.float32),
        lax.psum_scatter(
            grad_down.astype(jnp.bfloat16), "dp", scatter_dimension=0, tiled=True
        ).astype(jnp.float32),
    )
    sum_scale_up, sum_scale_gate = lax.psum((grad_scale_up, grad_scale_gate), "dp")
    stat_sums = lax.psum(partial_stats, ("dp", "tensor"))
    entry_count = row_count * model_width * lax.axis_size("dp") * spread
    stream_rms = jnp.sqrt(stat_sums / entry_count)
    return (
        result.astype(jnp.bfloat16),
        d_tokens.astype(jnp.bfloat16),
        sum_qkv,
        sum_out,
        sum_gain,
        sum_mix_attn,
        sum_mix_mlp,
        sum_up,
        sum_gate,
        sum_down,
        sum_scale_up,
        sum_scale_gate,
        stream_rms,
    )


MESH = pl.DeviceIdType.MESH
BF16 = jnp.bfloat16
F32 = jnp.float32
LOG2E = 1.4426950408889634
COPIES = 224
VMEM_BYTES = 63 * 2**20
CH = 32


def nn(left, right):
    return lax.dot_general(left, right, (((1,), (0,)), ((), ())), preferred_element_type=F32)


def nt(left, right):
    return lax.dot_general(left, right, (((1,), (1,)), ((), ())), preferred_element_type=F32)


def tn(left, right):
    return lax.dot_general(left, right, (((0,), (0,)), ((), ())), preferred_element_type=F32)


def flip(index, bits):
    bit = 1
    while bit <= bits:
        if bits & bit:
            index = index + bit - 2 * bit * lax.rem(lax.div(index, bit), 2)
        bit *= 2
    return index


def mean_rows(value):
    return jnp.mean(value, axis=-1, keepdims=True)


def rows(start, count=256):
    return pl.ds(pl.multiple_of(start * count, count), count)


def block(r):
    return pl.ds(r * 256, 256)


def fused_kernel(
    tokens, cotangent, bucket_start, w_qkv, w_out, s_qk, alpha_a, alpha_m, w_up, w_gate, w_down, scale_u,
    scale_v,
    layer_hbm, tokens_hbm, qkv_hbm, out_hbm, up_hbm, gate_hbm, down_hbm, stats_out,
    layer_out, grad_tokens, grad_qkv, grad_out, grad_up, grad_gate, grad_down,
    tok, cot, wq, wo, wu, wg, wd, small, small_t, small_d, gains,
    raw, qkv, linv, att, ato, branch, hid, h1, ur, gr, inn,
    part, from_core3, from_core1, from_y,
    dr2, dr1, d_inner_f32, db, dba, dat, dao, dqkv, delta,
    gd, x_down, x_down_x, x_up, x_gate, x_qkv, x_out, z_down, z_down_x, z_up, z_gate, z_qkv, z_out,
    o_core3, o_core1, o_y, osum, q_sum, q_low, q_piece, stats, s_tensor, s_x, s_z,
    send_sem, recv_sem, local_sem,
):
    d = lax.axis_index("dp")
    t = lax.axis_index("tensor")
    z = lax.div(d, 2)
    inner = lax.rem(lax.div(z + 1, 2), 2) == 1
    core, ynb, diag = (d, flip(t, 1)), (d, flip(t, 2)), (d, flip(t, 3))
    tensor_peer = {1: core, 2: ynb, 3: diag}
    xnb = (flip(d, 1), t)
    z_peer = {m: (flip(d, m), t) for m in (2, 4, 6)}

    barrier = pltpu.get_barrier_semaphore()
    peers = [core, ynb, diag, xnb] + [z_peer[m] for m in (2, 4, 6)]
    for peer in peers:
        pl.semaphore_signal(barrier, inc=1, device_id=peer, device_id_type=MESH)

    issued = []
    used = [0]

    def number():
        used[0] += 1
        return used[0] - 1

    def describe(src, dst, peer, at, to):
        return pltpu.make_async_remote_copy(
            src_ref=src,
            dst_ref=dst,
            send_sem=send_sem.at[at],
            recv_sem=recv_sem.at[to],
            device_id=peer,
            device_id_type=MESH,
        )

    def send(src, dst, peer):
        at = number()
        copy = describe(src, dst, peer, at, at)
        copy.start()
        issued.append(copy)
        return copy

    waited = set()

    def sent(copy):
        if id(copy) not in waited:
            waited.add(id(copy))
            copy.wait_send()

    locals_ = []

    def bring(src, dst):
        copy = pltpu.make_async_copy(src, dst, local_sem.at[len(locals_)])
        copy.start()
        locals_.append(copy)
        return copy

    outer = jnp.logical_not(inner)

    class Gather:
        def __init__(self, src, view):
            self.src, self.view = src, view
            self.at6, self.relay_at = number(), number()

        def start_x(self):
            self.x = [send(self.src, self.view(d), xnb)]

        def start_far(self):
            self.z = {4: send(self.src, self.view(d), z_peer[4])}
            self.start_straight()

        def start_straight(self):
            self.straight = describe(self.src, self.view(d), z_peer[6], self.at6, self.at6)
            pl.when(inner)(self.straight.start)

        def start_near(self):
            self.z[2] = send(self.src, self.view(d), z_peer[2])

        def start_z(self):
            self.start_far()
            self.start_near()

        def hop(self):
            self.z[4].wait_recv()
            self.hand_on()

        def hand_on(self):
            shard = self.view(flip(d, 4))
            self.relay = describe(shard, shard, z_peer[2], self.relay_at, self.at6)
            pl.when(inner)(self.relay.start)

        def forward_one(self, m):
            if m == 2:
                self.z[2].wait_recv()
            if m == 6:
                self.straight.wait_recv()
            shard = self.view(flip(d, m))
            self.x.append(send(shard, shard, xnb))

        def forward(self):
            self.forward_one(2)
            self.hop()
            self.forward_one(4)
            self.forward_one(6)

        def finish(self):
            for copy in self.x:
                copy.wait_recv()

        def release(self):
            for copy in [*self.z.values(), *self.x]:
                sent(copy)
            for copy in (self.straight, self.relay):
                pl.when(inner)(copy.wait_send)

    class GatherPairs(Gather):
        def __init__(self, src, shard, pair):
            super().__init__(src, pair)
            self.shard = shard

        def start_x(self):
            self.x = [send(self.src, self.shard(d), xnb)]

        def start_far(self):
            self.x[0].wait_recv()
            self.src = self.view(d)
            self.z = {4: send(self.src, self.view(d), z_peer[4])}

        def hop(self):
            self.z[4].wait_recv()
            self.start_straight()
            self.hand_on()

    def rows_of(ref, count=128):
        return lambda index: ref.at[rows(index, count)]

    def pair_of(ref):
        return lambda index: ref.at[rows(lax.div(index, 2))]

    take_qkv = Gather(wq.at[:, rows(d, 128), :], lambda index: wq.at[:, rows(index, 128), :])
    take_small = Gather(small_d.at[:, rows(d, 128)], lambda index: small_d.at[:, rows(index, 128)])
    take_out = Gather(w_out, lambda index: wo.at[index, t])
    take_up = Gather(w_up, rows_of(wu))
    take_gate = Gather(w_gate, rows_of(wg))
    take_down = GatherPairs(w_down, rows_of(wd), pair_of(wd))

    piece = s_qk.shape[0]
    own_qkv = pl.ds(pl.multiple_of(d * 128 + t * 32, 32), 32)

    def qkv_cols(slot, pair, j):
        return pl.ds(pl.multiple_of(j * 1024 + slot * 256 + pair * 128, 128), 128)

    def qkv_place(pair, j):
        return wq.at[pair, own_qkv, j * 128 : j * 128 + 128]

    parts_of_qkv = [(pair, j) for pair in range(2) for j in range(3)]
    local_qkv = [
        bring(w_qkv.at[:, qkv_cols(t, pair, j)], qkv_place(pair, j)) for pair, j in parts_of_qkv
    ]
    local_tok = bring(tokens, tok.at[block(0)])
    local_rest = [
        bring(w_out, wo.at[d, t]),
        bring(w_up, wu.at[rows(d, 128)]),
        bring(w_gate, wg.at[rows(d, 128)]),
        bring(w_down, wd.at[rows(d, 128)]),
        bring(cotangent, cot),
    ]
    place = jnp.where(
        lax.broadcasted_iota(jnp.int32, (piece, 128), 1)
        == lax.broadcasted_iota(jnp.int32, (piece, 128), 0) + t * piece,
        1.0,
        0.0,
    ).astype(BF16)
    small_row = lax.broadcasted_iota(jnp.int32, (16, 128), 0)
    placed = jnp.zeros((16, 128), F32)
    for index, vector in enumerate((s_qk, alpha_a, alpha_m)):
        placed = jnp.where(small_row == index, nn(vector[...].reshape(1, piece), place), placed)
    small[...] = placed.astype(BF16)
    stats[...] = jnp.zeros_like(stats)
    gain_u = scale_u[...].astype(F32).reshape(1, 1024)
    gain_v = scale_v[...].astype(F32).reshape(1, 1024)
    pl.semaphore_wait(barrier, len(peers))

    small_sends = [send(small, small_t.at[r - 1], tensor_peer[r]) for r in (2, 3, 1)]
    qkv_sends = [
        send(w_qkv.at[:, qkv_cols(flip(t, r), pair, j)], qkv_place(pair, j), tensor_peer[r])
        for r in (2, 3, 1)
        for pair, j in parts_of_qkv
    ]
    take_out.start_z()
    take_down.start_x()
    take_out.start_x()
    for copy in small_sends:
        copy.wait_recv()
    small_d[:, rows(d, 128)] = small[...] + small_t[0] + small_t[1] + small_t[2]
    take_small.start_z()
    take_small.start_x()
    for copy in local_qkv:
        copy.wait()
    for copy in qkv_sends:
        copy.wait_recv()
    take_qkv.start_z()
    take_qkv.start_x()
    tok_y = send(tokens, tok.at[block(2)], ynb)
    tok_core = send(tokens, tok.at[block(1)], core)
    take_up.start_far()

    take_out.hop()
    take_small.hop()
    take_small.forward_one(4)
    take_small.forward_one(2)
    take_qkv.hop()
    take_qkv.forward_one(4)
    take_up.start_near()
    take_qkv.forward_one(2)
    take_small.forward_one(6)
    take_qkv.forward_one(6)
    take_out.forward_one(4)
    take_out.forward_one(2)
    take_out.forward_one(6)
    take_up.start_x()
    take_gate.start_far()
    tok_y.wait_recv()
    tok_diag = send(tok.at[block(2)], tok.at[block(3)], core)
    take_small.finish()
    gains[...] = small_d[...].astype(F32)
    take_qkv.finish()
    local_tok.wait()
    tok_core.wait_recv()
    tok_diag.wait_recv()

    def gain_pair(pair):
        gain = gains[0:1, pl.ds(pl.multiple_of(t * 256 + pair * 128, 128), 128)]
        return jnp.concatenate([gain, gain], axis=1)

    first_head = lax.broadcasted_iota(jnp.int32, (256, 128), 1) < HEAD_DIM
    same_head = jnp.where(
        lax.div(lax.broadcasted_iota(jnp.int32, (256, 256), 0), HEAD_DIM)
        == lax.div(lax.broadcasted_iota(jnp.int32, (256, 256), 1), HEAD_DIM),
        1.0,
        0.0,
    ).astype(BF16)

    def head_sum(value):
        high = value.astype(BF16)
        low = (value - high.astype(F32)).astype(BF16)
        return nn(high, same_head) + nn(low, same_head)

    def qkv_step(r, carry):
        at = rows(r)
        x = tok[at, :]
        for pair in range(2):
            y = nn(x, wq[pair])
            qk = y[:, :256]
            raw[pair, at, :] = qk
            factor = lax.rsqrt(head_sum(qk * qk) + EPSILON)
            qkv[pair, at, :256] = (qk * factor * gain_pair(pair)).astype(BF16)
            qkv[pair, at, 256:] = y[:, 256:].astype(BF16)
        return carry

    lax.fori_loop(0, 4, qkv_step, 0)

    take_out.finish()
    local_rest[0].wait()
    wo_y = send(wo.at[:, t], wo.at[:, t], ynb)
    wo_core = send(wo.at[:, t], wo.at[:, t], core)

    def true_rows(i):
        return rows(flip(t, i))

    whole = jnp.where(bucket_start[d * 4] == bucket_start[d * 4 + 2], 1.0, 0.0)
    row_id = lax.broadcasted_iota(jnp.int32, (256, 256), 0)
    col_id = lax.broadcasted_iota(jnp.int32, (256, 256), 1)
    exp_scale = math.sqrt(HEAD_DIM) * LOG2E

    def two_heads(value):
        zero = jnp.zeros_like(value)
        return jnp.concatenate(
            [jnp.where(first_head, value, zero), jnp.where(first_head, zero, value)], axis=0
        )

    def one_of_two(value):
        return jnp.where(first_head, value[:256], value[256:])

    causal = jnp.concatenate([col_id <= row_id] * 2, axis=0)

    def attend(i):
        at = true_rows(i)

        def head_step(pair, carry):
            q = two_heads(qkv[pair, at, 0:128])
            acc = jnp.zeros((512, 128), F32)
            weight = jnp.zeros((512, 1), F32)
            for j in range(i + 1):
                key_at = true_rows(j)
                e = jnp.exp2(nt(q, qkv[pair, key_at, 128:256]) * exp_scale)
                if j == i:
                    e = jnp.where(causal, e, 0.0)
                elif j // 2 != i // 2:
                    e = e * whole
                weight = weight + jnp.sum(e, axis=1, keepdims=True)
                acc = acc + nn(e.astype(BF16), qkv[pair, key_at, 256:384])
            inverse = 1.0 / weight
            lanes = rows(pair, 128)
            linv[at, lanes] = one_of_two(jnp.broadcast_to(inverse, (512, 128)))
            att[at, lanes] = one_of_two(acc * inverse).astype(BF16)
            return carry

        lax.fori_loop(0, 2, head_step, 0)

    attend(0)
    attend(1)
    take_up.hop()
    take_up.forward_one(4)
    take_gate.start_near()
    take_gate.start_x()
    take_up.forward_one(2)
    for copy in local_rest[1:]:
        copy.wait()
    take_down.start_far()
    wo_y.wait_recv()
    wo_far = send(wo.at[:, flip(t, 2)], wo.at[:, flip(t, 2)], core)
    attend(2)
    attend(3)

    att_sends = [send(att.at[block(r)], ato.at[t], tensor_peer[r]) for r in (2, 3, 1)]
    ato[t] = att[block(0), :]
    take_up.forward_one(6)
    for copy in att_sends:
        copy.wait_recv()
    wo_core.wait_recv()
    wo_far.wait_recv()

    def out_rows(slot, columns):
        return wo[2 * slot : 2 * slot + 2, :, :, columns].reshape(256, 256)

    def out_step(n, carry):
        at = rows(n)
        acc = nn(ato[0], out_rows(0, at))
        for slot in range(1, 4):
            acc = acc + nn(ato[slot], out_rows(slot, at))
        branch[:, at] = acc
        return carry

    lax.fori_loop(0, 4, out_step, 0)

    mix_a = gains[1:2, :]
    mix_m = gains[2:3, :]

    def add_stat(row, value):
        stats[row : row + 1, :] = stats[row : row + 1, :] + jnp.sum(value, axis=0, keepdims=True)

    def first_norm(at):
        x = tok[at, :].astype(F32)
        ba = branch[at, :]
        fa = lax.rsqrt(mean_rows(ba * ba) + EPSILON)
        ha = ba * fa
        r1 = x + mix_a * (ha - x)
        f1 = lax.rsqrt(mean_rows(r1 * r1) + EPSILON)
        return x, ba, fa, ha, f1, r1 * f1

    def norm_step(c, carry):
        at = rows(c, CH)
        _, ba, _, _, _, hidden = first_norm(at)
        add_stat(3, ba * ba)
        hid[at, :] = hidden
        h1[at, :] = hidden.astype(BF16)
        return carry

    lax.fori_loop(0, 256 // CH, norm_step, 0)

    def spread(ref):
        return send(ref.at[block(0)], ref.at[block(2)], ynb), send(
            ref.at[block(0)], ref.at[block(1)], core
        )

    def relay(ref, from_ynb):
        from_ynb.wait_recv()
        return send(ref.at[block(2)], ref.at[block(3)], core)

    h1_y, h1_core = spread(h1)
    take_gate.hop()
    take_gate.forward_one(4)
    take_down.start_near()
    take_gate.forward_one(2)
    h1_far = relay(h1, h1_y)
    take_gate.forward_one(6)
    take_down.hop()
    take_up.finish()
    h1_core.wait_recv()
    h1_far.wait_recv()
    take_gate.finish()

    def up_step(r, carry):
        at = rows(r)
        hidden = h1[at, :]
        u_raw = nn(hidden, wu[...])
        g_raw = nn(hidden, wg[...])
        gate = g_raw * gain_v
        silu = gate / (1.0 + jnp.exp(-gate))
        ur[at, :] = u_raw.astype(BF16)
        gr[at, :] = g_raw.astype(BF16)
        inn[at, :] = (u_raw * gain_u * silu).astype(BF16)
        return carry

    lax.fori_loop(0, 4, up_step, 0)

    class Reduce:
        def __init__(self, which, before, make):
            self.which, self.before, self.make = which, before, make
            self.copies = {}

        def run(self, order):
            for r in order:
                self.step(r)

        def step(self, r):
            k = self.which
            if r in self.before.copies:
                before = self.before.copies[r]
                for copy in before if isinstance(before, list) else [before]:
                    sent(copy)
            self.make(r)
            if r == 3:
                self.copies[3] = send(part.at[block(3)], from_core3.at[k], core)
            elif r == 2:
                self.copies[3].wait_recv()
                part[block(2), :] = (
                    part[block(2), :].astype(F32) + from_core3[k].astype(F32)
                ).astype(BF16)
                self.copies[2] = send(part.at[block(2)], from_y.at[k], ynb)
            elif r == 1:
                self.copies[1] = send(part.at[block(1)], from_core1.at[k], core)

        def finish(self):
            self.copies[1].wait_recv()
            self.copies[2].wait_recv()

        def at(self, where):
            k = self.which
            return (
                part[where, :].astype(F32)
                + from_core1[k, where, :].astype(F32)
                + from_y[k, where, :].astype(F32)
            )

    class ReduceColumns:
        def __init__(self):
            self.copies = {r: [] for r in (1, 2, 3)}
            self.columns = []

        def step(self, k):
            cols = rows(lax.div(flip(d, 2 * k), 2))
            part[:, cols] = nt(inn[...], wd[cols, :]).astype(BF16)
            self.columns.append(cols)
            self.copies[3].append(send(part.at[block(3), cols], from_core3.at[0, :, cols], core))
            self.copies[1].append(send(part.at[block(1), cols], from_core1.at[0, :, cols], core))

        def pass_on(self):
            done = len(self.copies[2])
            cols = self.columns[done]
            self.copies[3][done].wait_recv()
            part[block(2), cols] = (
                part[block(2), cols].astype(F32) + from_core3[0, :, cols].astype(F32)
            ).astype(BF16)
            self.copies[2].append(send(part.at[block(2), cols], from_y.at[0, :, cols], ynb))

        def finish(self):
            for r in (1, 2):
                for copy in self.copies[r]:
                    copy.wait_recv()

        at = Reduce.at
        which = 0

    sum_m = ReduceColumns()
    sum_m.step(0)
    take_down.z[2].wait_recv()
    sum_m.step(1)
    sum_m.pass_on()
    sum_m.step(2)
    sum_m.pass_on()
    take_down.straight.wait_recv()
    sum_m.step(3)
    sum_m.pass_on()
    sum_m.pass_on()
    sum_m.finish()

    def loss_step(c, carry):
        at = rows(c, CH)
        bm = sum_m.at(at)
        hidden = hid[at, :]
        fm = lax.rsqrt(mean_rows(bm * bm) + EPSILON)
        hm = bm * fm
        r2 = hidden + mix_m * (hm - hidden)
        f2 = lax.rsqrt(mean_rows(r2 * r2) + EPSILON)
        result = r2 * f2
        layer_out[at, :] = result.astype(BF16)
        up = cot[at, :].astype(F32)
        grad = f2 * (up - result * mean_rows(up * result))
        dr2[at, :] = grad
        add_stat(1, grad * (hm - hidden))
        add_stat(4, bm * bm)
        add_stat(5, r2 * r2)
        c_m = mix_m * grad
        db[at, :] = (fm * (c_m - hm * mean_rows(c_m * hm))).astype(BF16)
        return carry

    class Spread:
        def __init__(self, ref):
            self.ref, self.y, self.core = ref, [], []

        def piece(self, r, c):
            return self.ref.at[pl.ds(r * 256 + c * 64, 64)]

        def start(self, c):
            self.y.append(send(self.piece(0, c), self.piece(2, c), ynb))
            self.core.append(send(self.piece(0, c), self.piece(1, c), core))

        def relay(self, c):
            self.y[c].wait_recv()
            self.core.append(send(self.piece(2, c), self.piece(3, c), core))

    db_rows = Spread(db)
    for c in range(4):
        lax.fori_loop(c * (64 // CH), (c + 1) * (64 // CH), loss_step, 0)
        db_rows.start(c)

    class AlongZ:
        def __init__(self, view, landing):
            self.view, self.landing = view, landing
            self.at6, self.relay_at = number(), number()
            self.z = {}

        def push(self, k):
            shard = self.view(flip(d, 2 * k))
            if k == 3:
                self.straight = describe(
                    shard, self.landing.at[2], z_peer[6], self.at6, self.at6
                )
                self.relay = describe(
                    shard, self.landing.at[3], z_peer[2], self.relay_at, self.relay_at
                )
                pl.when(inner)(self.straight.start)
                pl.when(outer)(self.relay.start)
            elif k == 2:

                @pl.when(inner)
                def _():
                    self.relay.wait_recv()
                    shard[...] = (shard[...].astype(F32) + self.landing[3].astype(F32)).astype(BF16)

                self.z[2] = send(shard, self.landing.at[1], z_peer[4])
            else:
                self.z[1] = send(shard, self.landing.at[0], z_peer[2])

        def total_into(self, out):
            self.z[1].wait_recv()
            self.z[2].wait_recv()
            out[...] = (
                self.view(d)[...].astype(F32)
                + self.landing[0].astype(F32)
                + self.landing[1].astype(F32)
            ).astype(out.dtype)

            @pl.when(inner)
            def _():
                self.straight.wait_recv()
                out[...] = (out[...].astype(F32) + self.landing[2].astype(F32)).astype(out.dtype)

        def settle(self):
            pl.when(inner)(self.straight.wait_send)
            pl.when(outer)(self.relay.wait_send)

    class Scatter(AlongZ):
        def __init__(self, view, from_x, landing):
            super().__init__(view, landing)
            self.from_x = from_x
            self.x = {}

        def ship(self, k):
            self.x[k] = send(self.view(flip(d, 2 * k + 1)), self.from_x.at[k], xnb)

        def fold(self, k):
            self.x[k].wait_recv()
            own = self.view(flip(d, 2 * k))
            own[...] = (own[...].astype(F32) + self.from_x[k].astype(F32)).astype(BF16)
            if k in (1, 3):
                self.push(k)

    def weight_grad(left, right, out, ship):
        for k in (3, 1, 2, 0):
            at = rows(lax.div(flip(d, 2 * k), 2))

            out[at, :] = tn(left[:, at], right[...]).astype(BF16)
            ship(k)

    def make_hidden(r):
        at = block(r)
        d_inner_f32[...] = nn(db[at, :], wd[...])

        def inner_step(c, carry):
            here = rows(c, CH)
            where = pl.ds(pl.multiple_of(r * 256 + c * CH, CH), CH)
            d_inner = d_inner_f32[here, :]
            u_raw = ur[where, :].astype(F32)
            g_raw = gr[where, :].astype(F32)
            gate = g_raw * gain_v
            sig = 1.0 / (1.0 + jnp.exp(-gate))
            up = u_raw * gain_u
            d_up = d_inner * (gate * sig)
            d_gate = d_inner * up * (sig * (1.0 + gate * (1.0 - sig)))
            add_stat(6, d_up * u_raw)
            add_stat(7, d_gate * g_raw)
            ur[where, :] = (d_up * gain_u).astype(BF16)
            gr[where, :] = (d_gate * gain_v).astype(BF16)
            return carry

        lax.fori_loop(0, 256 // CH, inner_step, 0)
        part[at, :] = (nt(ur[at, :], wu[...]) + nt(gr[at, :], wg[...])).astype(BF16)

    sum_h = Reduce(1, sum_m, make_hidden)
    for copy in db_rows.core[:4]:
        copy.wait_recv()
    sum_h.step(1)
    db_rows.relay(0)
    db_rows.relay(1)
    sum_h.step(0)
    db_rows.relay(2)
    db_rows.relay(3)
    for copy in db_rows.core[4:]:
        copy.wait_recv()
    half = slice(0, 512), slice(512, 1024)

    def down_pair(index):
        return gd.at[rows(lax.div(index, 2)), half[0]]

    def down_shard(index):
        return gd.at[rows(index, 128), half[1]]

    sum_down = AlongZ(down_pair, z_down)
    sum_down_x = Scatter(down_shard, x_down_x, z_down_x)

    def ship_down(k):
        if k == 3:
            sum_down.push(3)
        sum_down_x.ship(k)

    weight_grad(db, inn, gd, ship_down)
    sum_h.run((3, 2))

    gu, gg, go = wd, wu, wg
    for gather in (take_down, take_up, take_gate):
        gather.release()
    sum_up = Scatter(rows_of(gu), x_up, z_up)
    sum_gate = Scatter(rows_of(gg), x_gate, z_gate)
    weight_grad(h1, ur, gu, sum_up.ship)
    sum_down.push(2)
    sum_down.push(1)
    weight_grad(h1, gr, gg, sum_gate.ship)
    sum_down_x.fold(3)
    sum_down_x.fold(1)
    sum_h.finish()

    def mid_step(c, carry):
        at = rows(c, CH)
        x, _, fa, ha, f1, hidden = first_norm(at)
        d_hidden = (1.0 - mix_m) * dr2[at, :] + sum_h.at(at)
        grad = f1 * (d_hidden - hidden * mean_rows(d_hidden * hidden))
        dr1[at, :] = grad
        add_stat(0, grad * (ha - x))
        c_a = mix_a * grad
        dba[at, :] = (fa * (c_a - ha * mean_rows(c_a * ha))).astype(BF16)
        return carry

    lax.fori_loop(0, 256 // CH, mid_step, 0)

    dat_sends = []
    for r in (2, 3, 1, 0):
        slot = flip(t, r)
        weight = wo[pl.ds(2 * slot, 2)].reshape(256, 1024)
        value = nt(dba[...], weight).astype(BF16)
        if r:
            dat[r - 1] = value
            dat_sends.append(send(dat.at[r - 1], dao.at[block(r)], tensor_peer[r]))
        else:
            dao[block(0), :] = value
    for slot in range(4):
        g = tn(ato[slot], dba[...]).astype(BF16)
        for q in range(8):
            start = (q % 4) * 256 + (2 * slot + q // 4) * 32
            go[start : start + 32, :] = g[q * 32 : (q + 1) * 32, :]

    def go_rows(r):
        return rows(flip(t, r))

    go_core3 = send(go.at[go_rows(3)], o_core3, core)
    go_core1 = send(go.at[go_rows(1)], o_core1, core)
    sum_down_x.fold(2)
    sum_down_x.push(2)
    sum_down_x.fold(0)
    sum_up.fold(3)
    sum_up.fold(1)
    go_core3.wait_recv()
    go[go_rows(2), :] = (go[go_rows(2), :].astype(F32) + o_core3[...].astype(F32)).astype(BF16)
    go_y = send(go.at[go_rows(2)], o_y, ynb)

    head_rows = jnp.where(
        lax.broadcasted_iota(jnp.int32, (8, 256), 0)
        == lax.div(lax.broadcasted_iota(jnp.int32, (8, 256), 1), HEAD_DIM),
        1.0,
        0.0,
    ).astype(BF16)
    for copy in att_sends:
        sent(copy)

    def ready_step(r, carry):
        at = rows(r)
        scaled = (dao[at, :].astype(F32) * linv[at, :]).astype(BF16)
        dao[at, :] = scaled
        product = scaled.astype(F32) * att[at, :].astype(F32)
        high = product.astype(BF16)
        low = (product - high.astype(F32)).astype(BF16)
        delta[r] = nt(head_rows, high) + nt(head_rows, low)
        return carry

    key_grads, query_grads = branch, hid
    seen = jnp.concatenate([row_id <= col_id] * 2, axis=1)

    def lanes_of(r, half=0):
        return pl.ds(pl.multiple_of(r * 128 + half * 512, 128), 128)

    def attend_back(pair, query_r, key_r, visible):
        query_at, key_at = rows(query_r), rows(key_r)
        q = two_heads(qkv[pair, query_at, 0:128])
        do = two_heads(dao[query_at, pair * 128 : pair * 128 + 128])
        keys = qkv[pair, key_at, 128:256]
        e = visible(jnp.exp2(nt(keys, q) * exp_scale))
        d_prob = nt(qkv[pair, key_at, 256:384], do)
        shift = jnp.concatenate(
            [delta[query_r, 2 * pair + h : 2 * pair + h + 1, :] for h in range(2)], axis=1
        )
        d_score = (e * (d_prob - shift)).astype(BF16)
        key_grads[:, lanes_of(key_r)] += nn(d_score, q)
        key_grads[:, lanes_of(key_r, 1)] += nn(e.astype(BF16), do)
        query_grads[:, lanes_of(query_r)] += one_of_two(tn(d_score, keys))

    def diagonal(pair):
        def diagonal_step(r, carry):
            attend_back(pair, r, r, lambda e: jnp.where(seen, e, 0.0))
            return carry

        return diagonal_step

    def mixed(a, b):
        low = lax.rem(a, 2) + lax.rem(b, 2) - 2 * lax.rem(a, 2) * lax.rem(b, 2)
        high_a, high_b = lax.div(a, 2), lax.div(b, 2)
        return low + 2 * (high_a + high_b - 2 * high_a * high_b)

    def below(pair):
        def below_step(n, carry):
            i = 1 + lax.div(n, 3) + lax.div(n + 4, 5)
            j = n - lax.div(i * (i - 1), 2)
            apart = (lax.div(i, 2) - lax.div(j, 2)).astype(F32)
            factor = 1.0 - apart + apart * whole
            attend_back(pair, mixed(i, t), mixed(j, t), lambda e: e * factor)
            return carry

        return below_step

    def clear():
        key_grads[...] = jnp.zeros_like(key_grads)
        query_grads[...] = jnp.zeros_like(query_grads)

    def qkv_back(pair):
        scale = math.sqrt(HEAD_DIM)
        gain = gain_pair(pair)
        column = pl.ds(pl.multiple_of(t * 256 + pair * 128, 128), 128)

        def back_qkv_step(r, carry):
            at = rows(r)
            y = raw[pair, at, :]
            factor = lax.rsqrt(head_sum(y * y) + EPSILON)
            w = y * factor
            grad = (
                jnp.concatenate([query_grads[:, lanes_of(r)], key_grads[:, lanes_of(r)]], axis=1)
                * scale
            )
            both = jnp.sum(grad * w, axis=0, keepdims=True)
            stats[2:3, column] = stats[2:3, column] + both[:, :128] + both[:, 128:]
            c = grad * gain
            dqkv[pair, at, :256] = (factor * (c - w * head_sum(c * w))).astype(BF16)
            dqkv[pair, at, 256:] = key_grads[:, lanes_of(r, 1)].astype(BF16)
            return carry

        lax.fori_loop(0, 4, back_qkv_step, 0)

    gq = qkv

    def qkv_shard(pair):
        return lambda index: gq.at[pair, rows(index, 128), :]

    sum_qkv = [Scatter(qkv_shard(pair), x_qkv.at[pair], z_qkv.at[pair]) for pair in range(2)]

    def qkv_weight(pair):
        for k in (3, 1, 2, 0):
            at = rows(lax.div(flip(d, 2 * k), 2))
            gq[pair, at, :] = tn(tok[:, at], dqkv[pair]).astype(BF16)
            sum_qkv[pair].ship(k)

    clear()
    dat_sends[2].wait_recv()
    lax.fori_loop(0, 2, ready_step, 0)
    lax.fori_loop(0, 2, diagonal(0), 0)
    sum_up.fold(2)
    dat_sends[0].wait_recv()
    dat_sends[1].wait_recv()
    lax.fori_loop(2, 4, ready_step, 0)
    lax.fori_loop(2, 4, diagonal(0), 0)
    sum_up.push(2)
    sum_up.fold(0)
    lax.fori_loop(0, 6, below(0), 0)
    qkv_back(0)
    qkv_weight(0)
    clear()
    go_core1.wait_recv()
    go_y.wait_recv()
    osum[...] = (
        go[go_rows(0), :].astype(F32) + o_core1[...].astype(F32) + o_y[...].astype(F32)
    ).astype(BF16)
    sum_out = Scatter(rows_of(osum, 32), x_out, z_out)
    for k in (3, 1, 2, 0):
        sum_out.ship(k)
    sum_gate.fold(3)
    sum_gate.fold(1)
    lax.fori_loop(0, 4, diagonal(1), 0)
    sum_gate.fold(2)
    sum_gate.push(2)
    lax.fori_loop(0, 6, below(1), 0)
    qkv_back(1)
    qkv_weight(1)
    sum_gate.fold(0)
    sum_down.total_into(down_pair(d))
    down_x = send(gd.at[rows(flip(d, 1), 128), half[0]], x_down, xnb)

    small_back = [send(stats, s_tensor.at[r - 1], tensor_peer[r]) for r in (1, 2, 3)]

    def make_tokens(r):
        part[block(r), :] = (
            nt(dqkv[0, block(r), :], wq[0]) + nt(dqkv[1, block(r), :], wq[1])
        ).astype(BF16)

    sum_t = Reduce(2, sum_h, make_tokens)
    sum_t.run((3, 2))
    for k in (3, 1, 2, 0):
        sum_qkv[0].fold(k)
    sum_t.run((1, 0))
    sum_qkv[0].push(2)
    for k in (3, 1, 2, 0):
        sum_out.fold(k)
    sum_out.push(2)
    for copy in small_back:
        copy.wait_recv()
    over_tensor = s_tensor[0] + s_tensor[1] + s_tensor[2]
    shared = lax.broadcasted_iota(jnp.int32, (8, 1024), 0) < 6
    s_x[0] = stats[...] + jnp.where(shared, over_tensor, 0.0)
    stat_x = send(s_x.at[0], s_x.at[1], xnb)
    for k in (3, 1, 2, 0):
        sum_qkv[1].fold(k)
    sum_qkv[1].push(2)

    outgoing = []

    def put(src, dst):
        outgoing.append(bring(src, dst))

    put(layer_out, layer_hbm)
    down_x.wait_recv()
    grad_down[:, half[0]] = gd[rows(d, 128), half[0]].astype(F32) + x_down[...].astype(F32)
    sum_down_x.total_into(grad_down.at[:, half[1]])
    put(grad_down, down_hbm)
    sum_up.total_into(grad_up)
    put(grad_up, up_hbm)
    sum_gate.total_into(grad_gate)
    put(grad_gate, gate_hbm)
    sum_out.total_into(grad_out)
    put(grad_out, out_hbm)
    stat_x.wait_recv()
    s_z[0] = s_x[0] + s_x[1]
    stat_z = [send(s_z.at[0], s_z.at[k], z_peer[2 * k]) for k in (1, 2, 3)]
    for pair in range(2):
        sum_qkv[pair].total_into(q_sum.at[pair])
    q_low[...] = q_sum[...].astype(BF16)
    q_sends = [
        send(q_low.at[:, rows(flip(t, r), 32), :], q_piece.at[t], tensor_peer[r]) for r in (2, 3, 1)
    ]
    q_piece[t] = q_low[:, rows(t, 32), :]
    sum_t.finish()

    def last_step(c, carry):
        at = rows(c, CH)
        grad_tokens[at, :] = ((1.0 - mix_a) * dr1[at, :] + sum_t.at(at)).astype(BF16)
        return carry

    lax.fori_loop(0, 256 // CH, last_step, 0)
    put(grad_tokens, tokens_hbm)
    for copy in stat_z:
        copy.wait_recv()
    stats_out[...] = s_z[0] + s_z[1] + s_z[2] + s_z[3]
    for copy in q_sends:
        copy.wait_recv()
    for slot in range(4):
        for pair, j in parts_of_qkv:
            start = j * 1024 + slot * 256 + pair * 128
            grad_qkv[:, start : start + 128] = q_piece[
                slot, pair, :, j * 128 : j * 128 + 128
            ].astype(F32)
    put(grad_qkv, qkv_hbm)
    for gather in (take_qkv, take_small, take_out):
        gather.release()
    for scatter in (sum_down, sum_down_x, sum_up, sum_gate, sum_out, *sum_qkv):
        scatter.settle()
    for copy in issued:
        sent(copy)
    for copy in outgoing:
        copy.wait()


def finish_kernel(entries, *refs):
    large, stats, outs, held, sems = refs[:7], refs[7], refs[8:21], refs[21:28], refs[28]
    taken = [pltpu.make_async_copy(large[i], held[i], sems.at[0, i]) for i in range(7)]
    given = [pltpu.make_async_copy(held[i], outs[i], sems.at[1, i]) for i in range(7)]
    for copy in taken:
        copy.start()
    s_qk, alpha_a, alpha_m, s_u, s_v, stream = outs[7:]
    index = lax.axis_index("dp") * lax.axis_size("tensor") + lax.axis_index("tensor")
    piece = s_qk.shape[0]
    pick = lax.broadcasted_iota(jnp.int32, (1024, piece), 0) == (
        lax.broadcasted_iota(jnp.int32, (1024, piece), 1) + index * piece
    )
    own = lax.dot_general(
        stats[0:3, :],
        jnp.where(pick, 1.0, 0.0),
        (((1,), (0,)), ((), ())),
        precision=lax.Precision.HIGHEST,
        preferred_element_type=F32,
    )
    for ref, row in ((alpha_a, 0), (alpha_m, 1), (s_qk, 2)):
        ref[...] = own[row]
    s_u[...] = stats[6, :]
    s_v[...] = stats[7, :]
    stream[...] = jnp.sqrt(jnp.sum(stats[3:6, :], axis=1) / entries)
    for i in range(7):
        taken[i].wait()
        given[i].start()
    for copy in given:
        copy.wait()


def fits(mesh):
    return dict(mesh.shape) == {"dp": 8, "tensor": 4}


def fused(
    tokens, cotangent, bucket_start, w_qkv, w_out, s_qk, alpha_a, alpha_m, w_up, w_gate, w_down, s_u, s_v
):
    n_rows, width = tokens.shape
    piece = s_qk.shape[0]
    vmem = pl.BlockSpec(memory_space=pltpu.VMEM)
    smem = pl.BlockSpec(memory_space=pltpu.SMEM)
    hbm = pl.BlockSpec(memory_space=pl.ANY)
    bf = lambda *shape: pltpu.VMEM(shape, BF16)
    fl = lambda *shape: pltpu.VMEM(shape, F32)
    large = [
        jax.ShapeDtypeStruct(shape, kind)
        for shape, kind in (
            ((256, 1024), BF16), ((256, 1024), BF16), ((32, 3072), F32), ((32, 1024), F32),
            ((128, 1024), F32), ((128, 1024), F32), ((128, 1024), F32),
        )
    ]
    scratch = [
        *[pltpu.VMEM(leaf.shape, leaf.dtype) for leaf in large],
        bf(1024, 1024), bf(256, 1024), bf(2, 1024, 384), bf(8, 4, 32, 1024), bf(1024, 1024),
        bf(1024, 1024), bf(1024, 1024), bf(16, 128), bf(3, 16, 128), bf(16, 1024), fl(16, 1024),
        fl(2, 1024, 256), bf(2, 1024, 384), fl(1024, 256), bf(1024, 256), bf(4, 256, 256),
        fl(256, 1024), fl(256, 1024), bf(1024, 1024), bf(1024, 1024), bf(1024, 1024), bf(1024, 1024),
        bf(1024, 1024), bf(3, 256, 1024), bf(3, 256, 1024), bf(3, 256, 1024),
        fl(256, 1024), fl(256, 1024), fl(256, 1024), bf(1024, 1024), bf(256, 1024), bf(3, 256, 256),
        bf(1024, 256), bf(2, 1024, 384), fl(4, 8, 256),
        bf(1024, 1024), bf(128, 512), bf(4, 128, 512), bf(4, 128, 1024), bf(4, 128, 1024),
        bf(2, 4, 128, 384), bf(4, 32, 1024), bf(4, 256, 512), bf(4, 128, 512), bf(4, 128, 1024), bf(4, 128, 1024), bf(2, 4, 128, 384),
        bf(4, 32, 1024), bf(256, 1024), bf(256, 1024), bf(256, 1024), bf(256, 1024),
        fl(2, 128, 384), bf(2, 128, 384), bf(4, 2, 32, 384), fl(8, 1024), fl(3, 8, 1024), fl(2, 8, 1024), fl(4, 8, 1024),
        pltpu.SemaphoreType.DMA((COPIES,)), pltpu.SemaphoreType.DMA((COPIES,)),
        pltpu.SemaphoreType.DMA((32,)),
    ]
    *big, stats = pl.pallas_call(
        fused_kernel,
        out_shape=[*large, jax.ShapeDtypeStruct((8, 1024), F32)],
        in_specs=[hbm, hbm, smem, hbm, hbm, vmem, vmem, vmem, hbm, hbm, hbm, vmem, vmem],
        out_specs=[*[hbm] * 7, vmem],
        scratch_shapes=scratch,
        compiler_params=pltpu.CompilerParams(
            collective_id=0, has_side_effects=True, vmem_limit_bytes=VMEM_BYTES
        ),
        cost_estimate=pl.CostEstimate(
            flops=27_000_000_000, bytes_accessed=8_000_000, transcendentals=10_000_000
        ),
    )(
        tokens, cotangent, bucket_start, w_qkv, w_out, s_qk, alpha_a, alpha_m,
        w_up, w_gate, w_down, s_u, s_v,
    )
    entries = n_rows * width * lax.axis_size("dp") * lax.axis_size("tensor")
    flat = [(piece,), (piece,), (piece,), (1024,), (1024,), (3,)]
    *big, g_qk, g_a, g_m, g_u, g_v, stream = pl.pallas_call(
        functools.partial(finish_kernel, float(entries)),
        out_shape=[*large, *[jax.ShapeDtypeStruct(shape, F32) for shape in flat]],
        in_specs=[hbm] * 7 + [vmem],
        out_specs=[hbm] * 7 + [vmem] * 6,
        scratch_shapes=[
            *[pltpu.VMEM(leaf.shape, leaf.dtype) for leaf in large],
            pltpu.SemaphoreType.DMA((2, 7)),
        ],
    )(*big, stats)
    return (*big[:4], g_qk, g_a, g_m, *big[4:], g_u, g_v, stream)


def solution(mesh):
    body = fused if fits(mesh) else local
    return jax.shard_map(
        body,
        mesh=mesh,
        in_specs=(
            P(("dp", "tensor"), None),
            P(("dp", "tensor"), None),
            P(),
            P(("dp", "tensor"), None),
            P(("dp", "tensor"), None),
            P(("dp", "tensor")),
            P(("dp", "tensor")),
            P(("dp", "tensor")),
            P("dp", "tensor"),
            P("dp", "tensor"),
            P("dp", "tensor"),
            P("tensor"),
            P("tensor"),
        ),
        out_specs=(
            P(("dp", "tensor"), None),
            P(("dp", "tensor"), None),
            P(("dp", "tensor"), None),
            P(("dp", "tensor"), None),
            P(("dp", "tensor")),
            P(("dp", "tensor")),
            P(("dp", "tensor")),
            P("dp", "tensor"),
            P("dp", "tensor"),
            P("dp", "tensor"),
            P("tensor"),
            P("tensor"),
            P(),
        ),
        check_vma=False,
    )
```

```python
import functools
import math

import jax
import jax.numpy as jnp
from jax import lax
from jax.experimental import pallas as pl
from jax.experimental.pallas import tpu as pltpu
from jax.sharding import PartitionSpec as P

HEAD_DIM = 64


EPSILON = 1e-06
MASKED_SCORE = -1e30


def rms_rows(value):
    return value * lax.rsqrt(jnp.mean(value * value, axis=-1, keepdims=True) + EPSILON)


def rms_back(upstream, normed, source):
    factor = lax.rsqrt(jnp.mean(source * source, axis=-1, keepdims=True) + EPSILON)
    return factor * (upstream - normed * jnp.mean(upstream * normed, axis=-1, keepdims=True))


def unit_heads(value):
    shaped = value.reshape(value.shape[0], -1, HEAD_DIM)
    factor = lax.rsqrt(jnp.sum(shaped * shaped, axis=-1, keepdims=True) + EPSILON)
    return ((shaped * factor).reshape(value.shape), factor)


def unit_back(upstream, normed, factor):
    upper_grad = upstream.reshape(normed.shape[0], -1, HEAD_DIM)
    normed_heads = normed.reshape(normed.shape[0], -1, HEAD_DIM)
    result = factor * (
        upper_grad - normed_heads * jnp.sum(upper_grad * normed_heads, axis=-1, keepdims=True)
    )
    return result.reshape(upstream.shape)


def block_span(total_rows, row_count):
    units = total_rows // row_count
    block_units = max(1, min(units, 512 // row_count))
    while units % block_units:
        block_units -= 1
    return row_count * block_units


def local(
    tokens,
    cotangent,
    bucket_start,
    w_qkv,
    w_out,
    s_qk,
    alpha_a,
    alpha_m,
    w_up,
    w_gate,
    w_down,
    s_u,
    s_v,
):
    row_count, model_width = tokens.shape
    head_count = model_width // HEAD_DIM
    score_scale = math.sqrt(HEAD_DIM)
    spread = lax.axis_size("tensor")
    group_rows = spread * row_count
    tensor_slot = lax.axis_index("tensor")
    qkv_full, out_full, gain_qk, mix_attn, mix_mlp = (
        lax.all_gather(w_qkv, ("dp", "tensor"), axis=0, tiled=True),
        lax.all_gather(w_out, ("dp", "tensor"), axis=0, tiled=True),
        lax.all_gather(s_qk, ("dp", "tensor"), axis=0, tiled=True),
        lax.all_gather(alpha_a, ("dp", "tensor"), axis=0, tiled=True),
        lax.all_gather(alpha_m, ("dp", "tensor"), axis=0, tiled=True),
    )
    up_full, gate_full, down_full = (
        lax.all_gather(w_up, "dp", axis=0, tiled=True),
        lax.all_gather(w_gate, "dp", axis=0, tiled=True),
        lax.all_gather(w_down, "dp", axis=0, tiled=True),
    )
    gain_qk = gain_qk.astype(jnp.float32)
    mix_attn = mix_attn.astype(jnp.float32)
    mix_mlp = mix_mlp.astype(jnp.float32)
    scale_up = s_u.astype(jnp.float32)
    scale_gate = s_v.astype(jnp.float32)
    starts = lax.dynamic_slice_in_dim(bucket_start, lax.axis_index("dp") * spread, spread)
    key_seq = jnp.repeat(starts, row_count)
    own_seq = starts[tensor_slot]
    query_pos = tensor_slot * row_count + jnp.arange(row_count, dtype=jnp.int32)

    def allowed(key_start, key_count):
        key_pos = key_start + jnp.arange(key_count, dtype=jnp.int32)
        seq_part = lax.dynamic_slice_in_dim(key_seq, key_start, key_count)
        return (key_pos[None, :] <= query_pos[:, None]) & (seq_part[None, :] == own_seq)

    inputs = tokens.astype(jnp.float32)
    qkv = jnp.dot(tokens, qkv_full, preferred_element_type=jnp.float32)
    q_unit, q_factor = unit_heads(qkv[:, :model_width])
    k_unit, k_factor = unit_heads(qkv[:, model_width : 2 * model_width])
    query_low = (q_unit * gain_qk).astype(jnp.bfloat16)
    keys_low = (k_unit * gain_qk).astype(jnp.bfloat16)
    values_low = qkv[:, 2 * model_width :].astype(jnp.bfloat16)
    query_heads = query_low.reshape(row_count, head_count, HEAD_DIM)
    key_all, value_all = (
        lax.all_gather(keys_low, "tensor", axis=0, tiled=True),
        lax.all_gather(values_low, "tensor", axis=0, tiled=True),
    )
    key_block = block_span(group_rows, row_count)
    blocks = group_rows // key_block

    def block_scores(key_source, key_start, key_count):
        key_part = lax.dynamic_slice_in_dim(key_source, key_start, key_count).reshape(
            key_count, head_count, HEAD_DIM
        )
        return (
            jnp.einsum("qhd,khd->hqk", query_heads, key_part, preferred_element_type=jnp.float32)
            * score_scale
        )

    def stat_step(state_pair, block_index):
        row_top, row_total = state_pair
        key_start = block_index * key_block
        allowed_keys = allowed(key_start, key_block)[None]
        masked = jnp.where(allowed_keys, block_scores(key_all, key_start, key_block), MASKED_SCORE)
        new_top = jnp.maximum(row_top, jnp.max(masked, axis=-1))
        fresh = jnp.where(allowed_keys, jnp.exp(masked - new_top[..., None]), 0.0)
        row_total = row_total * jnp.exp(row_top - new_top) + jnp.sum(fresh, axis=-1)
        return ((new_top, row_total), None)

    start_state = (
        jnp.full((head_count, row_count), MASKED_SCORE, jnp.float32),
        jnp.zeros((head_count, row_count), jnp.float32),
    )
    (row_top, row_total), _ = lax.scan(stat_step, start_state, jnp.arange(blocks))
    log_total = row_top + jnp.log(row_total)

    def probs_for(key_source, key_start, key_count):
        scores = block_scores(key_source, key_start, key_count)
        allowed_keys = allowed(key_start, key_count)[None]
        return jnp.where(allowed_keys, jnp.exp(scores - log_total[..., None]), 0.0)

    def value_part(value_source, key_start, key_count):
        return lax.dynamic_slice_in_dim(value_source, key_start, key_count).reshape(
            key_count, head_count, HEAD_DIM
        )

    def out_step(carry_sum, block_index):
        key_start = block_index * key_block
        attn_probs = probs_for(key_all, key_start, key_block).astype(jnp.bfloat16)
        term = jnp.einsum(
            "hqk,khd->qhd",
            attn_probs,
            value_part(value_all, key_start, key_block),
            preferred_element_type=jnp.float32,
        )
        return (carry_sum + term, None)

    attended, _ = lax.scan(
        out_step, jnp.zeros((row_count, head_count, HEAD_DIM), jnp.float32), jnp.arange(blocks)
    )
    attended_low = attended.reshape(row_count, model_width).astype(jnp.bfloat16)
    branch_a = jnp.dot(attended_low, out_full, preferred_element_type=jnp.float32)
    h_attn = rms_rows(branch_a)
    resid_one = inputs + mix_attn * (h_attn - inputs)
    hidden_one = rms_rows(resid_one)
    hidden_low = hidden_one.astype(jnp.bfloat16)
    rows_all = lax.all_gather(hidden_low, "tensor", axis=0, tiled=True)
    up_raw = jnp.dot(rows_all, up_full, preferred_element_type=jnp.float32)
    gate_raw = jnp.dot(rows_all, gate_full, preferred_element_type=jnp.float32)
    up_scaled = up_raw * scale_up
    gate_scaled = gate_raw * scale_gate
    gate_sigmoid = jax.nn.sigmoid(gate_scaled)
    silu_gate = gate_scaled * gate_sigmoid
    inner_low = (up_scaled * silu_gate).astype(jnp.bfloat16)
    branch_m = lax.psum_scatter(
        jnp.einsum("tf,df->td", inner_low, down_full, preferred_element_type=jnp.float32).astype(
            jnp.bfloat16
        ),
        "tensor",
        scatter_dimension=0,
        tiled=True,
    ).astype(jnp.float32)
    h_mlp = rms_rows(branch_m)
    resid_two = hidden_one + mix_mlp * (h_mlp - hidden_one)
    result = rms_rows(resid_two)
    partial_stats = jnp.stack(
        [jnp.sum(branch_a * branch_a), jnp.sum(branch_m * branch_m), jnp.sum(resid_two * resid_two)]
    )
    upstream = cotangent.astype(jnp.float32)
    d_resid_two = rms_back(upstream, result, resid_two)
    grad_mix_mlp = jnp.sum(d_resid_two * (h_mlp - hidden_one), axis=0)
    d_branch_m = rms_back(mix_mlp * d_resid_two, h_mlp, branch_m).astype(jnp.bfloat16)
    grads_all = lax.all_gather(d_branch_m, "tensor", axis=0, tiled=True)
    d_inner = jnp.dot(grads_all, down_full, preferred_element_type=jnp.float32)
    grad_up_scaled = d_inner * silu_gate
    grad_gate_scaled = (
        d_inner * up_scaled * gate_sigmoid * (1.0 + gate_scaled * (1.0 - gate_sigmoid))
    )
    grad_scale_up = jnp.sum(grad_up_scaled * up_raw, axis=0)
    grad_scale_gate = jnp.sum(grad_gate_scaled * gate_raw, axis=0)
    up_grad_low = (grad_up_scaled * scale_up).astype(jnp.bfloat16)
    gate_grad_low = (grad_gate_scaled * scale_gate).astype(jnp.bfloat16)
    grad_down = jnp.einsum("td,tf->df", grads_all, inner_low, preferred_element_type=jnp.float32)
    grad_up = jnp.einsum("td,tf->df", rows_all, up_grad_low, preferred_element_type=jnp.float32)
    grad_gate = jnp.einsum("td,tf->df", rows_all, gate_grad_low, preferred_element_type=jnp.float32)
    first = jnp.einsum("tf,df->td", up_grad_low, up_full, preferred_element_type=jnp.float32)
    d_hidden_one = (1.0 - mix_mlp) * d_resid_two + lax.psum_scatter(
        (
            first
            + jnp.einsum("tf,df->td", gate_grad_low, gate_full, preferred_element_type=jnp.float32)
        ).astype(jnp.bfloat16),
        "tensor",
        scatter_dimension=0,
        tiled=True,
    ).astype(jnp.float32)
    d_resid_one = rms_back(d_hidden_one, hidden_one, resid_one)
    grad_mix_attn = jnp.sum(d_resid_one * (h_attn - inputs), axis=0)
    d_branch_a = rms_back(mix_attn * d_resid_one, h_attn, branch_a).astype(jnp.bfloat16)
    grad_out = jnp.einsum("tc,td->cd", attended_low, d_branch_a, preferred_element_type=jnp.float32)
    d_attended = jnp.einsum(
        "td,cd->tc", d_branch_a, out_full, preferred_element_type=jnp.float32
    ).astype(jnp.bfloat16)
    d_heads = d_attended.reshape(row_count, head_count, HEAD_DIM)
    row_delta = jnp.sum(d_heads.astype(jnp.float32) * attended, axis=-1).T
    key_back, value_back = (
        lax.all_gather(keys_low, "tensor", axis=0, tiled=True),
        lax.all_gather(values_low, "tensor", axis=0, tiled=True),
    )

    def score_grads(key_start, key_count):
        attn_probs = probs_for(key_back, key_start, key_count)
        d_probs = jnp.einsum(
            "qhd,khd->hqk",
            d_heads,
            value_part(value_back, key_start, key_count),
            preferred_element_type=jnp.float32,
        )
        d_scores = (attn_probs * (d_probs - row_delta[..., None])).astype(jnp.bfloat16)
        return (attn_probs, d_scores)

    def query_step(carry_sum, block_index):
        key_start = block_index * key_block
        attn_probs, d_scores = score_grads(key_start, key_block)
        key_part = lax.dynamic_slice_in_dim(key_back, key_start, key_block).reshape(
            key_block, head_count, HEAD_DIM
        )
        return (
            carry_sum
            + jnp.einsum("hqk,khd->qhd", d_scores, key_part, preferred_element_type=jnp.float32),
            None,
        )

    d_query, _ = lax.scan(
        query_step, jnp.zeros((row_count, head_count, HEAD_DIM), jnp.float32), jnp.arange(blocks)
    )
    d_query = d_query.reshape(row_count, model_width) * score_scale
    part_rows = lax.axis_size("tensor") * row_count
    sub_block = block_span(part_rows, row_count)

    def one_block(block_index):
        begin = block_index * sub_block
        attn_probs, d_scores = score_grads(begin, sub_block)
        d_keys = (
            jnp.einsum("hqk,qhd->khd", d_scores, query_heads, preferred_element_type=jnp.float32)
            * score_scale
        )
        d_values = jnp.einsum(
            "hqk,qhd->khd",
            attn_probs.astype(jnp.bfloat16),
            d_heads,
            preferred_element_type=jnp.float32,
        )
        return jnp.concatenate(
            [d_keys.reshape(sub_block, model_width), d_values.reshape(sub_block, model_width)],
            axis=1,
        )

    block_terms = lax.map(one_block, jnp.arange(part_rows // sub_block))
    key_grads = lax.psum_scatter(
        block_terms.reshape(part_rows, 2 * model_width).astype(jnp.bfloat16),
        "tensor",
        scatter_dimension=0,
        tiled=True,
    ).astype(jnp.float32)
    d_keys_own = key_grads[:, :model_width]
    d_values_own = key_grads[:, model_width:]
    grad_gain = jnp.sum(d_query * q_unit + d_keys_own * k_unit, axis=0)
    d_qkv = jnp.concatenate(
        [
            unit_back(d_query * gain_qk, q_unit, q_factor),
            unit_back(d_keys_own * gain_qk, k_unit, k_factor),
            d_values_own,
        ],
        axis=1,
    ).astype(jnp.bfloat16)
    grad_qkv = jnp.einsum("tc,tf->cf", tokens, d_qkv, preferred_element_type=jnp.float32)
    d_tokens = (1.0 - mix_attn) * d_resid_one + jnp.einsum(
        "tf,cf->tc", d_qkv, qkv_full, preferred_element_type=jnp.float32
    )
    sum_qkv, sum_out, sum_gain, sum_mix_attn, sum_mix_mlp = (
        lax.psum_scatter(grad_qkv, ("dp", "tensor"), scatter_dimension=0, tiled=True),
        lax.psum_scatter(grad_out, ("dp", "tensor"), scatter_dimension=0, tiled=True),
        lax.psum_scatter(grad_gain, ("dp", "tensor"), scatter_dimension=0, tiled=True),
        lax.psum_scatter(grad_mix_attn, ("dp", "tensor"), scatter_dimension=0, tiled=True),
        lax.psum_scatter(grad_mix_mlp, ("dp", "tensor"), scatter_dimension=0, tiled=True),
    )
    sum_up, sum_gate, sum_down = (
        lax.psum_scatter(
            grad_up.astype(jnp.bfloat16), "dp", scatter_dimension=0, tiled=True
        ).astype(jnp.float32),
        lax.psum_scatter(
            grad_gate.astype(jnp.bfloat16), "dp", scatter_dimension=0, tiled=True
        ).astype(jnp.float32),
        lax.psum_scatter(
            grad_down.astype(jnp.bfloat16), "dp", scatter_dimension=0, tiled=True
        ).astype(jnp.float32),
    )
    sum_scale_up, sum_scale_gate = lax.psum((grad_scale_up, grad_scale_gate), "dp")
    stat_sums = lax.psum(partial_stats, ("dp", "tensor"))
    entry_count = row_count * model_width * lax.axis_size("dp") * spread
    stream_rms = jnp.sqrt(stat_sums / entry_count)
    return (
        result.astype(jnp.bfloat16),
        d_tokens.astype(jnp.bfloat16),
        sum_qkv,
        sum_out,
        sum_gain,
        sum_mix_attn,
        sum_mix_mlp,
        sum_up,
        sum_gate,
        sum_down,
        sum_scale_up,
        sum_scale_gate,
        stream_rms,
    )


MESH = pl.DeviceIdType.MESH
BF16 = jnp.bfloat16
F32 = jnp.float32
LOG2E = 1.4426950408889634
COPIES = 224
VMEM_BYTES = 63 * 2**20
CH = 32


def nn(left, right):
    return lax.dot_general(left, right, (((1,), (0,)), ((), ())), preferred_element_type=F32)


def nt(left, right):
    return lax.dot_general(left, right, (((1,), (1,)), ((), ())), preferred_element_type=F32)


def tn(left, right):
    return lax.dot_general(left, right, (((0,), (0,)), ((), ())), preferred_element_type=F32)


def flip(index, bits):
    bit = 1
    while bit <= bits:
        if bits & bit:
            index = index + bit - 2 * bit * lax.rem(lax.div(index, bit), 2)
        bit *= 2
    return index


def mixed(a, b):
    low = lax.rem(a, 2) + lax.rem(b, 2) - 2 * lax.rem(a, 2) * lax.rem(b, 2)
    high_a, high_b = lax.div(a, 2), lax.div(b, 2)
    return low + 2 * (high_a + high_b - 2 * high_a * high_b)


def mean_rows(value):
    return jnp.mean(value, axis=-1, keepdims=True)


def rows(start, count=256):
    return pl.ds(pl.multiple_of(start * count, count), count)


def block(r):
    return pl.ds(r * 256, 256)


def fused_kernel(
    tokens, cotangent, bucket_start, w_qkv, w_out, s_qk, alpha_a, alpha_m, w_up, w_gate, w_down, scale_u,
    scale_v,
    layer_hbm, tokens_hbm, qkv_hbm, out_hbm, up_hbm, gate_hbm, down_hbm, stats_out,
    layer_out, grad_tokens, grad_qkv, grad_out, grad_up, grad_gate, grad_down,
    tok, cot, wq, wo, wu, wg, wd, small, small_t, small_d, gains,
    raw, qkv, linv, att, ato, branch, hid, h1, ur, gr, inn,
    part, from_core3, from_core1, from_y,
    dr2, dr1, d_inner_f32, db, dba, dat, dao, dqkv, delta,
    gd, x_down, x_down_x, x_up, x_gate, x_qkv, x_out, z_down, z_down_x, z_up, z_gate, z_qkv, z_out,
    o_core3, o_core1, o_y, osum, q_sum, q_low, q_piece, stats, s_tensor, s_x, s_z,
    send_sem, recv_sem, local_sem,
):
    d = lax.axis_index("dp")
    t = lax.axis_index("tensor")
    z = lax.div(d, 2)
    inner = lax.rem(lax.div(z + 1, 2), 2) == 1
    core, ynb, diag = (d, flip(t, 1)), (d, flip(t, 2)), (d, flip(t, 3))
    tensor_peer = {1: core, 2: ynb, 3: diag}
    xnb = (flip(d, 1), t)
    z_peer = {m: (flip(d, m), t) for m in (2, 4, 6)}

    barrier = pltpu.get_barrier_semaphore()
    peers = [core, ynb, diag, xnb] + [z_peer[m] for m in (2, 4, 6)]
    for peer in peers:
        pl.semaphore_signal(barrier, inc=1, device_id=peer, device_id_type=MESH)

    issued = []
    used = [0]

    def number():
        used[0] += 1
        return used[0] - 1

    def describe(src, dst, peer, at, to):
        return pltpu.make_async_remote_copy(
            src_ref=src,
            dst_ref=dst,
            send_sem=send_sem.at[at],
            recv_sem=recv_sem.at[to],
            device_id=peer,
            device_id_type=MESH,
        )

    def send(src, dst, peer):
        at = number()
        copy = describe(src, dst, peer, at, at)
        copy.start()
        issued.append(copy)
        return copy

    waited = set()

    def sent(copy):
        if id(copy) not in waited:
            waited.add(id(copy))
            copy.wait_send()

    locals_ = []

    def bring(src, dst):
        copy = pltpu.make_async_copy(src, dst, local_sem.at[len(locals_)])
        copy.start()
        locals_.append(copy)
        return copy

    outer = jnp.logical_not(inner)

    class Gather:
        def __init__(self, src, view):
            self.src, self.view = src, view
            self.at6, self.relay_at = number(), number()

        def start_x(self):
            self.x = [send(self.src, self.view(d), xnb)]

        def start_far(self):
            self.z = {4: send(self.src, self.view(d), z_peer[4])}
            self.start_straight()

        def start_straight(self):
            self.straight = describe(self.src, self.view(d), z_peer[6], self.at6, self.at6)
            pl.when(inner)(self.straight.start)

        def start_near(self):
            self.z[2] = send(self.src, self.view(d), z_peer[2])

        def start_z(self):
            self.start_far()
            self.start_near()

        def hop(self):
            self.z[4].wait_recv()
            self.hand_on()

        def hand_on(self):
            shard = self.view(flip(d, 4))
            self.relay = describe(shard, shard, z_peer[2], self.relay_at, self.at6)
            pl.when(inner)(self.relay.start)

        def forward_one(self, m):
            if m == 2:
                self.z[2].wait_recv()
            if m == 6:
                self.straight.wait_recv()
            shard = self.view(flip(d, m))
            self.x.append(send(shard, shard, xnb))

        def forward(self):
            self.forward_one(2)
            self.hop()
            self.forward_one(4)
            self.forward_one(6)

        def finish(self):
            for copy in self.x:
                copy.wait_recv()

        def release(self):
            for copy in [*self.z.values(), *self.x]:
                sent(copy)
            for copy in (self.straight, self.relay):
                pl.when(inner)(copy.wait_send)

    class GatherPairs(Gather):
        def __init__(self, src, shard, pair):
            super().__init__(src, pair)
            self.shard = shard

        def start_x(self):
            self.x = [send(self.src, self.shard(d), xnb)]

        def start_far(self):
            self.x[0].wait_recv()
            self.src = self.view(d)
            self.z = {4: send(self.src, self.view(d), z_peer[4])}

        def hop(self):
            self.z[4].wait_recv()
            self.start_straight()
            self.hand_on()

    def rows_of(ref, count=128):
        return lambda index: ref.at[rows(index, count)]

    def pair_of(ref):
        return lambda index: ref.at[rows(lax.div(index, 2))]

    take_qkv = Gather(wq.at[:, rows(d, 128), :], lambda index: wq.at[:, rows(index, 128), :])
    take_small = Gather(small_d.at[:, rows(d, 128)], lambda index: small_d.at[:, rows(index, 128)])
    take_out = Gather(w_out, lambda index: wo.at[index, t])
    take_up = Gather(w_up, rows_of(wu))
    take_gate = Gather(w_gate, rows_of(wg))
    take_down = GatherPairs(w_down, rows_of(wd), pair_of(wd))

    piece = s_qk.shape[0]
    own_qkv = pl.ds(pl.multiple_of(d * 128 + t * 32, 32), 32)

    def qkv_cols(slot, pair, j):
        return pl.ds(pl.multiple_of(j * 1024 + slot * 256 + pair * 128, 128), 128)

    def qkv_place(pair, j):
        return wq.at[pair, own_qkv, j * 128 : j * 128 + 128]

    parts_of_qkv = [(pair, j) for pair in range(2) for j in range(3)]
    local_qkv = [
        bring(w_qkv.at[:, qkv_cols(t, pair, j)], qkv_place(pair, j)) for pair, j in parts_of_qkv
    ]
    local_tok = bring(tokens, tok.at[block(0)])
    local_rest = [
        bring(w_out, wo.at[d, t]),
        bring(w_up, wu.at[rows(d, 128)]),
        bring(w_gate, wg.at[rows(d, 128)]),
        bring(w_down, wd.at[rows(d, 128)]),
        bring(cotangent, cot),
    ]
    place = jnp.where(
        lax.broadcasted_iota(jnp.int32, (piece, 128), 1)
        == lax.broadcasted_iota(jnp.int32, (piece, 128), 0) + t * piece,
        1.0,
        0.0,
    ).astype(BF16)
    small_row = lax.broadcasted_iota(jnp.int32, (16, 128), 0)
    placed = jnp.zeros((16, 128), F32)
    for index, vector in enumerate((s_qk, alpha_a, alpha_m)):
        placed = jnp.where(small_row == index, nn(vector[...].reshape(1, piece), place), placed)
    small[...] = placed.astype(BF16)
    stats[...] = jnp.zeros_like(stats)
    gain_u = scale_u[...].astype(F32).reshape(1, 1024)
    gain_v = scale_v[...].astype(F32).reshape(1, 1024)
    pl.semaphore_wait(barrier, len(peers))

    small_sends = [send(small, small_t.at[r - 1], tensor_peer[r]) for r in (2, 3, 1)]
    qkv_sends = [
        send(w_qkv.at[:, qkv_cols(flip(t, r), pair, j)], qkv_place(pair, j), tensor_peer[r])
        for r in (2, 3, 1)
        for pair, j in parts_of_qkv
    ]
    take_out.start_z()
    take_down.start_x()
    take_out.start_x()
    take_up.start_x()
    for copy in small_sends:
        copy.wait_recv()
    small_d[:, rows(d, 128)] = small[...] + small_t[0] + small_t[1] + small_t[2]
    take_small.start_z()
    take_small.start_x()
    for copy in local_qkv:
        copy.wait()
    for copy in qkv_sends:
        copy.wait_recv()
    take_qkv.start_z()
    take_qkv.start_x()
    tok_y = send(tokens, tok.at[block(2)], ynb)
    tok_core = send(tokens, tok.at[block(1)], core)
    take_up.start_far()

    take_out.hop()
    take_small.hop()
    take_small.forward_one(4)
    take_small.forward_one(2)
    take_qkv.hop()
    take_qkv.forward_one(4)
    take_up.start_near()
    take_qkv.forward_one(2)
    take_small.forward_one(6)
    take_qkv.forward_one(6)
    take_out.forward_one(4)
    take_out.forward_one(2)
    take_out.forward_one(6)
    take_gate.start_far()
    tok_y.wait_recv()
    tok_diag = send(tok.at[block(2)], tok.at[block(3)], core)
    take_small.finish()
    gains[...] = small_d[...].astype(F32)
    take_qkv.finish()
    local_tok.wait()
    tok_core.wait_recv()
    tok_diag.wait_recv()

    def gain_pair(pair):
        gain = gains[0:1, pl.ds(pl.multiple_of(t * 256 + pair * 128, 128), 128)]
        return jnp.concatenate([gain, gain], axis=1)

    first_head = lax.broadcasted_iota(jnp.int32, (256, 128), 1) < HEAD_DIM
    same_head = jnp.where(
        lax.div(lax.broadcasted_iota(jnp.int32, (256, 256), 0), HEAD_DIM)
        == lax.div(lax.broadcasted_iota(jnp.int32, (256, 256), 1), HEAD_DIM),
        1.0,
        0.0,
    ).astype(BF16)

    def head_sum(value):
        high = value.astype(BF16)
        low = (value - high.astype(F32)).astype(BF16)
        return nn(high, same_head) + nn(low, same_head)

    def qkv_step(r, carry):
        at = rows(r)
        x = tok[at, :]
        for pair in range(2):
            y = nn(x, wq[pair])
            qk = y[:, :256]
            raw[pair, at, :] = qk
            factor = lax.rsqrt(head_sum(qk * qk) + EPSILON)
            qkv[pair, at, :256] = (qk * factor * gain_pair(pair)).astype(BF16)
            qkv[pair, at, 256:] = y[:, 256:].astype(BF16)
        return carry

    lax.fori_loop(0, 4, qkv_step, 0)

    take_out.finish()
    local_rest[0].wait()
    wo_y = send(wo.at[:, t], wo.at[:, t], ynb)
    wo_core = send(wo.at[:, t], wo.at[:, t], core)

    def true_rows(i):
        return rows(flip(t, i))

    whole = jnp.where(bucket_start[d * 4] == bucket_start[d * 4 + 2], 1.0, 0.0)
    row_id = lax.broadcasted_iota(jnp.int32, (256, 256), 0)
    col_id = lax.broadcasted_iota(jnp.int32, (256, 256), 1)
    exp_scale = math.sqrt(HEAD_DIM) * LOG2E

    def two_heads(value):
        zero = jnp.zeros_like(value)
        return jnp.concatenate(
            [jnp.where(first_head, value, zero), jnp.where(first_head, zero, value)], axis=0
        )

    def one_of_two(value):
        return jnp.where(first_head, value[:256], value[256:])

    causal = jnp.concatenate([col_id <= row_id] * 2, axis=0)

    def attend(i):
        at = true_rows(i)

        def head_step(pair, carry):
            q = two_heads(qkv[pair, at, 0:128])
            acc = jnp.zeros((512, 128), F32)
            weight = jnp.zeros((512, 1), F32)
            for j in range(i + 1):
                key_at = true_rows(j)
                e = jnp.exp2(nt(q, qkv[pair, key_at, 128:256]) * exp_scale)
                if j == i:
                    e = jnp.where(causal, e, 0.0)
                elif j // 2 != i // 2:
                    e = e * whole
                weight = weight + jnp.sum(e, axis=1, keepdims=True)
                acc = acc + nn(e.astype(BF16), qkv[pair, key_at, 256:384])
            inverse = 1.0 / weight
            lanes = rows(pair, 128)
            linv[at, lanes] = one_of_two(jnp.broadcast_to(inverse, (512, 128)))
            att[at, lanes] = one_of_two(acc * inverse).astype(BF16)
            return carry

        lax.fori_loop(0, 2, head_step, 0)

    attend(0)
    attend(1)
    take_up.hop()
    take_up.forward_one(4)
    take_gate.start_near()
    take_gate.start_x()
    take_up.forward_one(2)
    for copy in local_rest[1:]:
        copy.wait()
    take_down.start_far()
    attend(2)
    attend(3)

    att_sends = [send(att.at[block(r)], ato.at[t], tensor_peer[r]) for r in (2, 3, 1)]
    ato[t] = att[block(0), :]
    wo_y.wait_recv()
    wo_far = send(wo.at[:, flip(t, 2)], wo.at[:, flip(t, 2)], core)
    take_up.forward_one(6)
    for copy in att_sends:
        copy.wait_recv()
    wo_core.wait_recv()
    wo_far.wait_recv()

    def out_rows(slot, columns):
        return wo[2 * slot : 2 * slot + 2, :, :, columns].reshape(256, 256)

    def out_step(n, carry):
        at = rows(n)
        acc = nn(ato[0], out_rows(0, at))
        for slot in range(1, 4):
            acc = acc + nn(ato[slot], out_rows(slot, at))
        branch[:, at] = acc
        return carry

    lax.fori_loop(0, 4, out_step, 0)

    mix_a = gains[1:2, :]
    mix_m = gains[2:3, :]

    def add_stat(row, value):
        stats[row : row + 1, :] = stats[row : row + 1, :] + jnp.sum(value, axis=0, keepdims=True)

    def first_norm(at):
        x = tok[at, :].astype(F32)
        ba = branch[at, :]
        fa = lax.rsqrt(mean_rows(ba * ba) + EPSILON)
        ha = ba * fa
        r1 = x + mix_a * (ha - x)
        f1 = lax.rsqrt(mean_rows(r1 * r1) + EPSILON)
        return x, ba, fa, ha, f1, r1 * f1

    def norm_step(c, carry):
        at = rows(c, CH)
        _, ba, _, _, _, hidden = first_norm(at)
        add_stat(3, ba * ba)
        hid[at, :] = hidden
        h1[at, :] = hidden.astype(BF16)
        return carry

    lax.fori_loop(0, 256 // CH, norm_step, 0)

    def spread(ref):
        return send(ref.at[block(0)], ref.at[block(2)], ynb), send(
            ref.at[block(0)], ref.at[block(1)], core
        )

    def relay(ref, from_ynb):
        from_ynb.wait_recv()
        return send(ref.at[block(2)], ref.at[block(3)], core)

    h1_y, h1_core = spread(h1)
    take_gate.hop()
    take_gate.forward_one(4)
    take_down.start_near()
    take_gate.forward_one(2)
    h1_far = relay(h1, h1_y)
    take_gate.forward_one(6)
    take_down.hop()
    take_up.finish()
    h1_core.wait_recv()
    h1_far.wait_recv()
    take_gate.finish()

    def up_step(r, carry):
        at = rows(r)
        hidden = h1[at, :]
        u_raw = nn(hidden, wu[...])
        g_raw = nn(hidden, wg[...])
        gate = g_raw * gain_v
        silu = gate / (1.0 + jnp.exp(-gate))
        ur[at, :] = u_raw.astype(BF16)
        gr[at, :] = g_raw.astype(BF16)
        inn[at, :] = (u_raw * gain_u * silu).astype(BF16)
        return carry

    lax.fori_loop(0, 4, up_step, 0)

    class Reduce:
        def __init__(self, which, before, make):
            self.which, self.before, self.make = which, before, make
            self.copies = {}

        def run(self, order):
            for r in order:
                self.step(r)

        def step(self, r):
            k = self.which
            if r in self.before.copies:
                before = self.before.copies[r]
                for copy in before if isinstance(before, list) else [before]:
                    sent(copy)
            self.make(r)
            if r == 3:
                self.copies[3] = send(part.at[block(3)], from_core3.at[k], core)
            elif r == 2:
                self.copies[3].wait_recv()
                part[block(2), :] = (
                    part[block(2), :].astype(F32) + from_core3[k].astype(F32)
                ).astype(BF16)
                self.copies[2] = send(part.at[block(2)], from_y.at[k], ynb)
            elif r == 1:
                self.copies[1] = send(part.at[block(1)], from_core1.at[k], core)

        def finish(self):
            self.copies[1].wait_recv()
            self.copies[2].wait_recv()

        def at(self, where):
            k = self.which
            return (
                part[where, :].astype(F32)
                + from_core1[k, where, :].astype(F32)
                + from_y[k, where, :].astype(F32)
            )

    class ReduceColumns:
        def __init__(self):
            self.copies = {r: [] for r in (1, 2, 3)}
            self.columns = []

        def step(self, k):
            cols = rows(lax.div(flip(d, 2 * k), 2))
            part[:, cols] = nt(inn[...], wd[cols, :]).astype(BF16)
            self.columns.append(cols)
            self.copies[3].append(send(part.at[block(3), cols], from_core3.at[0, :, cols], core))
            self.copies[1].append(send(part.at[block(1), cols], from_core1.at[0, :, cols], core))

        def pass_on(self):
            done = len(self.copies[2])
            cols = self.columns[done]
            self.copies[3][done].wait_recv()
            part[block(2), cols] = (
                part[block(2), cols].astype(F32) + from_core3[0, :, cols].astype(F32)
            ).astype(BF16)
            self.copies[2].append(send(part.at[block(2), cols], from_y.at[0, :, cols], ynb))

        def finish(self):
            for r in (1, 2):
                for copy in self.copies[r]:
                    copy.wait_recv()

        at = Reduce.at
        which = 0

    sum_m = ReduceColumns()
    sum_m.step(0)
    take_down.z[2].wait_recv()
    sum_m.step(1)
    sum_m.pass_on()
    sum_m.step(2)
    sum_m.pass_on()
    take_down.straight.wait_recv()
    sum_m.step(3)
    sum_m.pass_on()
    sum_m.pass_on()
    sum_m.finish()

    def loss_step(c, carry):
        at = rows(c, CH)
        bm = sum_m.at(at)
        hidden = hid[at, :]
        fm = lax.rsqrt(mean_rows(bm * bm) + EPSILON)
        hm = bm * fm
        r2 = hidden + mix_m * (hm - hidden)
        f2 = lax.rsqrt(mean_rows(r2 * r2) + EPSILON)
        result = r2 * f2
        layer_out[at, :] = result.astype(BF16)
        up = cot[at, :].astype(F32)
        grad = f2 * (up - result * mean_rows(up * result))
        dr2[at, :] = grad
        add_stat(1, grad * (hm - hidden))
        add_stat(4, bm * bm)
        add_stat(5, r2 * r2)
        c_m = mix_m * grad
        db[at, :] = (fm * (c_m - hm * mean_rows(c_m * hm))).astype(BF16)
        return carry

    class Spread:
        def __init__(self, ref):
            self.ref, self.y, self.core = ref, [], []

        def piece(self, r, c):
            return self.ref.at[pl.ds(r * 256 + c * 64, 64)]

        def start(self, c):
            self.y.append(send(self.piece(0, c), self.piece(2, c), ynb))
            self.core.append(send(self.piece(0, c), self.piece(1, c), core))

        def relay(self, c):
            self.y[c].wait_recv()
            self.core.append(send(self.piece(2, c), self.piece(3, c), core))

    db_rows = Spread(db)
    for c in range(4):
        lax.fori_loop(c * (64 // CH), (c + 1) * (64 // CH), loss_step, 0)
        db_rows.start(c)

    class AlongZ:
        def __init__(self, view, landing):
            self.view, self.landing = view, landing
            self.at6, self.relay_at = number(), number()
            self.z = {}

        def far_copies(self):
            shard = self.view(flip(d, 6))
            return (
                describe(shard, self.landing.at[2], z_peer[6], self.at6, self.at6),
                describe(shard, self.landing.at[3], z_peer[2], self.relay_at, self.relay_at),
            )

        def start_far(self):
            straight, over = self.far_copies()
            pl.when(inner)(straight.start)
            pl.when(outer)(over.start)

        def push(self, k):
            shard = self.view(flip(d, 2 * k))
            if k == 3:
                self.start_far()
                self.straight, self.relay = self.far_copies()
            elif k == 2:

                @pl.when(inner)
                def _():
                    self.relay.wait_recv()
                    shard[...] = (shard[...].astype(F32) + self.landing[3].astype(F32)).astype(BF16)

                self.z[2] = send(shard, self.landing.at[1], z_peer[4])
            else:
                self.z[1] = send(shard, self.landing.at[0], z_peer[2])

        def total_into(self, out):
            self.z[1].wait_recv()
            self.z[2].wait_recv()
            out[...] = (
                self.view(d)[...].astype(F32)
                + self.landing[0].astype(F32)
                + self.landing[1].astype(F32)
            ).astype(out.dtype)

            @pl.when(inner)
            def _():
                self.straight.wait_recv()
                out[...] = (out[...].astype(F32) + self.landing[2].astype(F32)).astype(out.dtype)

        def settle(self):
            pl.when(inner)(self.straight.wait_send)
            pl.when(outer)(self.relay.wait_send)

    class Scatter(AlongZ):
        def __init__(self, view, from_x, landing):
            super().__init__(view, landing)
            self.from_x = from_x
            self.x = {}

        def ship(self, k):
            self.x[k] = send(self.view(flip(d, 2 * k + 1)), self.from_x.at[k], xnb)

        def ship_as_made(self, make, also=None):
            numbers = [number() for _ in range(4)]

            def copy_of(k, shard):
                at = numbers[0] + k
                return describe(self.view(shard), self.from_x.at[k], xnb, at, at)

            def step(n, carry):
                k = (7 - 2 * n + n // 2) % 4
                pair = mixed(z, k)
                make(rows(pair))
                copy_of(k, 2 * pair + 1 - lax.rem(d, 2)).start()
                if also is not None:
                    pl.when(n == 0)(also)
                return carry

            lax.fori_loop(0, 4, step, 0)
            for k in range(4):
                self.x[k] = copy_of(k, flip(d, 2 * k + 1))
                issued.append(self.x[k])

        def fold(self, k):
            self.x[k].wait_recv()
            own = self.view(flip(d, 2 * k))
            own[...] = (own[...].astype(F32) + self.from_x[k].astype(F32)).astype(BF16)
            if k in (1, 3):
                self.push(k)

    def weight_grad(left, right, out, scatter, also=None):
        def make(at):
            out[at, :] = tn(left[:, at], right[...]).astype(BF16)

        scatter.ship_as_made(make, also)

    def make_hidden(r):
        at = block(r)
        d_inner_f32[...] = nn(db[at, :], wd[...])

        def inner_step(c, carry):
            here = rows(c, CH)
            where = pl.ds(pl.multiple_of(r * 256 + c * CH, CH), CH)
            d_inner = d_inner_f32[here, :]
            u_raw = ur[where, :].astype(F32)
            g_raw = gr[where, :].astype(F32)
            gate = g_raw * gain_v
            sig = 1.0 / (1.0 + jnp.exp(-gate))
            up = u_raw * gain_u
            d_up = d_inner * (gate * sig)
            d_gate = d_inner * up * (sig * (1.0 + gate * (1.0 - sig)))
            add_stat(6, d_up * u_raw)
            add_stat(7, d_gate * g_raw)
            ur[where, :] = (d_up * gain_u).astype(BF16)
            gr[where, :] = (d_gate * gain_v).astype(BF16)
            return carry

        lax.fori_loop(0, 256 // CH, inner_step, 0)
        part[at, :] = (nt(ur[at, :], wu[...]) + nt(gr[at, :], wg[...])).astype(BF16)

    sum_h = Reduce(1, sum_m, make_hidden)
    for copy in db_rows.core[:4]:
        copy.wait_recv()
    sum_h.step(1)
    db_rows.relay(0)
    db_rows.relay(1)
    sum_h.step(0)
    db_rows.relay(2)
    db_rows.relay(3)
    for copy in db_rows.core[4:]:
        copy.wait_recv()
    half = slice(0, 512), slice(512, 1024)

    def down_pair(index):
        return gd.at[rows(lax.div(index, 2)), half[0]]

    def down_shard(index):
        return gd.at[rows(index, 128), half[1]]

    sum_down = AlongZ(down_pair, z_down)
    sum_down_x = Scatter(down_shard, x_down_x, z_down_x)

    weight_grad(db, inn, gd, sum_down_x, sum_down.start_far)
    sum_down.straight, sum_down.relay = sum_down.far_copies()
    sum_h.run((3, 2))

    gu, gg, go = wd, wu, wg
    for gather in (take_down, take_up, take_gate):
        gather.release()
    sum_up = Scatter(rows_of(gu), x_up, z_up)
    sum_gate = Scatter(rows_of(gg), x_gate, z_gate)
    weight_grad(h1, ur, gu, sum_up)
    sum_down.push(2)
    sum_down.push(1)
    weight_grad(h1, gr, gg, sum_gate)
    sum_down_x.fold(3)
    sum_down_x.fold(1)
    sum_h.finish()

    def mid_step(c, carry):
        at = rows(c, CH)
        x, _, fa, ha, f1, hidden = first_norm(at)
        d_hidden = (1.0 - mix_m) * dr2[at, :] + sum_h.at(at)
        grad = f1 * (d_hidden - hidden * mean_rows(d_hidden * hidden))
        dr1[at, :] = grad
        add_stat(0, grad * (ha - x))
        c_a = mix_a * grad
        dba[at, :] = (fa * (c_a - ha * mean_rows(c_a * ha))).astype(BF16)
        return carry

    lax.fori_loop(0, 256 // CH, mid_step, 0)

    dat_sends = []
    for r in (2, 3, 1, 0):
        slot = flip(t, r)
        weight = wo[pl.ds(2 * slot, 2)].reshape(256, 1024)
        value = nt(dba[...], weight).astype(BF16)
        if r:
            dat[r - 1] = value
            dat_sends.append(send(dat.at[r - 1], dao.at[block(r)], tensor_peer[r]))
        else:
            dao[block(0), :] = value
    for slot in range(4):
        g = tn(ato[slot], dba[...]).astype(BF16)
        for q in range(8):
            start = (q % 4) * 256 + (2 * slot + q // 4) * 32
            go[start : start + 32, :] = g[q * 32 : (q + 1) * 32, :]

    def go_rows(r):
        return rows(flip(t, r))

    go_core3 = send(go.at[go_rows(3)], o_core3, core)
    go_core1 = send(go.at[go_rows(1)], o_core1, core)
    sum_down_x.fold(2)
    sum_down_x.push(2)
    sum_down_x.fold(0)
    sum_up.fold(3)
    sum_up.fold(1)
    go_core3.wait_recv()
    go[go_rows(2), :] = (go[go_rows(2), :].astype(F32) + o_core3[...].astype(F32)).astype(BF16)
    go_y = send(go.at[go_rows(2)], o_y, ynb)

    head_rows = jnp.where(
        lax.broadcasted_iota(jnp.int32, (8, 256), 0)
        == lax.div(lax.broadcasted_iota(jnp.int32, (8, 256), 1), HEAD_DIM),
        1.0,
        0.0,
    ).astype(BF16)
    for copy in att_sends:
        sent(copy)

    def ready_step(r, carry):
        at = rows(r)
        scaled = (dao[at, :].astype(F32) * linv[at, :]).astype(BF16)
        dao[at, :] = scaled
        product = scaled.astype(F32) * att[at, :].astype(F32)
        high = product.astype(BF16)
        low = (product - high.astype(F32)).astype(BF16)
        delta[r] = nt(head_rows, high) + nt(head_rows, low)
        return carry

    key_grads, query_grads = branch, hid
    seen = jnp.concatenate([row_id <= col_id] * 2, axis=1)

    def lanes_of(r, half=0):
        return pl.ds(pl.multiple_of(r * 128 + half * 512, 128), 128)

    def attend_back(pair, query_r, key_r, visible):
        query_at, key_at = rows(query_r), rows(key_r)
        q = two_heads(qkv[pair, query_at, 0:128])
        do = two_heads(dao[query_at, pair * 128 : pair * 128 + 128])
        keys = qkv[pair, key_at, 128:256]
        e = visible(jnp.exp2(nt(keys, q) * exp_scale))
        d_prob = nt(qkv[pair, key_at, 256:384], do)
        shift = jnp.concatenate(
            [delta[query_r, 2 * pair + h : 2 * pair + h + 1, :] for h in range(2)], axis=1
        )
        d_score = (e * (d_prob - shift)).astype(BF16)
        key_grads[:, lanes_of(key_r)] += nn(d_score, q)
        key_grads[:, lanes_of(key_r, 1)] += nn(e.astype(BF16), do)
        query_grads[:, lanes_of(query_r)] += one_of_two(tn(d_score, keys))

    def diagonal(pair):
        def diagonal_step(r, carry):
            attend_back(pair, r, r, lambda e: jnp.where(seen, e, 0.0))
            return carry

        return diagonal_step

    def below(pair):
        def below_step(n, carry):
            i = 1 + lax.div(n, 3) + lax.div(n + 4, 5)
            j = n - lax.div(i * (i - 1), 2)
            apart = (lax.div(i, 2) - lax.div(j, 2)).astype(F32)
            factor = 1.0 - apart + apart * whole
            attend_back(pair, mixed(i, t), mixed(j, t), lambda e: e * factor)
            return carry

        return below_step

    def clear():
        key_grads[...] = jnp.zeros_like(key_grads)
        query_grads[...] = jnp.zeros_like(query_grads)

    def qkv_back(pair):
        scale = math.sqrt(HEAD_DIM)
        gain = gain_pair(pair)
        column = pl.ds(pl.multiple_of(t * 256 + pair * 128, 128), 128)

        def back_qkv_step(r, carry):
            at = rows(r)
            y = raw[pair, at, :]
            factor = lax.rsqrt(head_sum(y * y) + EPSILON)
            w = y * factor
            grad = (
                jnp.concatenate([query_grads[:, lanes_of(r)], key_grads[:, lanes_of(r)]], axis=1)
                * scale
            )
            both = jnp.sum(grad * w, axis=0, keepdims=True)
            stats[2:3, column] = stats[2:3, column] + both[:, :128] + both[:, 128:]
            c = grad * gain
            dqkv[pair, at, :256] = (factor * (c - w * head_sum(c * w))).astype(BF16)
            dqkv[pair, at, 256:] = key_grads[:, lanes_of(r, 1)].astype(BF16)
            return carry

        lax.fori_loop(0, 4, back_qkv_step, 0)

    gq = qkv

    def qkv_shard(pair):
        return lambda index: gq.at[pair, rows(index, 128), :]

    sum_qkv = [Scatter(qkv_shard(pair), x_qkv.at[pair], z_qkv.at[pair]) for pair in range(2)]

    def qkv_weight(pair):
        def make(at):
            gq[pair, at, :] = tn(tok[:, at], dqkv[pair]).astype(BF16)

        sum_qkv[pair].ship_as_made(make)

    clear()
    dat_sends[2].wait_recv()
    lax.fori_loop(0, 2, ready_step, 0)
    lax.fori_loop(0, 2, diagonal(0), 0)
    sum_up.fold(2)
    dat_sends[0].wait_recv()
    dat_sends[1].wait_recv()
    lax.fori_loop(2, 4, ready_step, 0)
    lax.fori_loop(2, 4, diagonal(0), 0)
    sum_up.push(2)
    sum_up.fold(0)
    lax.fori_loop(0, 6, below(0), 0)
    qkv_back(0)
    qkv_weight(0)
    clear()
    go_core1.wait_recv()
    go_y.wait_recv()
    osum[...] = (
        go[go_rows(0), :].astype(F32) + o_core1[...].astype(F32) + o_y[...].astype(F32)
    ).astype(BF16)
    sum_out = Scatter(rows_of(osum, 32), x_out, z_out)
    for k in (3, 1, 2, 0):
        sum_out.ship(k)
    sum_gate.fold(3)
    sum_gate.fold(1)
    lax.fori_loop(0, 4, diagonal(1), 0)
    sum_gate.fold(2)
    sum_gate.push(2)
    lax.fori_loop(0, 6, below(1), 0)
    qkv_back(1)
    qkv_weight(1)
    sum_gate.fold(0)
    sum_down.total_into(down_pair(d))
    down_x = send(gd.at[rows(flip(d, 1), 128), half[0]], x_down, xnb)

    small_back = [send(stats, s_tensor.at[r - 1], tensor_peer[r]) for r in (1, 2, 3)]

    def make_tokens(r):
        part[block(r), :] = (
            nt(dqkv[0, block(r), :], wq[0]) + nt(dqkv[1, block(r), :], wq[1])
        ).astype(BF16)

    sum_t = Reduce(2, sum_h, make_tokens)
    sum_t.run((3, 2))
    for k in (3, 1, 0, 2):
        sum_qkv[0].fold(k)
    sum_t.run((1, 0))
    sum_qkv[0].push(2)
    for k in (3, 1, 2, 0):
        sum_out.fold(k)
    sum_out.push(2)
    for copy in small_back:
        copy.wait_recv()
    over_tensor = s_tensor[0] + s_tensor[1] + s_tensor[2]
    shared = lax.broadcasted_iota(jnp.int32, (8, 1024), 0) < 6
    s_x[0] = stats[...] + jnp.where(shared, over_tensor, 0.0)
    stat_x = send(s_x.at[0], s_x.at[1], xnb)
    for k in (3, 1, 0, 2):
        sum_qkv[1].fold(k)
    sum_qkv[1].push(2)

    outgoing = []

    def put(src, dst):
        outgoing.append(bring(src, dst))

    put(layer_out, layer_hbm)
    down_x.wait_recv()
    grad_down[:, half[0]] = gd[rows(d, 128), half[0]].astype(F32) + x_down[...].astype(F32)
    sum_down_x.total_into(grad_down.at[:, half[1]])
    put(grad_down, down_hbm)
    sum_up.total_into(grad_up)
    put(grad_up, up_hbm)
    sum_gate.total_into(grad_gate)
    put(grad_gate, gate_hbm)
    sum_out.total_into(grad_out)
    put(grad_out, out_hbm)
    stat_x.wait_recv()
    s_z[0] = s_x[0] + s_x[1]
    stat_z = [send(s_z.at[0], s_z.at[k], z_peer[2 * k]) for k in (1, 2, 3)]
    for pair in range(2):
        sum_qkv[pair].total_into(q_sum.at[pair])
    q_low[...] = q_sum[...].astype(BF16)
    q_sends = [
        send(q_low.at[:, rows(flip(t, r), 32), :], q_piece.at[t], tensor_peer[r]) for r in (2, 3, 1)
    ]
    q_piece[t] = q_low[:, rows(t, 32), :]
    sum_t.finish()

    def last_step(c, carry):
        at = rows(c, CH)
        grad_tokens[at, :] = ((1.0 - mix_a) * dr1[at, :] + sum_t.at(at)).astype(BF16)
        return carry

    lax.fori_loop(0, 256 // CH, last_step, 0)
    put(grad_tokens, tokens_hbm)
    for copy in stat_z:
        copy.wait_recv()
    stats_out[...] = s_z[0] + s_z[1] + s_z[2] + s_z[3]
    for copy in q_sends:
        copy.wait_recv()
    for slot in range(4):
        for pair, j in parts_of_qkv:
            start = j * 1024 + slot * 256 + pair * 128
            grad_qkv[:, start : start + 128] = q_piece[
                slot, pair, :, j * 128 : j * 128 + 128
            ].astype(F32)
    put(grad_qkv, qkv_hbm)
    for gather in (take_qkv, take_small, take_out):
        gather.release()
    for scatter in (sum_down, sum_down_x, sum_up, sum_gate, sum_out, *sum_qkv):
        scatter.settle()
    for copy in issued:
        sent(copy)
    for copy in outgoing:
        copy.wait()


def finish_kernel(entries, *refs):
    large, stats, outs, held, sems = refs[:7], refs[7], refs[8:21], refs[21:28], refs[28]
    taken = [pltpu.make_async_copy(large[i], held[i], sems.at[0, i]) for i in range(7)]
    given = [pltpu.make_async_copy(held[i], outs[i], sems.at[1, i]) for i in range(7)]
    for copy in taken:
        copy.start()
    s_qk, alpha_a, alpha_m, s_u, s_v, stream = outs[7:]
    index = lax.axis_index("dp") * lax.axis_size("tensor") + lax.axis_index("tensor")
    piece = s_qk.shape[0]
    pick = lax.broadcasted_iota(jnp.int32, (1024, piece), 0) == (
        lax.broadcasted_iota(jnp.int32, (1024, piece), 1) + index * piece
    )
    own = lax.dot_general(
        stats[0:3, :],
        jnp.where(pick, 1.0, 0.0),
        (((1,), (0,)), ((), ())),
        precision=lax.Precision.HIGHEST,
        preferred_element_type=F32,
    )
    for ref, row in ((alpha_a, 0), (alpha_m, 1), (s_qk, 2)):
        ref[...] = own[row]
    s_u[...] = stats[6, :]
    s_v[...] = stats[7, :]
    stream[...] = jnp.sqrt(jnp.sum(stats[3:6, :], axis=1) / entries)
    for i in range(7):
        taken[i].wait()
        given[i].start()
    for copy in given:
        copy.wait()


def fits(mesh):
    return dict(mesh.shape) == {"dp": 8, "tensor": 4}


def fused(
    tokens, cotangent, bucket_start, w_qkv, w_out, s_qk, alpha_a, alpha_m, w_up, w_gate, w_down, s_u, s_v
):
    n_rows, width = tokens.shape
    piece = s_qk.shape[0]
    vmem = pl.BlockSpec(memory_space=pltpu.VMEM)
    smem = pl.BlockSpec(memory_space=pltpu.SMEM)
    hbm = pl.BlockSpec(memory_space=pl.ANY)
    bf = lambda *shape: pltpu.VMEM(shape, BF16)
    fl = lambda *shape: pltpu.VMEM(shape, F32)
    large = [
        jax.ShapeDtypeStruct(shape, kind)
        for shape, kind in (
            ((256, 1024), BF16), ((256, 1024), BF16), ((32, 3072), F32), ((32, 1024), F32),
            ((128, 1024), F32), ((128, 1024), F32), ((128, 1024), F32),
        )
    ]
    scratch = [
        *[pltpu.VMEM(leaf.shape, leaf.dtype) for leaf in large],
        bf(1024, 1024), bf(256, 1024), bf(2, 1024, 384), bf(8, 4, 32, 1024), bf(1024, 1024),
        bf(1024, 1024), bf(1024, 1024), bf(16, 128), bf(3, 16, 128), bf(16, 1024), fl(16, 1024),
        fl(2, 1024, 256), bf(2, 1024, 384), fl(1024, 256), bf(1024, 256), bf(4, 256, 256),
        fl(256, 1024), fl(256, 1024), bf(1024, 1024), bf(1024, 1024), bf(1024, 1024), bf(1024, 1024),
        bf(1024, 1024), bf(3, 256, 1024), bf(3, 256, 1024), bf(3, 256, 1024),
        fl(256, 1024), fl(256, 1024), fl(256, 1024), bf(1024, 1024), bf(256, 1024), bf(3, 256, 256),
        bf(1024, 256), bf(2, 1024, 384), fl(4, 8, 256),
        bf(1024, 1024), bf(128, 512), bf(4, 128, 512), bf(4, 128, 1024), bf(4, 128, 1024),
        bf(2, 4, 128, 384), bf(4, 32, 1024), bf(4, 256, 512), bf(4, 128, 512), bf(4, 128, 1024), bf(4, 128, 1024), bf(2, 4, 128, 384),
        bf(4, 32, 1024), bf(256, 1024), bf(256, 1024), bf(256, 1024), bf(256, 1024),
        fl(2, 128, 384), bf(2, 128, 384), bf(4, 2, 32, 384), fl(8, 1024), fl(3, 8, 1024), fl(2, 8, 1024), fl(4, 8, 1024),
        pltpu.SemaphoreType.DMA((COPIES,)), pltpu.SemaphoreType.DMA((COPIES,)),
        pltpu.SemaphoreType.DMA((32,)),
    ]
    *big, stats = pl.pallas_call(
        fused_kernel,
        out_shape=[*large, jax.ShapeDtypeStruct((8, 1024), F32)],
        in_specs=[hbm, hbm, smem, hbm, hbm, vmem, vmem, vmem, hbm, hbm, hbm, vmem, vmem],
        out_specs=[*[hbm] * 7, vmem],
        scratch_shapes=scratch,
        compiler_params=pltpu.CompilerParams(
            collective_id=0, has_side_effects=True, vmem_limit_bytes=VMEM_BYTES
        ),
        cost_estimate=pl.CostEstimate(
            flops=27_000_000_000, bytes_accessed=8_000_000, transcendentals=10_000_000
        ),
    )(
        tokens, cotangent, bucket_start, w_qkv, w_out, s_qk, alpha_a, alpha_m,
        w_up, w_gate, w_down, s_u, s_v,
    )
    entries = n_rows * width * lax.axis_size("dp") * lax.axis_size("tensor")
    flat = [(piece,), (piece,), (piece,), (1024,), (1024,), (3,)]
    *big, g_qk, g_a, g_m, g_u, g_v, stream = pl.pallas_call(
        functools.partial(finish_kernel, float(entries)),
        out_shape=[*large, *[jax.ShapeDtypeStruct(shape, F32) for shape in flat]],
        in_specs=[hbm] * 7 + [vmem],
        out_specs=[hbm] * 7 + [vmem] * 6,
        scratch_shapes=[
            *[pltpu.VMEM(leaf.shape, leaf.dtype) for leaf in large],
            pltpu.SemaphoreType.DMA((2, 7)),
        ],
    )(*big, stats)
    return (*big[:4], g_qk, g_a, g_m, *big[4:], g_u, g_v, stream)


def solution(mesh):
    body = fused if fits(mesh) else local
    return jax.shard_map(
        body,
        mesh=mesh,
        in_specs=(
            P(("dp", "tensor"), None),
            P(("dp", "tensor"), None),
            P(),
            P(("dp", "tensor"), None),
            P(("dp", "tensor"), None),
            P(("dp", "tensor")),
            P(("dp", "tensor")),
            P(("dp", "tensor")),
            P("dp", "tensor"),
            P("dp", "tensor"),
            P("dp", "tensor"),
            P("tensor"),
            P("tensor"),
        ),
        out_specs=(
            P(("dp", "tensor"), None),
            P(("dp", "tensor"), None),
            P(("dp", "tensor"), None),
            P(("dp", "tensor"), None),
            P(("dp", "tensor")),
            P(("dp", "tensor")),
            P(("dp", "tensor")),
            P("dp", "tensor"),
            P("dp", "tensor"),
            P("dp", "tensor"),
            P("tensor"),
            P("tensor"),
            P(),
        ),
        check_vma=False,
    )
```

```python
import functools
import math

import jax
import jax.numpy as jnp
from jax import lax
from jax.experimental import pallas as pl
from jax.experimental.pallas import tpu as pltpu
from jax.sharding import PartitionSpec as P

HEAD_DIM = 64


EPSILON = 1e-06
MASKED_SCORE = -1e30


def rms_rows(value):
    return value * lax.rsqrt(jnp.mean(value * value, axis=-1, keepdims=True) + EPSILON)


def rms_back(upstream, normed, source):
    factor = lax.rsqrt(jnp.mean(source * source, axis=-1, keepdims=True) + EPSILON)
    return factor * (upstream - normed * jnp.mean(upstream * normed, axis=-1, keepdims=True))


def unit_heads(value):
    shaped = value.reshape(value.shape[0], -1, HEAD_DIM)
    factor = lax.rsqrt(jnp.sum(shaped * shaped, axis=-1, keepdims=True) + EPSILON)
    return ((shaped * factor).reshape(value.shape), factor)


def unit_back(upstream, normed, factor):
    upper_grad = upstream.reshape(normed.shape[0], -1, HEAD_DIM)
    normed_heads = normed.reshape(normed.shape[0], -1, HEAD_DIM)
    result = factor * (
        upper_grad - normed_heads * jnp.sum(upper_grad * normed_heads, axis=-1, keepdims=True)
    )
    return result.reshape(upstream.shape)


def block_span(total_rows, row_count):
    units = total_rows // row_count
    block_units = max(1, min(units, 512 // row_count))
    while units % block_units:
        block_units -= 1
    return row_count * block_units


def local(
    tokens,
    cotangent,
    bucket_start,
    w_qkv,
    w_out,
    s_qk,
    alpha_a,
    alpha_m,
    w_up,
    w_gate,
    w_down,
    s_u,
    s_v,
):
    row_count, model_width = tokens.shape
    head_count = model_width // HEAD_DIM
    score_scale = math.sqrt(HEAD_DIM)
    spread = lax.axis_size("tensor")
    group_rows = spread * row_count
    tensor_slot = lax.axis_index("tensor")
    qkv_full, out_full, gain_qk, mix_attn, mix_mlp = (
        lax.all_gather(w_qkv, ("dp", "tensor"), axis=0, tiled=True),
        lax.all_gather(w_out, ("dp", "tensor"), axis=0, tiled=True),
        lax.all_gather(s_qk, ("dp", "tensor"), axis=0, tiled=True),
        lax.all_gather(alpha_a, ("dp", "tensor"), axis=0, tiled=True),
        lax.all_gather(alpha_m, ("dp", "tensor"), axis=0, tiled=True),
    )
    up_full, gate_full, down_full = (
        lax.all_gather(w_up, "dp", axis=0, tiled=True),
        lax.all_gather(w_gate, "dp", axis=0, tiled=True),
        lax.all_gather(w_down, "dp", axis=0, tiled=True),
    )
    gain_qk = gain_qk.astype(jnp.float32)
    mix_attn = mix_attn.astype(jnp.float32)
    mix_mlp = mix_mlp.astype(jnp.float32)
    scale_up = s_u.astype(jnp.float32)
    scale_gate = s_v.astype(jnp.float32)
    starts = lax.dynamic_slice_in_dim(bucket_start, lax.axis_index("dp") * spread, spread)
    key_seq = jnp.repeat(starts, row_count)
    own_seq = starts[tensor_slot]
    query_pos = tensor_slot * row_count + jnp.arange(row_count, dtype=jnp.int32)

    def allowed(key_start, key_count):
        key_pos = key_start + jnp.arange(key_count, dtype=jnp.int32)
        seq_part = lax.dynamic_slice_in_dim(key_seq, key_start, key_count)
        return (key_pos[None, :] <= query_pos[:, None]) & (seq_part[None, :] == own_seq)

    inputs = tokens.astype(jnp.float32)
    qkv = jnp.dot(tokens, qkv_full, preferred_element_type=jnp.float32)
    q_unit, q_factor = unit_heads(qkv[:, :model_width])
    k_unit, k_factor = unit_heads(qkv[:, model_width : 2 * model_width])
    query_low = (q_unit * gain_qk).astype(jnp.bfloat16)
    keys_low = (k_unit * gain_qk).astype(jnp.bfloat16)
    values_low = qkv[:, 2 * model_width :].astype(jnp.bfloat16)
    query_heads = query_low.reshape(row_count, head_count, HEAD_DIM)
    key_all, value_all = (
        lax.all_gather(keys_low, "tensor", axis=0, tiled=True),
        lax.all_gather(values_low, "tensor", axis=0, tiled=True),
    )
    key_block = block_span(group_rows, row_count)
    blocks = group_rows // key_block

    def block_scores(key_source, key_start, key_count):
        key_part = lax.dynamic_slice_in_dim(key_source, key_start, key_count).reshape(
            key_count, head_count, HEAD_DIM
        )
        return (
            jnp.einsum("qhd,khd->hqk", query_heads, key_part, preferred_element_type=jnp.float32)
            * score_scale
        )

    def stat_step(state_pair, block_index):
        row_top, row_total = state_pair
        key_start = block_index * key_block
        allowed_keys = allowed(key_start, key_block)[None]
        masked = jnp.where(allowed_keys, block_scores(key_all, key_start, key_block), MASKED_SCORE)
        new_top = jnp.maximum(row_top, jnp.max(masked, axis=-1))
        fresh = jnp.where(allowed_keys, jnp.exp(masked - new_top[..., None]), 0.0)
        row_total = row_total * jnp.exp(row_top - new_top) + jnp.sum(fresh, axis=-1)
        return ((new_top, row_total), None)

    start_state = (
        jnp.full((head_count, row_count), MASKED_SCORE, jnp.float32),
        jnp.zeros((head_count, row_count), jnp.float32),
    )
    (row_top, row_total), _ = lax.scan(stat_step, start_state, jnp.arange(blocks))
    log_total = row_top + jnp.log(row_total)

    def probs_for(key_source, key_start, key_count):
        scores = block_scores(key_source, key_start, key_count)
        allowed_keys = allowed(key_start, key_count)[None]
        return jnp.where(allowed_keys, jnp.exp(scores - log_total[..., None]), 0.0)

    def value_part(value_source, key_start, key_count):
        return lax.dynamic_slice_in_dim(value_source, key_start, key_count).reshape(
            key_count, head_count, HEAD_DIM
        )

    def out_step(carry_sum, block_index):
        key_start = block_index * key_block
        attn_probs = probs_for(key_all, key_start, key_block).astype(jnp.bfloat16)
        term = jnp.einsum(
            "hqk,khd->qhd",
            attn_probs,
            value_part(value_all, key_start, key_block),
            preferred_element_type=jnp.float32,
        )
        return (carry_sum + term, None)

    attended, _ = lax.scan(
        out_step, jnp.zeros((row_count, head_count, HEAD_DIM), jnp.float32), jnp.arange(blocks)
    )
    attended_low = attended.reshape(row_count, model_width).astype(jnp.bfloat16)
    branch_a = jnp.dot(attended_low, out_full, preferred_element_type=jnp.float32)
    h_attn = rms_rows(branch_a)
    resid_one = inputs + mix_attn * (h_attn - inputs)
    hidden_one = rms_rows(resid_one)
    hidden_low = hidden_one.astype(jnp.bfloat16)
    rows_all = lax.all_gather(hidden_low, "tensor", axis=0, tiled=True)
    up_raw = jnp.dot(rows_all, up_full, preferred_element_type=jnp.float32)
    gate_raw = jnp.dot(rows_all, gate_full, preferred_element_type=jnp.float32)
    up_scaled = up_raw * scale_up
    gate_scaled = gate_raw * scale_gate
    gate_sigmoid = jax.nn.sigmoid(gate_scaled)
    silu_gate = gate_scaled * gate_sigmoid
    inner_low = (up_scaled * silu_gate).astype(jnp.bfloat16)
    branch_m = lax.psum_scatter(
        jnp.einsum("tf,df->td", inner_low, down_full, preferred_element_type=jnp.float32).astype(
            jnp.bfloat16
        ),
        "tensor",
        scatter_dimension=0,
        tiled=True,
    ).astype(jnp.float32)
    h_mlp = rms_rows(branch_m)
    resid_two = hidden_one + mix_mlp * (h_mlp - hidden_one)
    result = rms_rows(resid_two)
    partial_stats = jnp.stack(
        [jnp.sum(branch_a * branch_a), jnp.sum(branch_m * branch_m), jnp.sum(resid_two * resid_two)]
    )
    upstream = cotangent.astype(jnp.float32)
    d_resid_two = rms_back(upstream, result, resid_two)
    grad_mix_mlp = jnp.sum(d_resid_two * (h_mlp - hidden_one), axis=0)
    d_branch_m = rms_back(mix_mlp * d_resid_two, h_mlp, branch_m).astype(jnp.bfloat16)
    grads_all = lax.all_gather(d_branch_m, "tensor", axis=0, tiled=True)
    d_inner = jnp.dot(grads_all, down_full, preferred_element_type=jnp.float32)
    grad_up_scaled = d_inner * silu_gate
    grad_gate_scaled = (
        d_inner * up_scaled * gate_sigmoid * (1.0 + gate_scaled * (1.0 - gate_sigmoid))
    )
    grad_scale_up = jnp.sum(grad_up_scaled * up_raw, axis=0)
    grad_scale_gate = jnp.sum(grad_gate_scaled * gate_raw, axis=0)
    up_grad_low = (grad_up_scaled * scale_up).astype(jnp.bfloat16)
    gate_grad_low = (grad_gate_scaled * scale_gate).astype(jnp.bfloat16)
    grad_down = jnp.einsum("td,tf->df", grads_all, inner_low, preferred_element_type=jnp.float32)
    grad_up = jnp.einsum("td,tf->df", rows_all, up_grad_low, preferred_element_type=jnp.float32)
    grad_gate = jnp.einsum("td,tf->df", rows_all, gate_grad_low, preferred_element_type=jnp.float32)
    first = jnp.einsum("tf,df->td", up_grad_low, up_full, preferred_element_type=jnp.float32)
    d_hidden_one = (1.0 - mix_mlp) * d_resid_two + lax.psum_scatter(
        (
            first
            + jnp.einsum("tf,df->td", gate_grad_low, gate_full, preferred_element_type=jnp.float32)
        ).astype(jnp.bfloat16),
        "tensor",
        scatter_dimension=0,
        tiled=True,
    ).astype(jnp.float32)
    d_resid_one = rms_back(d_hidden_one, hidden_one, resid_one)
    grad_mix_attn = jnp.sum(d_resid_one * (h_attn - inputs), axis=0)
    d_branch_a = rms_back(mix_attn * d_resid_one, h_attn, branch_a).astype(jnp.bfloat16)
    grad_out = jnp.einsum("tc,td->cd", attended_low, d_branch_a, preferred_element_type=jnp.float32)
    d_attended = jnp.einsum(
        "td,cd->tc", d_branch_a, out_full, preferred_element_type=jnp.float32
    ).astype(jnp.bfloat16)
    d_heads = d_attended.reshape(row_count, head_count, HEAD_DIM)
    row_delta = jnp.sum(d_heads.astype(jnp.float32) * attended, axis=-1).T
    key_back, value_back = (
        lax.all_gather(keys_low, "tensor", axis=0, tiled=True),
        lax.all_gather(values_low, "tensor", axis=0, tiled=True),
    )

    def score_grads(key_start, key_count):
        attn_probs = probs_for(key_back, key_start, key_count)
        d_probs = jnp.einsum(
            "qhd,khd->hqk",
            d_heads,
            value_part(value_back, key_start, key_count),
            preferred_element_type=jnp.float32,
        )
        d_scores = (attn_probs * (d_probs - row_delta[..., None])).astype(jnp.bfloat16)
        return (attn_probs, d_scores)

    def query_step(carry_sum, block_index):
        key_start = block_index * key_block
        attn_probs, d_scores = score_grads(key_start, key_block)
        key_part = lax.dynamic_slice_in_dim(key_back, key_start, key_block).reshape(
            key_block, head_count, HEAD_DIM
        )
        return (
            carry_sum
            + jnp.einsum("hqk,khd->qhd", d_scores, key_part, preferred_element_type=jnp.float32),
            None,
        )

    d_query, _ = lax.scan(
        query_step, jnp.zeros((row_count, head_count, HEAD_DIM), jnp.float32), jnp.arange(blocks)
    )
    d_query = d_query.reshape(row_count, model_width) * score_scale
    part_rows = lax.axis_size("tensor") * row_count
    sub_block = block_span(part_rows, row_count)

    def one_block(block_index):
        begin = block_index * sub_block
        attn_probs, d_scores = score_grads(begin, sub_block)
        d_keys = (
            jnp.einsum("hqk,qhd->khd", d_scores, query_heads, preferred_element_type=jnp.float32)
            * score_scale
        )
        d_values = jnp.einsum(
            "hqk,qhd->khd",
            attn_probs.astype(jnp.bfloat16),
            d_heads,
            preferred_element_type=jnp.float32,
        )
        return jnp.concatenate(
            [d_keys.reshape(sub_block, model_width), d_values.reshape(sub_block, model_width)],
            axis=1,
        )

    block_terms = lax.map(one_block, jnp.arange(part_rows // sub_block))
    key_grads = lax.psum_scatter(
        block_terms.reshape(part_rows, 2 * model_width).astype(jnp.bfloat16),
        "tensor",
        scatter_dimension=0,
        tiled=True,
    ).astype(jnp.float32)
    d_keys_own = key_grads[:, :model_width]
    d_values_own = key_grads[:, model_width:]
    grad_gain = jnp.sum(d_query * q_unit + d_keys_own * k_unit, axis=0)
    d_qkv = jnp.concatenate(
        [
            unit_back(d_query * gain_qk, q_unit, q_factor),
            unit_back(d_keys_own * gain_qk, k_unit, k_factor),
            d_values_own,
        ],
        axis=1,
    ).astype(jnp.bfloat16)
    grad_qkv = jnp.einsum("tc,tf->cf", tokens, d_qkv, preferred_element_type=jnp.float32)
    d_tokens = (1.0 - mix_attn) * d_resid_one + jnp.einsum(
        "tf,cf->tc", d_qkv, qkv_full, preferred_element_type=jnp.float32
    )
    sum_qkv, sum_out, sum_gain, sum_mix_attn, sum_mix_mlp = (
        lax.psum_scatter(grad_qkv, ("dp", "tensor"), scatter_dimension=0, tiled=True),
        lax.psum_scatter(grad_out, ("dp", "tensor"), scatter_dimension=0, tiled=True),
        lax.psum_scatter(grad_gain, ("dp", "tensor"), scatter_dimension=0, tiled=True),
        lax.psum_scatter(grad_mix_attn, ("dp", "tensor"), scatter_dimension=0, tiled=True),
        lax.psum_scatter(grad_mix_mlp, ("dp", "tensor"), scatter_dimension=0, tiled=True),
    )
    sum_up, sum_gate, sum_down = (
        lax.psum_scatter(
            grad_up.astype(jnp.bfloat16), "dp", scatter_dimension=0, tiled=True
        ).astype(jnp.float32),
        lax.psum_scatter(
            grad_gate.astype(jnp.bfloat16), "dp", scatter_dimension=0, tiled=True
        ).astype(jnp.float32),
        lax.psum_scatter(
            grad_down.astype(jnp.bfloat16), "dp", scatter_dimension=0, tiled=True
        ).astype(jnp.float32),
    )
    sum_scale_up, sum_scale_gate = lax.psum((grad_scale_up, grad_scale_gate), "dp")
    stat_sums = lax.psum(partial_stats, ("dp", "tensor"))
    entry_count = row_count * model_width * lax.axis_size("dp") * spread
    stream_rms = jnp.sqrt(stat_sums / entry_count)
    return (
        result.astype(jnp.bfloat16),
        d_tokens.astype(jnp.bfloat16),
        sum_qkv,
        sum_out,
        sum_gain,
        sum_mix_attn,
        sum_mix_mlp,
        sum_up,
        sum_gate,
        sum_down,
        sum_scale_up,
        sum_scale_gate,
        stream_rms,
    )


MESH = pl.DeviceIdType.MESH
BF16 = jnp.bfloat16
F32 = jnp.float32
LOG2E = 1.4426950408889634
COPIES = 224
VMEM_BYTES = 63 * 2**20
CH = 32


def nn(left, right):
    return lax.dot_general(left, right, (((1,), (0,)), ((), ())), preferred_element_type=F32)


def nt(left, right):
    return lax.dot_general(left, right, (((1,), (1,)), ((), ())), preferred_element_type=F32)


def tn(left, right):
    return lax.dot_general(left, right, (((0,), (0,)), ((), ())), preferred_element_type=F32)


def flip(index, bits):
    bit = 1
    while bit <= bits:
        if bits & bit:
            index = index + bit - 2 * bit * lax.rem(lax.div(index, bit), 2)
        bit *= 2
    return index


def mixed(a, b):
    low = lax.rem(a, 2) + lax.rem(b, 2) - 2 * lax.rem(a, 2) * lax.rem(b, 2)
    high_a, high_b = lax.div(a, 2), lax.div(b, 2)
    return low + 2 * (high_a + high_b - 2 * high_a * high_b)


def mean_rows(value):
    return jnp.mean(value, axis=-1, keepdims=True)


def rows(start, count=256):
    return pl.ds(pl.multiple_of(start * count, count), count)


def block(r):
    return pl.ds(r * 256, 256)


def fused_kernel(
    tokens, cotangent, bucket_start, w_qkv, w_out, s_qk, alpha_a, alpha_m, w_up, w_gate, w_down, scale_u,
    scale_v,
    layer_hbm, tokens_hbm, qkv_hbm, out_hbm, up_hbm, gate_hbm, down_hbm, stats_hbm,
    layer_out, grad_tokens, grad_qkv, grad_out, grad_up, grad_gate, grad_down, stats_sum,
    tok, cot, wq, wo, wu, wg, wd, small, small_t, small_d, gains,
    raw, qkv, linv, att, ato, branch, hid, h1, ur, gr, inn,
    part, from_core3, from_core1, from_y,
    dr2, dr1, d_inner_f32, db, dba, dat, dao, dqkv, delta,
    gd, x_down, x_down_x, x_up, x_gate, x_qkv, x_out, z_down, z_down_x, z_up, z_gate, z_qkv, z_out,
    o_core3, o_core1, o_y, osum, q_sum, q_low, q_piece, stats, s_tensor, s_x, s_z,
    send_sem, recv_sem, local_sem,
):
    d = lax.axis_index("dp")
    t = lax.axis_index("tensor")
    z = lax.div(d, 2)
    inner = lax.rem(lax.div(z + 1, 2), 2) == 1
    core, ynb, diag = (d, flip(t, 1)), (d, flip(t, 2)), (d, flip(t, 3))
    tensor_peer = {1: core, 2: ynb, 3: diag}
    xnb = (flip(d, 1), t)
    z_peer = {m: (flip(d, m), t) for m in (2, 4, 6)}

    barrier = pltpu.get_barrier_semaphore()
    peers = [core, ynb, diag, xnb] + [z_peer[m] for m in (2, 4, 6)]
    for peer in peers:
        pl.semaphore_signal(barrier, inc=1, device_id=peer, device_id_type=MESH)

    issued = []
    used = [0]

    def number():
        used[0] += 1
        return used[0] - 1

    def describe(src, dst, peer, at, to):
        return pltpu.make_async_remote_copy(
            src_ref=src,
            dst_ref=dst,
            send_sem=send_sem.at[at],
            recv_sem=recv_sem.at[to],
            device_id=peer,
            device_id_type=MESH,
        )

    def send(src, dst, peer):
        at = number()
        copy = describe(src, dst, peer, at, at)
        copy.start()
        issued.append(copy)
        return copy

    waited = set()

    def sent(copy):
        if id(copy) not in waited:
            waited.add(id(copy))
            copy.wait_send()

    locals_ = []

    def bring(src, dst):
        copy = pltpu.make_async_copy(src, dst, local_sem.at[len(locals_)])
        copy.start()
        locals_.append(copy)
        return copy

    outer = jnp.logical_not(inner)

    class Gather:
        def __init__(self, src, view):
            self.src, self.view = src, view
            self.at6, self.relay_at = number(), number()

        def start_x(self):
            self.x = [send(self.src, self.view(d), xnb)]

        def start_far(self):
            self.z = {4: send(self.src, self.view(d), z_peer[4])}
            self.start_straight()

        def start_straight(self):
            self.straight = describe(self.src, self.view(d), z_peer[6], self.at6, self.at6)
            pl.when(inner)(self.straight.start)

        def start_near(self):
            self.z[2] = send(self.src, self.view(d), z_peer[2])

        def start_z(self):
            self.start_far()
            self.start_near()

        def hop(self):
            self.z[4].wait_recv()
            self.hand_on()

        def hand_on(self):
            shard = self.view(flip(d, 4))
            self.relay = describe(shard, shard, z_peer[2], self.relay_at, self.at6)
            pl.when(inner)(self.relay.start)

        def forward_one(self, m):
            if m == 2:
                self.z[2].wait_recv()
            if m == 6:
                self.straight.wait_recv()
            shard = self.view(flip(d, m))
            self.x.append(send(shard, shard, xnb))

        def forward(self):
            self.forward_one(2)
            self.hop()
            self.forward_one(4)
            self.forward_one(6)

        def finish(self):
            for copy in self.x:
                copy.wait_recv()

        def release(self):
            for copy in [*self.z.values(), *self.x]:
                sent(copy)
            for copy in (self.straight, self.relay):
                pl.when(inner)(copy.wait_send)

    class GatherPairs(Gather):
        def __init__(self, src, shard, pair):
            super().__init__(src, pair)
            self.shard = shard

        def start_x(self):
            self.x = [send(self.src, self.shard(d), xnb)]

        def start_far(self):
            self.x[0].wait_recv()
            self.src = self.view(d)
            self.z = {4: send(self.src, self.view(d), z_peer[4])}

        def hop(self):
            self.z[4].wait_recv()
            self.start_straight()
            self.hand_on()

    def rows_of(ref, count=128):
        return lambda index: ref.at[rows(index, count)]

    def pair_of(ref):
        return lambda index: ref.at[rows(lax.div(index, 2))]

    take_qkv = Gather(wq.at[:, rows(d, 128), :], lambda index: wq.at[:, rows(index, 128), :])
    take_small = Gather(small_d.at[:, rows(d, 128)], lambda index: small_d.at[:, rows(index, 128)])
    take_out = Gather(w_out, lambda index: wo.at[index, t])
    take_up = Gather(w_up, rows_of(wu))
    take_gate = Gather(w_gate, rows_of(wg))
    take_down = GatherPairs(w_down, rows_of(wd), pair_of(wd))

    piece = s_qk.shape[0]
    own_qkv = pl.ds(pl.multiple_of(d * 128 + t * 32, 32), 32)

    def qkv_cols(slot, pair, j):
        return pl.ds(pl.multiple_of(j * 1024 + slot * 256 + pair * 128, 128), 128)

    def qkv_place(pair, j):
        return wq.at[pair, own_qkv, j * 128 : j * 128 + 128]

    parts_of_qkv = [(pair, j) for pair in range(2) for j in range(3)]
    local_qkv = [
        bring(w_qkv.at[:, qkv_cols(t, pair, j)], qkv_place(pair, j)) for pair, j in parts_of_qkv
    ]
    local_tok = bring(tokens, tok.at[block(0)])
    local_rest = [
        bring(w_out, wo.at[d, t]),
        bring(w_up, wu.at[rows(d, 128)]),
        bring(w_gate, wg.at[rows(d, 128)]),
        bring(w_down, wd.at[rows(d, 128)]),
        bring(cotangent, cot),
    ]
    place = jnp.where(
        lax.broadcasted_iota(jnp.int32, (piece, 128), 1)
        == lax.broadcasted_iota(jnp.int32, (piece, 128), 0) + t * piece,
        1.0,
        0.0,
    ).astype(BF16)
    small_row = lax.broadcasted_iota(jnp.int32, (16, 128), 0)
    placed = jnp.zeros((16, 128), F32)
    for index, vector in enumerate((s_qk, alpha_a, alpha_m)):
        placed = jnp.where(small_row == index, nn(vector[...].reshape(1, piece), place), placed)
    small[...] = placed.astype(BF16)
    stats[...] = jnp.zeros_like(stats)
    gain_u = scale_u[...].astype(F32).reshape(1, 1024)
    gain_v = scale_v[...].astype(F32).reshape(1, 1024)
    pl.semaphore_wait(barrier, len(peers))

    small_sends = [send(small, small_t.at[r - 1], tensor_peer[r]) for r in (2, 3, 1)]
    qkv_sends = [
        send(w_qkv.at[:, qkv_cols(flip(t, r), pair, j)], qkv_place(pair, j), tensor_peer[r])
        for r in (2, 3, 1)
        for pair, j in parts_of_qkv
    ]
    take_out.start_z()
    take_down.start_x()
    take_out.start_x()
    take_up.start_x()
    for copy in small_sends:
        copy.wait_recv()
    small_d[:, rows(d, 128)] = small[...] + small_t[0] + small_t[1] + small_t[2]
    take_small.start_z()
    take_small.start_x()
    for copy in local_qkv:
        copy.wait()
    for copy in qkv_sends:
        copy.wait_recv()
    take_qkv.start_z()
    take_qkv.start_x()
    tok_y = send(tokens, tok.at[block(2)], ynb)
    tok_core = send(tokens, tok.at[block(1)], core)
    take_up.start_far()

    take_out.hop()
    take_small.hop()
    take_small.forward_one(4)
    take_small.forward_one(2)
    take_qkv.hop()
    take_qkv.forward_one(4)
    take_up.start_near()
    take_qkv.forward_one(2)
    take_small.forward_one(6)
    take_qkv.forward_one(6)
    take_out.forward_one(4)
    take_out.forward_one(2)
    take_out.forward_one(6)
    take_gate.start_far()
    tok_y.wait_recv()
    tok_diag = send(tok.at[block(2)], tok.at[block(3)], core)
    take_small.finish()
    gains[...] = small_d[...].astype(F32)
    take_qkv.finish()
    local_tok.wait()
    tok_core.wait_recv()
    tok_diag.wait_recv()

    def gain_pair(pair):
        gain = gains[0:1, pl.ds(pl.multiple_of(t * 256 + pair * 128, 128), 128)]
        return jnp.concatenate([gain, gain], axis=1)

    first_head = lax.broadcasted_iota(jnp.int32, (256, 128), 1) < HEAD_DIM
    same_head = jnp.where(
        lax.div(lax.broadcasted_iota(jnp.int32, (256, 256), 0), HEAD_DIM)
        == lax.div(lax.broadcasted_iota(jnp.int32, (256, 256), 1), HEAD_DIM),
        1.0,
        0.0,
    ).astype(BF16)

    def head_sum(value):
        high = value.astype(BF16)
        low = (value - high.astype(F32)).astype(BF16)
        return nn(high, same_head) + nn(low, same_head)

    def qkv_step(r, carry):
        at = rows(r)
        x = tok[at, :]
        for pair in range(2):
            y = nn(x, wq[pair])
            qk = y[:, :256]
            raw[pair, at, :] = qk
            factor = lax.rsqrt(head_sum(qk * qk) + EPSILON)
            qkv[pair, at, :256] = (qk * factor * gain_pair(pair)).astype(BF16)
            qkv[pair, at, 256:] = y[:, 256:].astype(BF16)
        return carry

    lax.fori_loop(0, 4, qkv_step, 0)

    take_out.finish()
    local_rest[0].wait()
    wo_y = send(wo.at[:, t], wo.at[:, t], ynb)
    wo_core = send(wo.at[:, t], wo.at[:, t], core)

    def true_rows(i):
        return rows(flip(t, i))

    whole = jnp.where(bucket_start[d * 4] == bucket_start[d * 4 + 2], 1.0, 0.0)
    row_id = lax.broadcasted_iota(jnp.int32, (256, 256), 0)
    col_id = lax.broadcasted_iota(jnp.int32, (256, 256), 1)
    exp_scale = math.sqrt(HEAD_DIM) * LOG2E

    def two_heads(value):
        zero = jnp.zeros_like(value)
        return jnp.concatenate(
            [jnp.where(first_head, value, zero), jnp.where(first_head, zero, value)], axis=0
        )

    def one_of_two(value):
        return jnp.where(first_head, value[:256], value[256:])

    causal = jnp.concatenate([col_id <= row_id] * 2, axis=0)

    def attend(i):
        at = true_rows(i)

        def head_step(pair, carry):
            q = two_heads(qkv[pair, at, 0:128])
            acc = jnp.zeros((512, 128), F32)
            weight = jnp.zeros((512, 1), F32)
            for j in range(i + 1):
                key_at = true_rows(j)
                e = jnp.exp2(nt(q, qkv[pair, key_at, 128:256]) * exp_scale)
                if j == i:
                    e = jnp.where(causal, e, 0.0)
                elif j // 2 != i // 2:
                    e = e * whole
                weight = weight + jnp.sum(e, axis=1, keepdims=True)
                acc = acc + nn(e.astype(BF16), qkv[pair, key_at, 256:384])
            inverse = 1.0 / weight
            lanes = rows(pair, 128)
            linv[at, lanes] = one_of_two(jnp.broadcast_to(inverse, (512, 128)))
            att[at, lanes] = one_of_two(acc * inverse).astype(BF16)
            return carry

        lax.fori_loop(0, 2, head_step, 0)

    attend(0)
    attend(1)
    take_up.hop()
    take_up.forward_one(4)
    take_gate.start_near()
    take_gate.start_x()
    take_up.forward_one(2)
    for copy in local_rest[1:]:
        copy.wait()
    take_down.start_far()
    attend(2)
    attend(3)

    att_sends = [send(att.at[block(r)], ato.at[t], tensor_peer[r]) for r in (2, 3, 1)]
    ato[t] = att[block(0), :]
    wo_y.wait_recv()
    wo_far = send(wo.at[:, flip(t, 2)], wo.at[:, flip(t, 2)], core)
    take_up.forward_one(6)
    for copy in att_sends:
        copy.wait_recv()
    wo_core.wait_recv()
    wo_far.wait_recv()

    def out_rows(slot, columns):
        return wo[2 * slot : 2 * slot + 2, :, :, columns].reshape(256, 256)

    def out_step(n, carry):
        at = rows(n)
        acc = nn(ato[0], out_rows(0, at))
        for slot in range(1, 4):
            acc = acc + nn(ato[slot], out_rows(slot, at))
        branch[:, at] = acc
        return carry

    lax.fori_loop(0, 4, out_step, 0)

    mix_a = gains[1:2, :]
    mix_m = gains[2:3, :]

    def add_stat(row, value):
        stats[row : row + 1, :] = stats[row : row + 1, :] + jnp.sum(value, axis=0, keepdims=True)

    def first_norm(at):
        x = tok[at, :].astype(F32)
        ba = branch[at, :]
        fa = lax.rsqrt(mean_rows(ba * ba) + EPSILON)
        ha = ba * fa
        r1 = x + mix_a * (ha - x)
        f1 = lax.rsqrt(mean_rows(r1 * r1) + EPSILON)
        return x, ba, fa, ha, f1, r1 * f1

    def norm_step(c, carry):
        at = rows(c, CH)
        _, ba, _, _, _, hidden = first_norm(at)
        add_stat(3, ba * ba)
        hid[at, :] = hidden
        h1[at, :] = hidden.astype(BF16)
        return carry

    lax.fori_loop(0, 256 // CH, norm_step, 0)

    def spread(ref):
        return send(ref.at[block(0)], ref.at[block(2)], ynb), send(
            ref.at[block(0)], ref.at[block(1)], core
        )

    def relay(ref, from_ynb):
        from_ynb.wait_recv()
        return send(ref.at[block(2)], ref.at[block(3)], core)

    h1_y, h1_core = spread(h1)
    take_gate.hop()
    take_gate.forward_one(4)
    take_down.start_near()
    take_gate.forward_one(2)
    h1_far = relay(h1, h1_y)
    take_gate.forward_one(6)
    take_down.hop()
    take_up.finish()
    h1_core.wait_recv()
    h1_far.wait_recv()
    take_gate.finish()

    def up_step(r, carry):
        at = rows(r)
        hidden = h1[at, :]
        u_raw = nn(hidden, wu[...])
        g_raw = nn(hidden, wg[...])
        gate = g_raw * gain_v
        silu = gate / (1.0 + jnp.exp(-gate))
        ur[at, :] = u_raw.astype(BF16)
        gr[at, :] = g_raw.astype(BF16)
        inn[at, :] = (u_raw * gain_u * silu).astype(BF16)
        return carry

    lax.fori_loop(0, 4, up_step, 0)

    class Reduce:
        def __init__(self, which, before, make):
            self.which, self.before, self.make = which, before, make
            self.copies = {}

        def run(self, order):
            for r in order:
                self.step(r)

        def step(self, r):
            k = self.which
            if r in self.before.copies:
                before = self.before.copies[r]
                for copy in before if isinstance(before, list) else [before]:
                    sent(copy)
            self.make(r)
            if r == 3:
                self.copies[3] = send(part.at[block(3)], from_core3.at[k], core)
            elif r == 2:
                self.copies[3].wait_recv()
                self.copies[2] = []
                for c in range(4):
                    here, there = pl.ds(512 + c * 64, 64), pl.ds(c * 64, 64)
                    part[here, :] = (
                        part[here, :].astype(F32) + from_core3[k, there, :].astype(F32)
                    ).astype(BF16)
                    self.copies[2].append(send(part.at[here], from_y.at[k, there], ynb))
            elif r == 1:
                self.copies[1] = send(part.at[block(1)], from_core1.at[k], core)

        def finish(self):
            self.copies[1].wait_recv()
            for copy in self.copies[2]:
                copy.wait_recv()

        def at(self, where):
            k = self.which
            return (
                part[where, :].astype(F32)
                + from_core1[k, where, :].astype(F32)
                + from_y[k, where, :].astype(F32)
            )

    class ReduceColumns:
        def __init__(self):
            self.copies = {r: [] for r in (1, 2, 3)}
            self.columns = []

        def step(self, k):
            cols = rows(lax.div(flip(d, 2 * k), 2))
            part[:, cols] = nt(inn[...], wd[cols, :]).astype(BF16)
            self.columns.append(cols)
            self.copies[3].append(send(part.at[block(3), cols], from_core3.at[0, :, cols], core))
            self.copies[1].append(send(part.at[block(1), cols], from_core1.at[0, :, cols], core))

        def pass_on(self, parts=1):
            done = len(self.copies[2])
            cols = self.columns[done]
            self.copies[3][done].wait_recv()
            count = 256 // parts
            for c in range(parts):
                here, there = pl.ds(512 + c * count, count), pl.ds(c * count, count)
                part[here, cols] = (
                    part[here, cols].astype(F32) + from_core3[0, there, cols].astype(F32)
                ).astype(BF16)
                self.copies[2].append(
                    send(part.at[here, cols], from_y.at[0, there, cols], ynb)
                )

        def finish(self):
            for copy in self.copies[1] + self.copies[2][:-4]:
                copy.wait_recv()

        def finish_rows(self, c):
            self.copies[2][c - 4].wait_recv()

        at = Reduce.at
        which = 0

    sum_m = ReduceColumns()
    sum_m.step(0)
    take_down.z[2].wait_recv()
    sum_m.step(1)
    sum_m.pass_on()
    sum_m.step(2)
    sum_m.pass_on()
    take_down.straight.wait_recv()
    sum_m.step(3)
    sum_m.pass_on()
    sum_m.pass_on(4)
    sum_m.finish()

    def loss_step(c, carry):
        at = rows(c, CH)
        bm = sum_m.at(at)
        hidden = hid[at, :]
        fm = lax.rsqrt(mean_rows(bm * bm) + EPSILON)
        hm = bm * fm
        r2 = hidden + mix_m * (hm - hidden)
        f2 = lax.rsqrt(mean_rows(r2 * r2) + EPSILON)
        result = r2 * f2
        layer_out[at, :] = result.astype(BF16)
        up = cot[at, :].astype(F32)
        grad = f2 * (up - result * mean_rows(up * result))
        dr2[at, :] = grad
        add_stat(1, grad * (hm - hidden))
        add_stat(4, bm * bm)
        add_stat(5, r2 * r2)
        c_m = mix_m * grad
        db[at, :] = (fm * (c_m - hm * mean_rows(c_m * hm))).astype(BF16)
        return carry

    class Spread:
        def __init__(self, ref):
            self.ref, self.y, self.core = ref, [], []

        def piece(self, r, c):
            return self.ref.at[pl.ds(r * 256 + c * 64, 64)]

        def start(self, c):
            self.y.append(send(self.piece(0, c), self.piece(2, c), ynb))
            self.core.append(send(self.piece(0, c), self.piece(1, c), core))

        def relay(self, c):
            self.y[c].wait_recv()
            self.core.append(send(self.piece(2, c), self.piece(3, c), core))

    db_rows = Spread(db)
    for c in range(4):
        sum_m.finish_rows(c)
        lax.fori_loop(c * (64 // CH), (c + 1) * (64 // CH), loss_step, 0)
        db_rows.start(c)

    class AlongZ:
        def __init__(self, view, landing):
            self.view, self.landing = view, landing
            self.at6, self.relay_at = number(), number()
            self.z = {}

        def far_copies(self):
            shard = self.view(flip(d, 6))
            return (
                describe(shard, self.landing.at[2], z_peer[6], self.at6, self.at6),
                describe(shard, self.landing.at[3], z_peer[2], self.relay_at, self.relay_at),
            )

        def start_far(self):
            straight, over = self.far_copies()
            pl.when(inner)(straight.start)
            pl.when(outer)(over.start)

        def push(self, k):
            shard = self.view(flip(d, 2 * k))
            if k == 3:
                self.start_far()
                self.straight, self.relay = self.far_copies()
            elif k == 2:

                @pl.when(inner)
                def _():
                    self.relay.wait_recv()
                    shard[...] = (shard[...].astype(F32) + self.landing[3].astype(F32)).astype(BF16)

                self.z[2] = send(shard, self.landing.at[1], z_peer[4])
            else:
                self.z[1] = send(shard, self.landing.at[0], z_peer[2])

        def total_into(self, out):
            self.z[1].wait_recv()
            self.z[2].wait_recv()
            out[...] = (
                self.view(d)[...].astype(F32)
                + self.landing[0].astype(F32)
                + self.landing[1].astype(F32)
            ).astype(out.dtype)

            @pl.when(inner)
            def _():
                self.straight.wait_recv()
                out[...] = (out[...].astype(F32) + self.landing[2].astype(F32)).astype(out.dtype)

        def settle(self):
            pl.when(inner)(self.straight.wait_send)
            pl.when(outer)(self.relay.wait_send)

    class Scatter(AlongZ):
        def __init__(self, view, from_x, landing):
            super().__init__(view, landing)
            self.from_x = from_x
            self.x = {}

        def ship(self, k):
            self.x[k] = send(self.view(flip(d, 2 * k + 1)), self.from_x.at[k], xnb)

        def ship_as_made(self, make, also=None):
            numbers = [number() for _ in range(4)]

            def copy_of(k, shard):
                at = numbers[0] + k
                return describe(self.view(shard), self.from_x.at[k], xnb, at, at)

            def step(n, carry):
                k = (7 - 2 * n + n // 2) % 4
                pair = mixed(z, k)
                make(rows(pair))
                copy_of(k, 2 * pair + 1 - lax.rem(d, 2)).start()
                if also is not None:
                    pl.when(n == 0)(also)
                return carry

            lax.fori_loop(0, 4, step, 0)
            for k in range(4):
                self.x[k] = copy_of(k, flip(d, 2 * k + 1))
                issued.append(self.x[k])

        def fold(self, k):
            self.x[k].wait_recv()
            own = self.view(flip(d, 2 * k))
            own[...] = (own[...].astype(F32) + self.from_x[k].astype(F32)).astype(BF16)
            if k in (1, 3):
                self.push(k)

    def weight_grad(left, right, out, scatter, also=None):
        def make(at):
            out[at, :] = tn(left[:, at], right[...]).astype(BF16)

        scatter.ship_as_made(make, also)

    def make_hidden(r):
        at = block(r)
        d_inner_f32[...] = nn(db[at, :], wd[...])

        def inner_step(c, carry):
            here = rows(c, CH)
            where = pl.ds(pl.multiple_of(r * 256 + c * CH, CH), CH)
            d_inner = d_inner_f32[here, :]
            u_raw = ur[where, :].astype(F32)
            g_raw = gr[where, :].astype(F32)
            gate = g_raw * gain_v
            sig = 1.0 / (1.0 + jnp.exp(-gate))
            up = u_raw * gain_u
            d_up = d_inner * (gate * sig)
            d_gate = d_inner * up * (sig * (1.0 + gate * (1.0 - sig)))
            add_stat(6, d_up * u_raw)
            add_stat(7, d_gate * g_raw)
            ur[where, :] = (d_up * gain_u).astype(BF16)
            gr[where, :] = (d_gate * gain_v).astype(BF16)
            return carry

        lax.fori_loop(0, 256 // CH, inner_step, 0)
        part[at, :] = (nt(ur[at, :], wu[...]) + nt(gr[at, :], wg[...])).astype(BF16)

    forward_sends = len(issued)
    sum_h = Reduce(1, sum_m, make_hidden)
    for copy in db_rows.core[:4]:
        copy.wait_recv()
    sum_h.step(1)
    db_rows.relay(0)
    db_rows.relay(1)
    sum_h.step(0)
    db_rows.relay(2)
    db_rows.relay(3)
    for copy in db_rows.core[4:]:
        copy.wait_recv()
    half = slice(0, 512), slice(512, 1024)

    def down_pair(index):
        return gd.at[rows(lax.div(index, 2)), half[0]]

    def down_shard(index):
        return gd.at[rows(index, 128), half[1]]

    sum_down = AlongZ(down_pair, z_down)
    sum_down_x = Scatter(down_shard, x_down_x, z_down_x)

    weight_grad(db, inn, gd, sum_down_x, sum_down.start_far)
    sum_down.straight, sum_down.relay = sum_down.far_copies()
    sum_h.run((3, 2))

    gu, gg, go = wd, wu, wg
    for gather in (take_down, take_up, take_gate):
        gather.release()
    sum_up = Scatter(rows_of(gu), x_up, z_up)
    sum_gate = Scatter(rows_of(gg), x_gate, z_gate)
    weight_grad(h1, ur, gu, sum_up)
    sum_down.push(2)
    sum_down.push(1)
    weight_grad(h1, gr, gg, sum_gate)
    sum_down_x.fold(3)
    sum_down_x.fold(1)

    def mid_step(c, carry):
        at = rows(c, CH)
        x, _, fa, ha, f1, hidden = first_norm(at)
        d_hidden = (1.0 - mix_m) * dr2[at, :] + sum_h.at(at)
        grad = f1 * (d_hidden - hidden * mean_rows(d_hidden * hidden))
        dr1[at, :] = grad
        add_stat(0, grad * (ha - x))
        c_a = mix_a * grad
        dba[at, :] = (fa * (c_a - ha * mean_rows(c_a * ha))).astype(BF16)
        return carry

    sum_h.copies[1].wait_recv()
    for c in range(4):
        sum_h.copies[2][c].wait_recv()
        lax.fori_loop(c * (64 // CH), (c + 1) * (64 // CH), mid_step, 0)

    dat_sends = []
    for r in (2, 3, 1, 0):
        slot = flip(t, r)
        weight = wo[pl.ds(2 * slot, 2)].reshape(256, 1024)
        value = nt(dba[...], weight).astype(BF16)
        if r:
            dat[r - 1] = value
            dat_sends.append(send(dat.at[r - 1], dao.at[block(r)], tensor_peer[r]))
        else:
            dao[block(0), :] = value
    for slot in range(4):
        g = tn(ato[slot], dba[...]).astype(BF16)
        for q in range(8):
            start = (q % 4) * 256 + (2 * slot + q // 4) * 32
            go[start : start + 32, :] = g[q * 32 : (q + 1) * 32, :]

    def go_rows(r):
        return rows(flip(t, r))

    go_core3 = send(go.at[go_rows(3)], o_core3, core)
    go_core1 = send(go.at[go_rows(1)], o_core1, core)
    sum_down_x.fold(2)
    sum_down_x.push(2)
    sum_down_x.fold(0)
    sum_up.fold(3)
    sum_up.fold(1)
    go_core3.wait_recv()
    go[go_rows(2), :] = (go[go_rows(2), :].astype(F32) + o_core3[...].astype(F32)).astype(BF16)
    go_y = send(go.at[go_rows(2)], o_y, ynb)

    head_rows = jnp.where(
        lax.broadcasted_iota(jnp.int32, (8, 256), 0)
        == lax.div(lax.broadcasted_iota(jnp.int32, (8, 256), 1), HEAD_DIM),
        1.0,
        0.0,
    ).astype(BF16)
    for copy in att_sends:
        sent(copy)

    def ready_step(r, carry):
        at = rows(r)
        scaled = (dao[at, :].astype(F32) * linv[at, :]).astype(BF16)
        dao[at, :] = scaled
        product = scaled.astype(F32) * att[at, :].astype(F32)
        high = product.astype(BF16)
        low = (product - high.astype(F32)).astype(BF16)
        delta[r] = nt(head_rows, high) + nt(head_rows, low)
        return carry

    key_grads, query_grads = branch, hid
    seen = jnp.concatenate([row_id <= col_id] * 2, axis=1)

    def lanes_of(r, half=0):
        return pl.ds(pl.multiple_of(r * 128 + half * 512, 128), 128)

    def attend_back(pair, query_r, key_r, visible):
        query_at, key_at = rows(query_r), rows(key_r)
        q = two_heads(qkv[pair, query_at, 0:128])
        do = two_heads(dao[query_at, pair * 128 : pair * 128 + 128])
        keys = qkv[pair, key_at, 128:256]
        e = visible(jnp.exp2(nt(keys, q) * exp_scale))
        d_prob = nt(qkv[pair, key_at, 256:384], do)
        shift = jnp.concatenate(
            [delta[query_r, 2 * pair + h : 2 * pair + h + 1, :] for h in range(2)], axis=1
        )
        d_score = (e * (d_prob - shift)).astype(BF16)
        key_grads[:, lanes_of(key_r)] += nn(d_score, q)
        key_grads[:, lanes_of(key_r, 1)] += nn(e.astype(BF16), do)
        query_grads[:, lanes_of(query_r)] += one_of_two(tn(d_score, keys))

    def diagonal(pair):
        def diagonal_step(r, carry):
            attend_back(pair, r, r, lambda e: jnp.where(seen, e, 0.0))
            return carry

        return diagonal_step

    def below(pair):
        def below_step(n, carry):
            i = 1 + lax.div(n, 3) + lax.div(n + 4, 5)
            j = n - lax.div(i * (i - 1), 2)
            apart = (lax.div(i, 2) - lax.div(j, 2)).astype(F32)
            factor = 1.0 - apart + apart * whole
            attend_back(pair, mixed(i, t), mixed(j, t), lambda e: e * factor)
            return carry

        return below_step

    def clear():
        key_grads[...] = jnp.zeros_like(key_grads)
        query_grads[...] = jnp.zeros_like(query_grads)

    def qkv_back(pair):
        scale = math.sqrt(HEAD_DIM)
        gain = gain_pair(pair)
        column = pl.ds(pl.multiple_of(t * 256 + pair * 128, 128), 128)

        def back_qkv_step(r, carry):
            at = rows(r)
            y = raw[pair, at, :]
            factor = lax.rsqrt(head_sum(y * y) + EPSILON)
            w = y * factor
            grad = (
                jnp.concatenate([query_grads[:, lanes_of(r)], key_grads[:, lanes_of(r)]], axis=1)
                * scale
            )
            both = jnp.sum(grad * w, axis=0, keepdims=True)
            stats[2:3, column] = stats[2:3, column] + both[:, :128] + both[:, 128:]
            c = grad * gain
            dqkv[pair, at, :256] = (factor * (c - w * head_sum(c * w))).astype(BF16)
            dqkv[pair, at, 256:] = key_grads[:, lanes_of(r, 1)].astype(BF16)
            return carry

        lax.fori_loop(0, 4, back_qkv_step, 0)

    gq = qkv

    def qkv_shard(pair):
        return lambda index: gq.at[pair, rows(index, 128), :]

    sum_qkv = [Scatter(qkv_shard(pair), x_qkv.at[pair], z_qkv.at[pair]) for pair in range(2)]

    def qkv_weight(pair):
        def make(at):
            gq[pair, at, :] = tn(tok[:, at], dqkv[pair]).astype(BF16)

        sum_qkv[pair].ship_as_made(make)

    clear()
    dat_sends[2].wait_recv()
    lax.fori_loop(0, 2, ready_step, 0)
    lax.fori_loop(0, 2, diagonal(0), 0)
    sum_up.fold(2)
    dat_sends[0].wait_recv()
    dat_sends[1].wait_recv()
    lax.fori_loop(2, 4, ready_step, 0)
    lax.fori_loop(2, 4, diagonal(0), 0)
    sum_up.push(2)
    sum_up.fold(0)
    lax.fori_loop(0, 6, below(0), 0)
    qkv_back(0)
    qkv_weight(0)
    clear()
    go_core1.wait_recv()
    go_y.wait_recv()
    osum[...] = (
        go[go_rows(0), :].astype(F32) + o_core1[...].astype(F32) + o_y[...].astype(F32)
    ).astype(BF16)
    sum_out = Scatter(rows_of(osum, 32), x_out, z_out)
    for k in (3, 1, 2, 0):
        sum_out.ship(k)
    sum_gate.fold(3)
    sum_gate.fold(1)
    lax.fori_loop(0, 4, diagonal(1), 0)
    sum_gate.fold(2)
    sum_gate.push(2)
    lax.fori_loop(0, 6, below(1), 0)
    qkv_back(1)
    qkv_weight(1)
    sum_gate.fold(0)
    sum_down.total_into(down_pair(d))
    down_x = send(gd.at[rows(flip(d, 1), 128), half[0]], x_down, xnb)

    small_back = [send(stats, s_tensor.at[r - 1], tensor_peer[r]) for r in (1, 2, 3)]

    def make_tokens(r):
        part[block(r), :] = (
            nt(dqkv[0, block(r), :], wq[0]) + nt(dqkv[1, block(r), :], wq[1])
        ).astype(BF16)

    sum_t = Reduce(2, sum_h, make_tokens)
    sum_t.run((3, 2))
    for k in (3, 1, 0, 2):
        sum_qkv[0].fold(k)
    sum_t.run((1, 0))
    sum_qkv[0].push(2)
    for k in (3, 1, 2, 0):
        sum_out.fold(k)
    sum_out.push(2)
    for copy in small_back:
        copy.wait_recv()
    over_tensor = s_tensor[0] + s_tensor[1] + s_tensor[2]
    shared = lax.broadcasted_iota(jnp.int32, (8, 1024), 0) < 6
    s_x[0] = stats[...] + jnp.where(shared, over_tensor, 0.0)
    stat_x = send(s_x.at[0], s_x.at[1], xnb)
    for k in (3, 1, 0, 2):
        sum_qkv[1].fold(k)
    sum_qkv[1].push(2)

    outgoing = []

    def put(src, dst):
        outgoing.append(bring(src, dst))

    put(layer_out, layer_hbm)
    for gather in (take_qkv, take_small, take_out):
        gather.release()
    for copy in issued[:forward_sends]:
        sent(copy)
    down_x.wait_recv()
    grad_down[:, half[0]] = gd[rows(d, 128), half[0]].astype(F32) + x_down[...].astype(F32)
    sum_down_x.total_into(grad_down.at[:, half[1]])
    put(grad_down, down_hbm)
    sum_up.total_into(grad_up)
    put(grad_up, up_hbm)
    sum_gate.total_into(grad_gate)
    put(grad_gate, gate_hbm)
    sum_out.total_into(grad_out)
    put(grad_out, out_hbm)
    stat_x.wait_recv()
    s_z[0] = s_x[0] + s_x[1]
    stat_z = [send(s_z.at[0], s_z.at[k], z_peer[2 * k]) for k in (1, 2, 3)]
    for pair in range(2):
        sum_qkv[pair].total_into(q_sum.at[pair])
    q_low[...] = q_sum[...].astype(BF16)
    q_sends = [
        send(q_low.at[:, rows(flip(t, r), 32), :], q_piece.at[t], tensor_peer[r]) for r in (2, 3, 1)
    ]
    q_piece[t] = q_low[:, rows(t, 32), :]
    sum_t.finish()

    def last_step(c, carry):
        at = rows(c, CH)
        grad_tokens[at, :] = ((1.0 - mix_a) * dr1[at, :] + sum_t.at(at)).astype(BF16)
        return carry

    lax.fori_loop(0, 256 // CH, last_step, 0)
    put(grad_tokens, tokens_hbm)
    for copy in stat_z:
        copy.wait_recv()
    stats_sum[...] = s_z[0] + s_z[1] + s_z[2] + s_z[3]
    put(stats_sum, stats_hbm)
    for copy in q_sends:
        copy.wait_recv()
    for slot in range(4):
        for pair, j in parts_of_qkv:
            start = j * 1024 + slot * 256 + pair * 128
            grad_qkv[:, start : start + 128] = q_piece[
                slot, pair, :, j * 128 : j * 128 + 128
            ].astype(F32)
    put(grad_qkv, qkv_hbm)
    for scatter in (sum_down, sum_down_x, sum_up, sum_gate, sum_out, *sum_qkv):
        scatter.settle()
    for copy in issued:
        sent(copy)
    for copy in outgoing:
        copy.wait()


def finish_kernel(entries, *refs):
    taken, given, held, sems = refs[:8], refs[8:21], refs[21:35], refs[35]
    pull = [pltpu.make_async_copy(taken[i], held[i], sems.at[i]) for i in range(8)]
    push = [
        pltpu.make_async_copy(held[i if i < 7 else i + 1], given[i], sems.at[8 + i])
        for i in range(13)
    ]
    for copy in (pull[7], *pull[:7]):
        copy.start()
    stats, outs = held[7], held[8:]
    s_qk, alpha_a, alpha_m, s_u, s_v, stream = outs
    index = lax.axis_index("dp") * lax.axis_size("tensor") + lax.axis_index("tensor")
    piece = s_qk.shape[0]
    pick = lax.broadcasted_iota(jnp.int32, (1024, piece), 0) == (
        lax.broadcasted_iota(jnp.int32, (1024, piece), 1) + index * piece
    )
    pull[7].wait()
    own = lax.dot_general(
        stats[0:3, :],
        jnp.where(pick, 1.0, 0.0),
        (((1,), (0,)), ((), ())),
        precision=lax.Precision.HIGHEST,
        preferred_element_type=F32,
    )
    for ref, row in ((alpha_a, 0), (alpha_m, 1), (s_qk, 2)):
        ref[...] = own[row]
    s_u[...] = stats[6, :]
    s_v[...] = stats[7, :]
    stream[...] = jnp.sqrt(jnp.sum(stats[3:6, :], axis=1) / entries)
    for copy in push[7:]:
        copy.start()
    for i in range(7):
        pull[i].wait()
        push[i].start()
    for copy in push:
        copy.wait()


def fits(mesh):
    return dict(mesh.shape) == {"dp": 8, "tensor": 4}


def fused(
    tokens, cotangent, bucket_start, w_qkv, w_out, s_qk, alpha_a, alpha_m, w_up, w_gate, w_down, s_u, s_v
):
    n_rows, width = tokens.shape
    piece = s_qk.shape[0]
    vmem = pl.BlockSpec(memory_space=pltpu.VMEM)
    smem = pl.BlockSpec(memory_space=pltpu.SMEM)
    hbm = pl.BlockSpec(memory_space=pl.ANY)
    bf = lambda *shape: pltpu.VMEM(shape, BF16)
    fl = lambda *shape: pltpu.VMEM(shape, F32)
    large = [
        jax.ShapeDtypeStruct(shape, kind)
        for shape, kind in (
            ((256, 1024), BF16), ((256, 1024), BF16), ((32, 3072), F32), ((32, 1024), F32),
            ((128, 1024), F32), ((128, 1024), F32), ((128, 1024), F32),
        )
    ]
    scratch = [
        *[pltpu.VMEM(leaf.shape, leaf.dtype) for leaf in large], fl(8, 1024),
        bf(1024, 1024), bf(256, 1024), bf(2, 1024, 384), bf(8, 4, 32, 1024), bf(1024, 1024),
        bf(1024, 1024), bf(1024, 1024), bf(16, 128), bf(3, 16, 128), bf(16, 1024), fl(16, 1024),
        fl(2, 1024, 256), bf(2, 1024, 384), fl(1024, 256), bf(1024, 256), bf(4, 256, 256),
        fl(256, 1024), fl(256, 1024), bf(1024, 1024), bf(1024, 1024), bf(1024, 1024), bf(1024, 1024),
        bf(1024, 1024), bf(3, 256, 1024), bf(3, 256, 1024), bf(3, 256, 1024),
        fl(256, 1024), fl(256, 1024), fl(256, 1024), bf(1024, 1024), bf(256, 1024), bf(3, 256, 256),
        bf(1024, 256), bf(2, 1024, 384), fl(4, 8, 256),
        bf(1024, 1024), bf(128, 512), bf(4, 128, 512), bf(4, 128, 1024), bf(4, 128, 1024),
        bf(2, 4, 128, 384), bf(4, 32, 1024), bf(4, 256, 512), bf(4, 128, 512), bf(4, 128, 1024), bf(4, 128, 1024), bf(2, 4, 128, 384),
        bf(4, 32, 1024), bf(256, 1024), bf(256, 1024), bf(256, 1024), bf(256, 1024),
        fl(2, 128, 384), bf(2, 128, 384), bf(4, 2, 32, 384), fl(8, 1024), fl(3, 8, 1024), fl(2, 8, 1024), fl(4, 8, 1024),
        pltpu.SemaphoreType.DMA((COPIES,)), pltpu.SemaphoreType.DMA((COPIES,)),
        pltpu.SemaphoreType.DMA((32,)),
    ]
    *big, stats = pl.pallas_call(
        fused_kernel,
        out_shape=[*large, jax.ShapeDtypeStruct((8, 1024), F32)],
        in_specs=[hbm, hbm, smem, hbm, hbm, vmem, vmem, vmem, hbm, hbm, hbm, vmem, vmem],
        out_specs=[hbm] * 8,
        scratch_shapes=scratch,
        compiler_params=pltpu.CompilerParams(
            collective_id=0, has_side_effects=True, vmem_limit_bytes=VMEM_BYTES
        ),
        cost_estimate=pl.CostEstimate(
            flops=27_000_000_000, bytes_accessed=8_000_000, transcendentals=10_000_000
        ),
    )(
        tokens, cotangent, bucket_start, w_qkv, w_out, s_qk, alpha_a, alpha_m,
        w_up, w_gate, w_down, s_u, s_v,
    )
    entries = n_rows * width * lax.axis_size("dp") * lax.axis_size("tensor")
    flat = [(piece,), (piece,), (piece,), (1024,), (1024,), (3,)]
    *big, g_qk, g_a, g_m, g_u, g_v, stream = pl.pallas_call(
        functools.partial(finish_kernel, float(entries)),
        out_shape=[*large, *[jax.ShapeDtypeStruct(shape, F32) for shape in flat]],
        in_specs=[hbm] * 8,
        out_specs=[hbm] * 13,
        scratch_shapes=[
            *[pltpu.VMEM(leaf.shape, leaf.dtype) for leaf in large],
            fl(8, 1024),
            *[fl(*shape) for shape in flat],
            pltpu.SemaphoreType.DMA((21,)),
        ],
    )(*big, stats)
    return (*big[:4], g_qk, g_a, g_m, *big[4:], g_u, g_v, stream)


def solution(mesh):
    body = fused if fits(mesh) else local
    return jax.shard_map(
        body,
        mesh=mesh,
        in_specs=(
            P(("dp", "tensor"), None),
            P(("dp", "tensor"), None),
            P(),
            P(("dp", "tensor"), None),
            P(("dp", "tensor"), None),
            P(("dp", "tensor")),
            P(("dp", "tensor")),
            P(("dp", "tensor")),
            P("dp", "tensor"),
            P("dp", "tensor"),
            P("dp", "tensor"),
            P("tensor"),
            P("tensor"),
        ),
        out_specs=(
            P(("dp", "tensor"), None),
            P(("dp", "tensor"), None),
            P(("dp", "tensor"), None),
            P(("dp", "tensor"), None),
            P(("dp", "tensor")),
            P(("dp", "tensor")),
            P(("dp", "tensor")),
            P("dp", "tensor"),
            P("dp", "tensor"),
            P("dp", "tensor"),
            P("tensor"),
            P("tensor"),
            P(),
        ),
        check_vma=False,
    )
```

```python
import functools
import math

import jax
import jax.numpy as jnp
from jax import lax
from jax.experimental import pallas as pl
from jax.experimental.pallas import tpu as pltpu
from jax.sharding import PartitionSpec as P

HEAD_DIM = 64


EPSILON = 1e-06
MASKED_SCORE = -1e30


def rms_rows(value):
    return value * lax.rsqrt(jnp.mean(value * value, axis=-1, keepdims=True) + EPSILON)


def rms_back(upstream, normed, source):
    factor = lax.rsqrt(jnp.mean(source * source, axis=-1, keepdims=True) + EPSILON)
    return factor * (upstream - normed * jnp.mean(upstream * normed, axis=-1, keepdims=True))


def unit_heads(value):
    shaped = value.reshape(value.shape[0], -1, HEAD_DIM)
    factor = lax.rsqrt(jnp.sum(shaped * shaped, axis=-1, keepdims=True) + EPSILON)
    return ((shaped * factor).reshape(value.shape), factor)


def unit_back(upstream, normed, factor):
    upper_grad = upstream.reshape(normed.shape[0], -1, HEAD_DIM)
    normed_heads = normed.reshape(normed.shape[0], -1, HEAD_DIM)
    result = factor * (
        upper_grad - normed_heads * jnp.sum(upper_grad * normed_heads, axis=-1, keepdims=True)
    )
    return result.reshape(upstream.shape)


def block_span(total_rows, row_count):
    units = total_rows // row_count
    block_units = max(1, min(units, 512 // row_count))
    while units % block_units:
        block_units -= 1
    return row_count * block_units


def local(
    tokens,
    cotangent,
    bucket_start,
    w_qkv,
    w_out,
    s_qk,
    alpha_a,
    alpha_m,
    w_up,
    w_gate,
    w_down,
    s_u,
    s_v,
):
    row_count, model_width = tokens.shape
    head_count = model_width // HEAD_DIM
    score_scale = math.sqrt(HEAD_DIM)
    spread = lax.axis_size("tensor")
    group_rows = spread * row_count
    tensor_slot = lax.axis_index("tensor")
    qkv_full, out_full, gain_qk, mix_attn, mix_mlp = (
        lax.all_gather(w_qkv, ("dp", "tensor"), axis=0, tiled=True),
        lax.all_gather(w_out, ("dp", "tensor"), axis=0, tiled=True),
        lax.all_gather(s_qk, ("dp", "tensor"), axis=0, tiled=True),
        lax.all_gather(alpha_a, ("dp", "tensor"), axis=0, tiled=True),
        lax.all_gather(alpha_m, ("dp", "tensor"), axis=0, tiled=True),
    )
    up_full, gate_full, down_full = (
        lax.all_gather(w_up, "dp", axis=0, tiled=True),
        lax.all_gather(w_gate, "dp", axis=0, tiled=True),
        lax.all_gather(w_down, "dp", axis=0, tiled=True),
    )
    gain_qk = gain_qk.astype(jnp.float32)
    mix_attn = mix_attn.astype(jnp.float32)
    mix_mlp = mix_mlp.astype(jnp.float32)
    scale_up = s_u.astype(jnp.float32)
    scale_gate = s_v.astype(jnp.float32)
    starts = lax.dynamic_slice_in_dim(bucket_start, lax.axis_index("dp") * spread, spread)
    key_seq = jnp.repeat(starts, row_count)
    own_seq = starts[tensor_slot]
    query_pos = tensor_slot * row_count + jnp.arange(row_count, dtype=jnp.int32)

    def allowed(key_start, key_count):
        key_pos = key_start + jnp.arange(key_count, dtype=jnp.int32)
        seq_part = lax.dynamic_slice_in_dim(key_seq, key_start, key_count)
        return (key_pos[None, :] <= query_pos[:, None]) & (seq_part[None, :] == own_seq)

    inputs = tokens.astype(jnp.float32)
    qkv = jnp.dot(tokens, qkv_full, preferred_element_type=jnp.float32)
    q_unit, q_factor = unit_heads(qkv[:, :model_width])
    k_unit, k_factor = unit_heads(qkv[:, model_width : 2 * model_width])
    query_low = (q_unit * gain_qk).astype(jnp.bfloat16)
    keys_low = (k_unit * gain_qk).astype(jnp.bfloat16)
    values_low = qkv[:, 2 * model_width :].astype(jnp.bfloat16)
    query_heads = query_low.reshape(row_count, head_count, HEAD_DIM)
    key_all, value_all = (
        lax.all_gather(keys_low, "tensor", axis=0, tiled=True),
        lax.all_gather(values_low, "tensor", axis=0, tiled=True),
    )
    key_block = block_span(group_rows, row_count)
    blocks = group_rows // key_block

    def block_scores(key_source, key_start, key_count):
        key_part = lax.dynamic_slice_in_dim(key_source, key_start, key_count).reshape(
            key_count, head_count, HEAD_DIM
        )
        return (
            jnp.einsum("qhd,khd->hqk", query_heads, key_part, preferred_element_type=jnp.float32)
            * score_scale
        )

    def stat_step(state_pair, block_index):
        row_top, row_total = state_pair
        key_start = block_index * key_block
        allowed_keys = allowed(key_start, key_block)[None]
        masked = jnp.where(allowed_keys, block_scores(key_all, key_start, key_block), MASKED_SCORE)
        new_top = jnp.maximum(row_top, jnp.max(masked, axis=-1))
        fresh = jnp.where(allowed_keys, jnp.exp(masked - new_top[..., None]), 0.0)
        row_total = row_total * jnp.exp(row_top - new_top) + jnp.sum(fresh, axis=-1)
        return ((new_top, row_total), None)

    start_state = (
        jnp.full((head_count, row_count), MASKED_SCORE, jnp.float32),
        jnp.zeros((head_count, row_count), jnp.float32),
    )
    (row_top, row_total), _ = lax.scan(stat_step, start_state, jnp.arange(blocks))
    log_total = row_top + jnp.log(row_total)

    def probs_for(key_source, key_start, key_count):
        scores = block_scores(key_source, key_start, key_count)
        allowed_keys = allowed(key_start, key_count)[None]
        return jnp.where(allowed_keys, jnp.exp(scores - log_total[..., None]), 0.0)

    def value_part(value_source, key_start, key_count):
        return lax.dynamic_slice_in_dim(value_source, key_start, key_count).reshape(
            key_count, head_count, HEAD_DIM
        )

    def out_step(carry_sum, block_index):
        key_start = block_index * key_block
        attn_probs = probs_for(key_all, key_start, key_block).astype(jnp.bfloat16)
        term = jnp.einsum(
            "hqk,khd->qhd",
            attn_probs,
            value_part(value_all, key_start, key_block),
            preferred_element_type=jnp.float32,
        )
        return (carry_sum + term, None)

    attended, _ = lax.scan(
        out_step, jnp.zeros((row_count, head_count, HEAD_DIM), jnp.float32), jnp.arange(blocks)
    )
    attended_low = attended.reshape(row_count, model_width).astype(jnp.bfloat16)
    branch_a = jnp.dot(attended_low, out_full, preferred_element_type=jnp.float32)
    h_attn = rms_rows(branch_a)
    resid_one = inputs + mix_attn * (h_attn - inputs)
    hidden_one = rms_rows(resid_one)
    hidden_low = hidden_one.astype(jnp.bfloat16)
    rows_all = lax.all_gather(hidden_low, "tensor", axis=0, tiled=True)
    up_raw = jnp.dot(rows_all, up_full, preferred_element_type=jnp.float32)
    gate_raw = jnp.dot(rows_all, gate_full, preferred_element_type=jnp.float32)
    up_scaled = up_raw * scale_up
    gate_scaled = gate_raw * scale_gate
    gate_sigmoid = jax.nn.sigmoid(gate_scaled)
    silu_gate = gate_scaled * gate_sigmoid
    inner_low = (up_scaled * silu_gate).astype(jnp.bfloat16)
    branch_m = lax.psum_scatter(
        jnp.einsum("tf,df->td", inner_low, down_full, preferred_element_type=jnp.float32).astype(
            jnp.bfloat16
        ),
        "tensor",
        scatter_dimension=0,
        tiled=True,
    ).astype(jnp.float32)
    h_mlp = rms_rows(branch_m)
    resid_two = hidden_one + mix_mlp * (h_mlp - hidden_one)
    result = rms_rows(resid_two)
    partial_stats = jnp.stack(
        [jnp.sum(branch_a * branch_a), jnp.sum(branch_m * branch_m), jnp.sum(resid_two * resid_two)]
    )
    upstream = cotangent.astype(jnp.float32)
    d_resid_two = rms_back(upstream, result, resid_two)
    grad_mix_mlp = jnp.sum(d_resid_two * (h_mlp - hidden_one), axis=0)
    d_branch_m = rms_back(mix_mlp * d_resid_two, h_mlp, branch_m).astype(jnp.bfloat16)
    grads_all = lax.all_gather(d_branch_m, "tensor", axis=0, tiled=True)
    d_inner = jnp.dot(grads_all, down_full, preferred_element_type=jnp.float32)
    grad_up_scaled = d_inner * silu_gate
    grad_gate_scaled = (
        d_inner * up_scaled * gate_sigmoid * (1.0 + gate_scaled * (1.0 - gate_sigmoid))
    )
    grad_scale_up = jnp.sum(grad_up_scaled * up_raw, axis=0)
    grad_scale_gate = jnp.sum(grad_gate_scaled * gate_raw, axis=0)
    up_grad_low = (grad_up_scaled * scale_up).astype(jnp.bfloat16)
    gate_grad_low = (grad_gate_scaled * scale_gate).astype(jnp.bfloat16)
    grad_down = jnp.einsum("td,tf->df", grads_all, inner_low, preferred_element_type=jnp.float32)
    grad_up = jnp.einsum("td,tf->df", rows_all, up_grad_low, preferred_element_type=jnp.float32)
    grad_gate = jnp.einsum("td,tf->df", rows_all, gate_grad_low, preferred_element_type=jnp.float32)
    first = jnp.einsum("tf,df->td", up_grad_low, up_full, preferred_element_type=jnp.float32)
    d_hidden_one = (1.0 - mix_mlp) * d_resid_two + lax.psum_scatter(
        (
            first
            + jnp.einsum("tf,df->td", gate_grad_low, gate_full, preferred_element_type=jnp.float32)
        ).astype(jnp.bfloat16),
        "tensor",
        scatter_dimension=0,
        tiled=True,
    ).astype(jnp.float32)
    d_resid_one = rms_back(d_hidden_one, hidden_one, resid_one)
    grad_mix_attn = jnp.sum(d_resid_one * (h_attn - inputs), axis=0)
    d_branch_a = rms_back(mix_attn * d_resid_one, h_attn, branch_a).astype(jnp.bfloat16)
    grad_out = jnp.einsum("tc,td->cd", attended_low, d_branch_a, preferred_element_type=jnp.float32)
    d_attended = jnp.einsum(
        "td,cd->tc", d_branch_a, out_full, preferred_element_type=jnp.float32
    ).astype(jnp.bfloat16)
    d_heads = d_attended.reshape(row_count, head_count, HEAD_DIM)
    row_delta = jnp.sum(d_heads.astype(jnp.float32) * attended, axis=-1).T
    key_back, value_back = (
        lax.all_gather(keys_low, "tensor", axis=0, tiled=True),
        lax.all_gather(values_low, "tensor", axis=0, tiled=True),
    )

    def score_grads(key_start, key_count):
        attn_probs = probs_for(key_back, key_start, key_count)
        d_probs = jnp.einsum(
            "qhd,khd->hqk",
            d_heads,
            value_part(value_back, key_start, key_count),
            preferred_element_type=jnp.float32,
        )
        d_scores = (attn_probs * (d_probs - row_delta[..., None])).astype(jnp.bfloat16)
        return (attn_probs, d_scores)

    def query_step(carry_sum, block_index):
        key_start = block_index * key_block
        attn_probs, d_scores = score_grads(key_start, key_block)
        key_part = lax.dynamic_slice_in_dim(key_back, key_start, key_block).reshape(
            key_block, head_count, HEAD_DIM
        )
        return (
            carry_sum
            + jnp.einsum("hqk,khd->qhd", d_scores, key_part, preferred_element_type=jnp.float32),
            None,
        )

    d_query, _ = lax.scan(
        query_step, jnp.zeros((row_count, head_count, HEAD_DIM), jnp.float32), jnp.arange(blocks)
    )
    d_query = d_query.reshape(row_count, model_width) * score_scale
    part_rows = lax.axis_size("tensor") * row_count
    sub_block = block_span(part_rows, row_count)

    def one_block(block_index):
        begin = block_index * sub_block
        attn_probs, d_scores = score_grads(begin, sub_block)
        d_keys = (
            jnp.einsum("hqk,qhd->khd", d_scores, query_heads, preferred_element_type=jnp.float32)
            * score_scale
        )
        d_values = jnp.einsum(
            "hqk,qhd->khd",
            attn_probs.astype(jnp.bfloat16),
            d_heads,
            preferred_element_type=jnp.float32,
        )
        return jnp.concatenate(
            [d_keys.reshape(sub_block, model_width), d_values.reshape(sub_block, model_width)],
            axis=1,
        )

    block_terms = lax.map(one_block, jnp.arange(part_rows // sub_block))
    key_grads = lax.psum_scatter(
        block_terms.reshape(part_rows, 2 * model_width).astype(jnp.bfloat16),
        "tensor",
        scatter_dimension=0,
        tiled=True,
    ).astype(jnp.float32)
    d_keys_own = key_grads[:, :model_width]
    d_values_own = key_grads[:, model_width:]
    grad_gain = jnp.sum(d_query * q_unit + d_keys_own * k_unit, axis=0)
    d_qkv = jnp.concatenate(
        [
            unit_back(d_query * gain_qk, q_unit, q_factor),
            unit_back(d_keys_own * gain_qk, k_unit, k_factor),
            d_values_own,
        ],
        axis=1,
    ).astype(jnp.bfloat16)
    grad_qkv = jnp.einsum("tc,tf->cf", tokens, d_qkv, preferred_element_type=jnp.float32)
    d_tokens = (1.0 - mix_attn) * d_resid_one + jnp.einsum(
        "tf,cf->tc", d_qkv, qkv_full, preferred_element_type=jnp.float32
    )
    sum_qkv, sum_out, sum_gain, sum_mix_attn, sum_mix_mlp = (
        lax.psum_scatter(grad_qkv, ("dp", "tensor"), scatter_dimension=0, tiled=True),
        lax.psum_scatter(grad_out, ("dp", "tensor"), scatter_dimension=0, tiled=True),
        lax.psum_scatter(grad_gain, ("dp", "tensor"), scatter_dimension=0, tiled=True),
        lax.psum_scatter(grad_mix_attn, ("dp", "tensor"), scatter_dimension=0, tiled=True),
        lax.psum_scatter(grad_mix_mlp, ("dp", "tensor"), scatter_dimension=0, tiled=True),
    )
    sum_up, sum_gate, sum_down = (
        lax.psum_scatter(
            grad_up.astype(jnp.bfloat16), "dp", scatter_dimension=0, tiled=True
        ).astype(jnp.float32),
        lax.psum_scatter(
            grad_gate.astype(jnp.bfloat16), "dp", scatter_dimension=0, tiled=True
        ).astype(jnp.float32),
        lax.psum_scatter(
            grad_down.astype(jnp.bfloat16), "dp", scatter_dimension=0, tiled=True
        ).astype(jnp.float32),
    )
    sum_scale_up, sum_scale_gate = lax.psum((grad_scale_up, grad_scale_gate), "dp")
    stat_sums = lax.psum(partial_stats, ("dp", "tensor"))
    entry_count = row_count * model_width * lax.axis_size("dp") * spread
    stream_rms = jnp.sqrt(stat_sums / entry_count)
    return (
        result.astype(jnp.bfloat16),
        d_tokens.astype(jnp.bfloat16),
        sum_qkv,
        sum_out,
        sum_gain,
        sum_mix_attn,
        sum_mix_mlp,
        sum_up,
        sum_gate,
        sum_down,
        sum_scale_up,
        sum_scale_gate,
        stream_rms,
    )


MESH = pl.DeviceIdType.MESH
BF16 = jnp.bfloat16
F32 = jnp.float32
LOG2E = 1.4426950408889634
COPIES = 224
VMEM_BYTES = 63 * 2**20
CH = 32


def nn(left, right):
    return lax.dot_general(left, right, (((1,), (0,)), ((), ())), preferred_element_type=F32)


def nt(left, right):
    return lax.dot_general(left, right, (((1,), (1,)), ((), ())), preferred_element_type=F32)


def tn(left, right):
    return lax.dot_general(left, right, (((0,), (0,)), ((), ())), preferred_element_type=F32)


def flip(index, bits):
    bit = 1
    while bit <= bits:
        if bits & bit:
            index = index + bit - 2 * bit * lax.rem(lax.div(index, bit), 2)
        bit *= 2
    return index


def mixed(a, b):
    low = lax.rem(a, 2) + lax.rem(b, 2) - 2 * lax.rem(a, 2) * lax.rem(b, 2)
    high_a, high_b = lax.div(a, 2), lax.div(b, 2)
    return low + 2 * (high_a + high_b - 2 * high_a * high_b)


def mean_rows(value):
    return jnp.mean(value, axis=-1, keepdims=True)


def rows(start, count=256):
    return pl.ds(pl.multiple_of(start * count, count), count)


def block(r):
    return pl.ds(r * 256, 256)


def fused_kernel(
    tokens, cotangent, starts_hbm, w_qkv, w_out, s_qk_hbm, alpha_a_hbm, alpha_m_hbm, w_up, w_gate,
    w_down, scale_u_hbm, scale_v_hbm,
    layer_hbm, tokens_hbm, qkv_hbm, out_hbm, up_hbm, gate_hbm, down_hbm, stats_hbm,
    layer_out, grad_tokens, grad_qkv, grad_out, grad_up, grad_gate, grad_down, stats_sum,
    bucket_start, s_qk, alpha_a, alpha_m, scale_u, scale_v,
    tok, cot, wq, wo, wu, wg, wd, small, small_t, small_d, gains,
    raw, qkv, linv, att, ato, branch, hid, h1, ur, gr, inn,
    part, from_core3, from_core1, from_y,
    dr2, dr1, d_inner_f32, db, dba, dat, dao, dqkv, delta,
    gd, x_down, x_down_x, x_up, x_gate, x_qkv, x_out, z_down, z_down_x, z_up, z_gate, z_qkv, z_out,
    o_core3, o_core1, o_y, osum, q_sum, q_low, q_piece, stats, s_tensor, s_x, s_z,
    send_sem, recv_sem, local_sem,
):
    d = lax.axis_index("dp")
    t = lax.axis_index("tensor")
    z = lax.div(d, 2)
    inner = lax.rem(lax.div(z + 1, 2), 2) == 1
    core, ynb, diag = (d, flip(t, 1)), (d, flip(t, 2)), (d, flip(t, 3))
    tensor_peer = {1: core, 2: ynb, 3: diag}
    xnb = (flip(d, 1), t)
    z_peer = {m: (flip(d, m), t) for m in (2, 4, 6)}

    barrier = pltpu.get_barrier_semaphore()
    peers = [core, ynb, diag, xnb] + [z_peer[m] for m in (2, 4, 6)]
    for peer in peers:
        pl.semaphore_signal(barrier, inc=1, device_id=peer, device_id_type=MESH)

    issued = []
    used = [0]

    def number():
        used[0] += 1
        return used[0] - 1

    def describe(src, dst, peer, at, to):
        return pltpu.make_async_remote_copy(
            src_ref=src,
            dst_ref=dst,
            send_sem=send_sem.at[at],
            recv_sem=recv_sem.at[to],
            device_id=peer,
            device_id_type=MESH,
        )

    def send(src, dst, peer):
        at = number()
        copy = describe(src, dst, peer, at, at)
        copy.start()
        issued.append(copy)
        return copy

    waited = set()

    def sent(copy):
        if id(copy) not in waited:
            waited.add(id(copy))
            copy.wait_send()

    locals_ = []

    def bring(src, dst):
        copy = pltpu.make_async_copy(src, dst, local_sem.at[len(locals_)])
        copy.start()
        locals_.append(copy)
        return copy

    outer = jnp.logical_not(inner)

    class Gather:
        def __init__(self, src, view):
            self.src, self.view = src, view
            self.at6, self.relay_at = number(), number()

        def start_x(self):
            self.x = [send(self.src, self.view(d), xnb)]

        def start_far(self):
            self.z = {4: send(self.src, self.view(d), z_peer[4])}
            self.start_straight()

        def start_straight(self):
            self.straight = describe(self.src, self.view(d), z_peer[6], self.at6, self.at6)
            pl.when(inner)(self.straight.start)

        def start_near(self):
            self.z[2] = send(self.src, self.view(d), z_peer[2])

        def start_z(self):
            self.start_far()
            self.start_near()

        def hop(self):
            self.z[4].wait_recv()
            self.hand_on()

        def hand_on(self):
            shard = self.view(flip(d, 4))
            self.relay = describe(shard, shard, z_peer[2], self.relay_at, self.at6)
            pl.when(inner)(self.relay.start)

        def forward_one(self, m):
            if m == 2:
                self.z[2].wait_recv()
            if m == 6:
                self.straight.wait_recv()
            shard = self.view(flip(d, m))
            self.x.append(send(shard, shard, xnb))

        def forward(self):
            self.forward_one(2)
            self.hop()
            self.forward_one(4)
            self.forward_one(6)

        def finish(self):
            for copy in self.x:
                copy.wait_recv()

        def release(self):
            for copy in [*self.z.values(), *self.x]:
                sent(copy)
            for copy in (self.straight, self.relay):
                pl.when(inner)(copy.wait_send)

    class GatherPairs(Gather):
        def __init__(self, src, shard, pair):
            super().__init__(src, pair)
            self.shard = shard

        def start_x(self):
            self.x = [send(self.src, self.shard(d), xnb)]

        def start_far(self):
            self.x[0].wait_recv()
            self.src = self.view(d)
            self.z = {4: send(self.src, self.view(d), z_peer[4])}

        def hop(self):
            self.z[4].wait_recv()
            self.start_straight()
            self.hand_on()

    def rows_of(ref, count=128):
        return lambda index: ref.at[rows(index, count)]

    def pair_of(ref):
        return lambda index: ref.at[rows(lax.div(index, 2))]

    take_qkv = Gather(wq.at[:, rows(d, 128), :], lambda index: wq.at[:, rows(index, 128), :])
    take_small = Gather(small_d.at[:, rows(d, 128)], lambda index: small_d.at[:, rows(index, 128)])
    take_out = Gather(w_out, lambda index: wo.at[index, t])
    take_up = Gather(w_up, rows_of(wu))
    take_gate = Gather(w_gate, rows_of(wg))
    take_down = GatherPairs(w_down, rows_of(wd), pair_of(wd))

    local_small = [
        bring(src, dst)
        for src, dst in (
            (s_qk_hbm, s_qk),
            (alpha_a_hbm, alpha_a),
            (alpha_m_hbm, alpha_m),
            (scale_u_hbm, scale_u),
            (scale_v_hbm, scale_v),
            (starts_hbm, bucket_start),
        )
    ]
    piece = s_qk.shape[0]
    own_qkv = pl.ds(pl.multiple_of(d * 128 + t * 32, 32), 32)

    def qkv_cols(slot, pair, j):
        return pl.ds(pl.multiple_of(j * 1024 + slot * 256 + pair * 128, 128), 128)

    def qkv_place(pair, j):
        return wq.at[pair, own_qkv, j * 128 : j * 128 + 128]

    parts_of_qkv = [(pair, j) for pair in range(2) for j in range(3)]
    local_qkv = [
        bring(w_qkv.at[:, qkv_cols(t, pair, j)], qkv_place(pair, j)) for pair, j in parts_of_qkv
    ]
    local_tok = bring(tokens, tok.at[block(0)])
    local_rest = [
        bring(w_out, wo.at[d, t]),
        bring(w_up, wu.at[rows(d, 128)]),
        bring(w_gate, wg.at[rows(d, 128)]),
        bring(w_down, wd.at[rows(d, 128)]),
        bring(cotangent, cot),
    ]
    place = jnp.where(
        lax.broadcasted_iota(jnp.int32, (piece, 128), 1)
        == lax.broadcasted_iota(jnp.int32, (piece, 128), 0) + t * piece,
        1.0,
        0.0,
    ).astype(BF16)
    small_row = lax.broadcasted_iota(jnp.int32, (16, 128), 0)
    for copy in local_small:
        copy.wait()
    placed = jnp.zeros((16, 128), F32)
    for index, vector in enumerate((s_qk, alpha_a, alpha_m)):
        placed = jnp.where(small_row == index, nn(vector[...].reshape(1, piece), place), placed)
    small[...] = placed.astype(BF16)
    stats[...] = jnp.zeros_like(stats)
    gain_u = scale_u[...].astype(F32).reshape(1, 1024)
    gain_v = scale_v[...].astype(F32).reshape(1, 1024)
    pl.semaphore_wait(barrier, len(peers))

    small_sends = [send(small, small_t.at[r - 1], tensor_peer[r]) for r in (2, 3, 1)]
    qkv_sends = [
        send(w_qkv.at[:, qkv_cols(flip(t, r), pair, j)], qkv_place(pair, j), tensor_peer[r])
        for r in (2, 3, 1)
        for pair, j in parts_of_qkv
    ]
    take_out.start_z()
    take_down.start_x()
    take_out.start_x()
    take_up.start_x()
    for copy in small_sends:
        copy.wait_recv()
    small_d[:, rows(d, 128)] = small[...] + small_t[0] + small_t[1] + small_t[2]
    take_small.start_z()
    take_small.start_x()
    for copy in local_qkv:
        copy.wait()
    for copy in qkv_sends:
        copy.wait_recv()
    take_qkv.start_z()
    take_qkv.start_x()
    tok_y = send(tokens, tok.at[block(2)], ynb)
    tok_core = send(tokens, tok.at[block(1)], core)
    take_up.start_far()

    take_out.hop()
    take_small.hop()
    take_small.forward_one(4)
    take_small.forward_one(2)
    take_qkv.hop()
    take_qkv.forward_one(4)
    take_up.start_near()
    take_qkv.forward_one(2)
    take_small.forward_one(6)
    take_qkv.forward_one(6)
    take_out.forward_one(4)
    take_out.forward_one(2)
    take_out.forward_one(6)
    take_gate.start_far()
    tok_y.wait_recv()
    tok_diag = send(tok.at[block(2)], tok.at[block(3)], core)
    take_small.finish()
    gains[...] = small_d[...].astype(F32)
    take_qkv.finish()
    local_tok.wait()
    tok_core.wait_recv()
    tok_diag.wait_recv()

    def gain_pair(pair):
        gain = gains[0:1, pl.ds(pl.multiple_of(t * 256 + pair * 128, 128), 128)]
        return jnp.concatenate([gain, gain], axis=1)

    first_head = lax.broadcasted_iota(jnp.int32, (256, 128), 1) < HEAD_DIM
    same_head = jnp.where(
        lax.div(lax.broadcasted_iota(jnp.int32, (256, 256), 0), HEAD_DIM)
        == lax.div(lax.broadcasted_iota(jnp.int32, (256, 256), 1), HEAD_DIM),
        1.0,
        0.0,
    ).astype(BF16)

    def head_sum(value):
        high = value.astype(BF16)
        low = (value - high.astype(F32)).astype(BF16)
        return nn(high, same_head) + nn(low, same_head)

    def qkv_step(r, carry):
        at = rows(r)
        x = tok[at, :]
        for pair in range(2):
            y = nn(x, wq[pair])
            qk = y[:, :256]
            raw[pair, at, :] = qk
            factor = lax.rsqrt(head_sum(qk * qk) + EPSILON)
            qkv[pair, at, :256] = (qk * factor * gain_pair(pair)).astype(BF16)
            qkv[pair, at, 256:] = y[:, 256:].astype(BF16)
        return carry

    lax.fori_loop(0, 4, qkv_step, 0)

    take_out.finish()
    local_rest[0].wait()
    wo_y = send(wo.at[:, t], wo.at[:, t], ynb)
    wo_core = send(wo.at[:, t], wo.at[:, t], core)

    def true_rows(i):
        return rows(flip(t, i))

    whole = jnp.where(bucket_start[d * 4] == bucket_start[d * 4 + 2], 1.0, 0.0)
    row_id = lax.broadcasted_iota(jnp.int32, (256, 256), 0)
    col_id = lax.broadcasted_iota(jnp.int32, (256, 256), 1)
    exp_scale = math.sqrt(HEAD_DIM) * LOG2E

    def two_heads(value):
        zero = jnp.zeros_like(value)
        return jnp.concatenate(
            [jnp.where(first_head, value, zero), jnp.where(first_head, zero, value)], axis=0
        )

    def one_of_two(value):
        return jnp.where(first_head, value[:256], value[256:])

    causal = jnp.concatenate([col_id <= row_id] * 2, axis=0)

    def attend(i):
        at = true_rows(i)

        def head_step(pair, carry):
            q = two_heads(qkv[pair, at, 0:128])
            acc = jnp.zeros((512, 128), F32)
            weight = jnp.zeros((512, 1), F32)
            for j in range(i + 1):
                key_at = true_rows(j)
                e = jnp.exp2(nt(q, qkv[pair, key_at, 128:256]) * exp_scale)
                if j == i:
                    e = jnp.where(causal, e, 0.0)
                elif j // 2 != i // 2:
                    e = e * whole
                weight = weight + jnp.sum(e, axis=1, keepdims=True)
                acc = acc + nn(e.astype(BF16), qkv[pair, key_at, 256:384])
            inverse = 1.0 / weight
            lanes = rows(pair, 128)
            linv[at, lanes] = one_of_two(jnp.broadcast_to(inverse, (512, 128)))
            att[at, lanes] = one_of_two(acc * inverse).astype(BF16)
            return carry

        lax.fori_loop(0, 2, head_step, 0)

    attend(0)
    attend(1)
    take_up.hop()
    take_up.forward_one(4)
    take_gate.start_near()
    take_gate.start_x()
    take_up.forward_one(2)
    for copy in local_rest[1:]:
        copy.wait()
    take_down.start_far()
    attend(2)
    attend(3)

    att_sends = [send(att.at[block(r)], ato.at[t], tensor_peer[r]) for r in (2, 3, 1)]
    ato[t] = att[block(0), :]
    wo_y.wait_recv()
    wo_far = send(wo.at[:, flip(t, 2)], wo.at[:, flip(t, 2)], core)
    take_up.forward_one(6)
    for copy in att_sends:
        copy.wait_recv()
    wo_core.wait_recv()
    wo_far.wait_recv()

    def out_rows(slot, columns):
        return wo[2 * slot : 2 * slot + 2, :, :, columns].reshape(256, 256)

    def out_step(n, carry):
        at = rows(n)
        acc = nn(ato[0], out_rows(0, at))
        for slot in range(1, 4):
            acc = acc + nn(ato[slot], out_rows(slot, at))
        branch[:, at] = acc
        return carry

    lax.fori_loop(0, 4, out_step, 0)

    mix_a = gains[1:2, :]
    mix_m = gains[2:3, :]

    def add_stat(row, value):
        stats[row : row + 1, :] = stats[row : row + 1, :] + jnp.sum(value, axis=0, keepdims=True)

    def first_norm(at):
        x = tok[at, :].astype(F32)
        ba = branch[at, :]
        fa = lax.rsqrt(mean_rows(ba * ba) + EPSILON)
        ha = ba * fa
        r1 = x + mix_a * (ha - x)
        f1 = lax.rsqrt(mean_rows(r1 * r1) + EPSILON)
        return x, ba, fa, ha, f1, r1 * f1

    def norm_step(c, carry):
        at = rows(c, CH)
        _, ba, _, _, _, hidden = first_norm(at)
        add_stat(3, ba * ba)
        hid[at, :] = hidden
        h1[at, :] = hidden.astype(BF16)
        return carry

    lax.fori_loop(0, 256 // CH, norm_step, 0)

    def spread(ref):
        return send(ref.at[block(0)], ref.at[block(2)], ynb), send(
            ref.at[block(0)], ref.at[block(1)], core
        )

    def relay(ref, from_ynb):
        from_ynb.wait_recv()
        return send(ref.at[block(2)], ref.at[block(3)], core)

    h1_y, h1_core = spread(h1)
    take_gate.hop()
    take_gate.forward_one(4)
    take_down.start_near()
    take_gate.forward_one(2)
    h1_far = relay(h1, h1_y)
    take_gate.forward_one(6)
    take_down.hop()
    take_up.finish()
    h1_core.wait_recv()
    h1_far.wait_recv()
    take_gate.finish()

    def up_step(r, carry):
        at = rows(r)
        hidden = h1[at, :]
        u_raw = nn(hidden, wu[...])
        g_raw = nn(hidden, wg[...])
        gate = g_raw * gain_v
        silu = gate / (1.0 + jnp.exp(-gate))
        ur[at, :] = u_raw.astype(BF16)
        gr[at, :] = g_raw.astype(BF16)
        inn[at, :] = (u_raw * gain_u * silu).astype(BF16)
        return carry

    lax.fori_loop(0, 4, up_step, 0)

    class Reduce:
        def __init__(self, which, before, make):
            self.which, self.before, self.make = which, before, make
            self.copies = {}

        def run(self, order):
            for r in order:
                self.step(r)

        def step(self, r):
            k = self.which
            if r in self.before.copies:
                before = self.before.copies[r]
                for copy in before if isinstance(before, list) else [before]:
                    sent(copy)
            self.make(r)
            if r == 3:
                self.copies[3] = send(part.at[block(3)], from_core3.at[k], core)
            elif r == 2:
                self.copies[3].wait_recv()
                self.copies[2] = []
                for c in range(4):
                    here, there = pl.ds(512 + c * 64, 64), pl.ds(c * 64, 64)
                    part[here, :] = (
                        part[here, :].astype(F32) + from_core3[k, there, :].astype(F32)
                    ).astype(BF16)
                    self.copies[2].append(send(part.at[here], from_y.at[k, there], ynb))
            elif r == 1:
                self.copies[1] = send(part.at[block(1)], from_core1.at[k], core)

        def finish(self):
            self.copies[1].wait_recv()
            for copy in self.copies[2]:
                copy.wait_recv()

        def at(self, where):
            k = self.which
            return (
                part[where, :].astype(F32)
                + from_core1[k, where, :].astype(F32)
                + from_y[k, where, :].astype(F32)
            )

    class ReduceColumns:
        def __init__(self):
            self.copies = {r: [] for r in (1, 2, 3)}
            self.columns = []

        def step(self, k):
            cols = rows(lax.div(flip(d, 2 * k), 2))
            part[:, cols] = nt(inn[...], wd[cols, :]).astype(BF16)
            self.columns.append(cols)
            self.copies[3].append(send(part.at[block(3), cols], from_core3.at[0, :, cols], core))
            self.copies[1].append(send(part.at[block(1), cols], from_core1.at[0, :, cols], core))

        def pass_on(self, parts=1):
            done = len(self.copies[2])
            cols = self.columns[done]
            self.copies[3][done].wait_recv()
            count = 256 // parts
            for c in range(parts):
                here, there = pl.ds(512 + c * count, count), pl.ds(c * count, count)
                part[here, cols] = (
                    part[here, cols].astype(F32) + from_core3[0, there, cols].astype(F32)
                ).astype(BF16)
                self.copies[2].append(
                    send(part.at[here, cols], from_y.at[0, there, cols], ynb)
                )

        def finish(self):
            for copy in self.copies[1] + self.copies[2][:-4]:
                copy.wait_recv()

        def finish_rows(self, c):
            self.copies[2][c - 4].wait_recv()

        at = Reduce.at
        which = 0

    sum_m = ReduceColumns()
    sum_m.step(0)
    take_down.z[2].wait_recv()
    sum_m.step(1)
    sum_m.pass_on()
    sum_m.step(2)
    sum_m.pass_on()
    take_down.straight.wait_recv()
    sum_m.step(3)
    sum_m.pass_on()
    sum_m.pass_on(4)
    sum_m.finish()

    def loss_step(c, carry):
        at = rows(c, CH)
        bm = sum_m.at(at)
        hidden = hid[at, :]
        fm = lax.rsqrt(mean_rows(bm * bm) + EPSILON)
        hm = bm * fm
        r2 = hidden + mix_m * (hm - hidden)
        f2 = lax.rsqrt(mean_rows(r2 * r2) + EPSILON)
        result = r2 * f2
        layer_out[at, :] = result.astype(BF16)
        up = cot[at, :].astype(F32)
        grad = f2 * (up - result * mean_rows(up * result))
        dr2[at, :] = grad
        add_stat(1, grad * (hm - hidden))
        add_stat(4, bm * bm)
        add_stat(5, r2 * r2)
        c_m = mix_m * grad
        db[at, :] = (fm * (c_m - hm * mean_rows(c_m * hm))).astype(BF16)
        return carry

    class Spread:
        def __init__(self, ref):
            self.ref, self.y, self.core = ref, [], []

        def piece(self, r, c):
            return self.ref.at[pl.ds(r * 256 + c * 64, 64)]

        def start(self, c):
            self.y.append(send(self.piece(0, c), self.piece(2, c), ynb))
            self.core.append(send(self.piece(0, c), self.piece(1, c), core))

        def relay(self, c):
            self.y[c].wait_recv()
            self.core.append(send(self.piece(2, c), self.piece(3, c), core))

    db_rows = Spread(db)
    for c in range(4):
        sum_m.finish_rows(c)
        lax.fori_loop(c * (64 // CH), (c + 1) * (64 // CH), loss_step, 0)
        db_rows.start(c)

    class AlongZ:
        def __init__(self, view, landing):
            self.view, self.landing = view, landing
            self.at6, self.relay_at = number(), number()
            self.z = {}

        def far_copies(self):
            shard = self.view(flip(d, 6))
            return (
                describe(shard, self.landing.at[2], z_peer[6], self.at6, self.at6),
                describe(shard, self.landing.at[3], z_peer[2], self.relay_at, self.relay_at),
            )

        def start_far(self):
            straight, over = self.far_copies()
            pl.when(inner)(straight.start)
            pl.when(outer)(over.start)

        def push(self, k):
            shard = self.view(flip(d, 2 * k))
            if k == 3:
                self.start_far()
                self.straight, self.relay = self.far_copies()
            elif k == 2:

                @pl.when(inner)
                def _():
                    self.relay.wait_recv()
                    shard[...] = (shard[...].astype(F32) + self.landing[3].astype(F32)).astype(BF16)

                self.z[2] = send(shard, self.landing.at[1], z_peer[4])
            else:
                self.z[1] = send(shard, self.landing.at[0], z_peer[2])

        def total_into(self, out):
            self.z[1].wait_recv()
            self.z[2].wait_recv()
            out[...] = (
                self.view(d)[...].astype(F32)
                + self.landing[0].astype(F32)
                + self.landing[1].astype(F32)
            ).astype(out.dtype)

            @pl.when(inner)
            def _():
                self.straight.wait_recv()
                out[...] = (out[...].astype(F32) + self.landing[2].astype(F32)).astype(out.dtype)

        def settle(self):
            pl.when(inner)(self.straight.wait_send)
            pl.when(outer)(self.relay.wait_send)

    class Scatter(AlongZ):
        def __init__(self, view, from_x, landing):
            super().__init__(view, landing)
            self.from_x = from_x
            self.x = {}

        def ship(self, k):
            self.x[k] = send(self.view(flip(d, 2 * k + 1)), self.from_x.at[k], xnb)

        def ship_as_made(self, make, also=None):
            numbers = [number() for _ in range(4)]

            def copy_of(k, shard):
                at = numbers[0] + k
                return describe(self.view(shard), self.from_x.at[k], xnb, at, at)

            def step(n, carry):
                k = (7 - 2 * n + n // 2) % 4
                pair = mixed(z, k)
                make(rows(pair))
                copy_of(k, 2 * pair + 1 - lax.rem(d, 2)).start()
                if also is not None:
                    pl.when(n == 0)(also)
                return carry

            lax.fori_loop(0, 4, step, 0)
            for k in range(4):
                self.x[k] = copy_of(k, flip(d, 2 * k + 1))
                issued.append(self.x[k])

        def fold(self, k):
            self.x[k].wait_recv()
            own = self.view(flip(d, 2 * k))
            own[...] = (own[...].astype(F32) + self.from_x[k].astype(F32)).astype(BF16)
            if k in (1, 3):
                self.push(k)

    def weight_grad(left, right, out, scatter, also=None):
        def make(at):
            out[at, :] = tn(left[:, at], right[...]).astype(BF16)

        scatter.ship_as_made(make, also)

    def make_hidden(r):
        at = block(r)
        d_inner_f32[...] = nn(db[at, :], wd[...])

        def inner_step(c, carry):
            here = rows(c, CH)
            where = pl.ds(pl.multiple_of(r * 256 + c * CH, CH), CH)
            d_inner = d_inner_f32[here, :]
            u_raw = ur[where, :].astype(F32)
            g_raw = gr[where, :].astype(F32)
            gate = g_raw * gain_v
            sig = 1.0 / (1.0 + jnp.exp(-gate))
            up = u_raw * gain_u
            d_up = d_inner * (gate * sig)
            d_gate = d_inner * up * (sig * (1.0 + gate * (1.0 - sig)))
            add_stat(6, d_up * u_raw)
            add_stat(7, d_gate * g_raw)
            ur[where, :] = (d_up * gain_u).astype(BF16)
            gr[where, :] = (d_gate * gain_v).astype(BF16)
            return carry

        lax.fori_loop(0, 256 // CH, inner_step, 0)
        part[at, :] = (nt(ur[at, :], wu[...]) + nt(gr[at, :], wg[...])).astype(BF16)

    forward_sends = len(issued)
    sum_h = Reduce(1, sum_m, make_hidden)
    for copy in db_rows.core[:4]:
        copy.wait_recv()
    sum_h.step(1)
    db_rows.relay(0)
    db_rows.relay(1)
    sum_h.step(0)
    db_rows.relay(2)
    db_rows.relay(3)
    for copy in db_rows.core[4:]:
        copy.wait_recv()
    half = slice(0, 512), slice(512, 1024)

    def down_pair(index):
        return gd.at[rows(lax.div(index, 2)), half[0]]

    def down_shard(index):
        return gd.at[rows(index, 128), half[1]]

    sum_down = AlongZ(down_pair, z_down)
    sum_down_x = Scatter(down_shard, x_down_x, z_down_x)

    weight_grad(db, inn, gd, sum_down_x, sum_down.start_far)
    sum_down.straight, sum_down.relay = sum_down.far_copies()
    sum_h.run((3, 2))

    gu, gg, go = wd, wu, wg
    for gather in (take_down, take_up, take_gate):
        gather.release()
    sum_up = Scatter(rows_of(gu), x_up, z_up)
    sum_gate = Scatter(rows_of(gg), x_gate, z_gate)
    weight_grad(h1, ur, gu, sum_up)
    sum_down.push(2)
    sum_down.push(1)
    weight_grad(h1, gr, gg, sum_gate)
    sum_down_x.fold(3)
    sum_down_x.fold(1)

    def mid_step(c, carry):
        at = rows(c, CH)
        x, _, fa, ha, f1, hidden = first_norm(at)
        d_hidden = (1.0 - mix_m) * dr2[at, :] + sum_h.at(at)
        grad = f1 * (d_hidden - hidden * mean_rows(d_hidden * hidden))
        dr1[at, :] = grad
        add_stat(0, grad * (ha - x))
        c_a = mix_a * grad
        dba[at, :] = (fa * (c_a - ha * mean_rows(c_a * ha))).astype(BF16)
        return carry

    sum_h.copies[1].wait_recv()
    for c in range(4):
        sum_h.copies[2][c].wait_recv()
        lax.fori_loop(c * (64 // CH), (c + 1) * (64 // CH), mid_step, 0)

    dat_sends = []
    for r in (2, 3, 1, 0):
        slot = flip(t, r)
        weight = wo[pl.ds(2 * slot, 2)].reshape(256, 1024)
        value = nt(dba[...], weight).astype(BF16)
        if r:
            dat[r - 1] = value
            dat_sends.append(send(dat.at[r - 1], dao.at[block(r)], tensor_peer[r]))
        else:
            dao[block(0), :] = value
    for slot in range(4):
        g = tn(ato[slot], dba[...]).astype(BF16)
        for q in range(8):
            start = (q % 4) * 256 + (2 * slot + q // 4) * 32
            go[start : start + 32, :] = g[q * 32 : (q + 1) * 32, :]

    def go_rows(r):
        return rows(flip(t, r))

    go_core3 = send(go.at[go_rows(3)], o_core3, core)
    go_core1 = send(go.at[go_rows(1)], o_core1, core)
    sum_down_x.fold(2)
    sum_down_x.push(2)
    sum_down_x.fold(0)
    sum_up.fold(3)
    sum_up.fold(1)
    go_core3.wait_recv()
    go[go_rows(2), :] = (go[go_rows(2), :].astype(F32) + o_core3[...].astype(F32)).astype(BF16)
    go_y = send(go.at[go_rows(2)], o_y, ynb)

    head_rows = jnp.where(
        lax.broadcasted_iota(jnp.int32, (8, 256), 0)
        == lax.div(lax.broadcasted_iota(jnp.int32, (8, 256), 1), HEAD_DIM),
        1.0,
        0.0,
    ).astype(BF16)
    for copy in att_sends:
        sent(copy)

    def ready_step(r, carry):
        at = rows(r)
        scaled = (dao[at, :].astype(F32) * linv[at, :]).astype(BF16)
        dao[at, :] = scaled
        product = scaled.astype(F32) * att[at, :].astype(F32)
        high = product.astype(BF16)
        low = (product - high.astype(F32)).astype(BF16)
        delta[r] = nt(head_rows, high) + nt(head_rows, low)
        return carry

    key_grads, query_grads = branch, hid
    seen = jnp.concatenate([row_id <= col_id] * 2, axis=1)

    def lanes_of(r, half=0):
        return pl.ds(pl.multiple_of(r * 128 + half * 512, 128), 128)

    def attend_back(pair, query_r, key_r, visible):
        query_at, key_at = rows(query_r), rows(key_r)
        q = two_heads(qkv[pair, query_at, 0:128])
        do = two_heads(dao[query_at, pair * 128 : pair * 128 + 128])
        keys = qkv[pair, key_at, 128:256]
        e = visible(jnp.exp2(nt(keys, q) * exp_scale))
        d_prob = nt(qkv[pair, key_at, 256:384], do)
        shift = jnp.concatenate(
            [delta[query_r, 2 * pair + h : 2 * pair + h + 1, :] for h in range(2)], axis=1
        )
        d_score = (e * (d_prob - shift)).astype(BF16)
        key_grads[:, lanes_of(key_r)] += nn(d_score, q)
        key_grads[:, lanes_of(key_r, 1)] += nn(e.astype(BF16), do)
        query_grads[:, lanes_of(query_r)] += one_of_two(tn(d_score, keys))

    def diagonal(pair):
        def diagonal_step(r, carry):
            attend_back(pair, r, r, lambda e: jnp.where(seen, e, 0.0))
            return carry

        return diagonal_step

    def below(pair):
        def below_step(n, carry):
            i = 1 + lax.div(n, 3) + lax.div(n + 4, 5)
            j = n - lax.div(i * (i - 1), 2)
            apart = (lax.div(i, 2) - lax.div(j, 2)).astype(F32)
            factor = 1.0 - apart + apart * whole
            attend_back(pair, mixed(i, t), mixed(j, t), lambda e: e * factor)
            return carry

        return below_step

    def clear():
        key_grads[...] = jnp.zeros_like(key_grads)
        query_grads[...] = jnp.zeros_like(query_grads)

    def qkv_back(pair):
        scale = math.sqrt(HEAD_DIM)
        gain = gain_pair(pair)
        column = pl.ds(pl.multiple_of(t * 256 + pair * 128, 128), 128)

        def back_qkv_step(r, carry):
            at = rows(r)
            y = raw[pair, at, :]
            factor = lax.rsqrt(head_sum(y * y) + EPSILON)
            w = y * factor
            grad = (
                jnp.concatenate([query_grads[:, lanes_of(r)], key_grads[:, lanes_of(r)]], axis=1)
                * scale
            )
            both = jnp.sum(grad * w, axis=0, keepdims=True)
            stats[2:3, column] = stats[2:3, column] + both[:, :128] + both[:, 128:]
            c = grad * gain
            dqkv[pair, at, :256] = (factor * (c - w * head_sum(c * w))).astype(BF16)
            dqkv[pair, at, 256:] = key_grads[:, lanes_of(r, 1)].astype(BF16)
            return carry

        lax.fori_loop(0, 4, back_qkv_step, 0)

    gq = qkv

    def qkv_shard(pair):
        return lambda index: gq.at[pair, rows(index, 128), :]

    sum_qkv = [Scatter(qkv_shard(pair), x_qkv.at[pair], z_qkv.at[pair]) for pair in range(2)]

    def qkv_weight(pair):
        def make(at):
            gq[pair, at, :] = tn(tok[:, at], dqkv[pair]).astype(BF16)

        sum_qkv[pair].ship_as_made(make)

    clear()
    dat_sends[2].wait_recv()
    lax.fori_loop(0, 2, ready_step, 0)
    lax.fori_loop(0, 2, diagonal(0), 0)
    sum_up.fold(2)
    dat_sends[0].wait_recv()
    dat_sends[1].wait_recv()
    lax.fori_loop(2, 4, ready_step, 0)
    lax.fori_loop(2, 4, diagonal(0), 0)
    sum_up.push(2)
    sum_up.fold(0)
    lax.fori_loop(0, 6, below(0), 0)
    qkv_back(0)
    qkv_weight(0)
    clear()
    sum_gate.fold(3)
    sum_gate.fold(1)
    lax.fori_loop(0, 4, diagonal(1), 0)
    sum_gate.fold(2)
    sum_gate.push(2)
    lax.fori_loop(0, 6, below(1), 0)
    qkv_back(1)
    qkv_weight(1)
    go_core1.wait_recv()
    go_y.wait_recv()
    osum[...] = (
        go[go_rows(0), :].astype(F32) + o_core1[...].astype(F32) + o_y[...].astype(F32)
    ).astype(BF16)
    sum_out = Scatter(rows_of(osum, 32), x_out, z_out)
    for k in (3, 1, 2, 0):
        sum_out.ship(k)
    sum_gate.fold(0)
    sum_down.total_into(down_pair(d))
    down_x = send(gd.at[rows(flip(d, 1), 128), half[0]], x_down, xnb)

    small_back = [send(stats, s_tensor.at[r - 1], tensor_peer[r]) for r in (1, 2, 3)]

    def make_tokens(r):
        part[block(r), :] = (
            nt(dqkv[0, block(r), :], wq[0]) + nt(dqkv[1, block(r), :], wq[1])
        ).astype(BF16)

    sum_t = Reduce(2, sum_h, make_tokens)
    sum_t.run((3, 2))
    for k in (3, 1, 0, 2):
        sum_qkv[0].fold(k)
    sum_t.run((1, 0))
    sum_qkv[0].push(2)
    for copy in small_back:
        copy.wait_recv()
    over_tensor = s_tensor[0] + s_tensor[1] + s_tensor[2]
    shared = lax.broadcasted_iota(jnp.int32, (8, 1024), 0) < 6
    s_x[0] = stats[...] + jnp.where(shared, over_tensor, 0.0)
    stat_x = send(s_x.at[0], s_x.at[1], xnb)
    for k in (3, 1, 0, 2):
        sum_qkv[1].fold(k)
    sum_qkv[1].push(2)
    for k in (3, 1, 2, 0):
        sum_out.fold(k)
    sum_out.push(2)

    outgoing = []

    def put(src, dst):
        outgoing.append(bring(src, dst))

    put(layer_out, layer_hbm)
    for gather in (take_qkv, take_small, take_out):
        gather.release()
    for copy in issued[:forward_sends]:
        sent(copy)
    sum_down_x.total_into(grad_down.at[:, half[1]])
    sum_up.total_into(grad_up)
    put(grad_up, up_hbm)
    sum_gate.total_into(grad_gate)
    put(grad_gate, gate_hbm)
    stat_x.wait_recv()
    s_z[0] = s_x[0] + s_x[1]
    stat_z = [send(s_z.at[0], s_z.at[k], z_peer[2 * k]) for k in (1, 2, 3)]
    for pair in range(2):
        sum_qkv[pair].total_into(q_sum.at[pair])
    q_low[...] = q_sum[...].astype(BF16)
    q_sends = [
        send(q_low.at[:, rows(flip(t, r), 32), :], q_piece.at[t], tensor_peer[r]) for r in (2, 3, 1)
    ]
    q_piece[t] = q_low[:, rows(t, 32), :]
    sum_t.finish()

    def last_step(c, carry):
        at = rows(c, CH)
        grad_tokens[at, :] = ((1.0 - mix_a) * dr1[at, :] + sum_t.at(at)).astype(BF16)
        return carry

    lax.fori_loop(0, 256 // CH, last_step, 0)
    put(grad_tokens, tokens_hbm)
    sum_out.total_into(grad_out)
    put(grad_out, out_hbm)
    down_x.wait_recv()
    grad_down[:, half[0]] = gd[rows(d, 128), half[0]].astype(F32) + x_down[...].astype(F32)
    put(grad_down, down_hbm)
    for copy in stat_z:
        copy.wait_recv()
    stats_sum[...] = s_z[0] + s_z[1] + s_z[2] + s_z[3]
    put(stats_sum, stats_hbm)
    for copy in q_sends:
        copy.wait_recv()
    for slot in range(4):
        for pair, j in parts_of_qkv:
            start = j * 1024 + slot * 256 + pair * 128
            grad_qkv[:, start : start + 128] = q_piece[
                slot, pair, :, j * 128 : j * 128 + 128
            ].astype(F32)
    put(grad_qkv, qkv_hbm)
    for scatter in (sum_down, sum_down_x, sum_up, sum_gate, sum_out, *sum_qkv):
        scatter.settle()
    for copy in issued:
        sent(copy)
    for copy in outgoing:
        copy.wait()


def finish_kernel(entries, *refs):
    taken, given, held, sems = refs[:8], refs[8:21], refs[21:35], refs[35]
    pull = [pltpu.make_async_copy(taken[i], held[i], sems.at[i]) for i in range(8)]
    push = [
        pltpu.make_async_copy(held[i if i < 7 else i + 1], given[i], sems.at[8 + i])
        for i in range(13)
    ]
    for copy in (pull[7], *pull[:7]):
        copy.start()
    stats, outs = held[7], held[8:]
    s_qk, alpha_a, alpha_m, s_u, s_v, stream = outs
    index = lax.axis_index("dp") * lax.axis_size("tensor") + lax.axis_index("tensor")
    piece = s_qk.shape[0]
    pick = lax.broadcasted_iota(jnp.int32, (1024, piece), 0) == (
        lax.broadcasted_iota(jnp.int32, (1024, piece), 1) + index * piece
    )
    pull[7].wait()
    own = lax.dot_general(
        stats[0:3, :],
        jnp.where(pick, 1.0, 0.0),
        (((1,), (0,)), ((), ())),
        precision=lax.Precision.HIGHEST,
        preferred_element_type=F32,
    )
    for ref, row in ((alpha_a, 0), (alpha_m, 1), (s_qk, 2)):
        ref[...] = own[row]
    s_u[...] = stats[6, :]
    s_v[...] = stats[7, :]
    stream[...] = jnp.sqrt(jnp.sum(stats[3:6, :], axis=1) / entries)
    for copy in push[7:]:
        copy.start()
    for i in range(7):
        pull[i].wait()
        push[i].start()
    for copy in push:
        copy.wait()


def fits(mesh):
    return dict(mesh.shape) == {"dp": 8, "tensor": 4}


def fused(
    tokens, cotangent, bucket_start, w_qkv, w_out, s_qk, alpha_a, alpha_m, w_up, w_gate, w_down, s_u, s_v
):
    n_rows, width = tokens.shape
    piece = s_qk.shape[0]
    hbm = pl.BlockSpec(memory_space=pl.ANY)
    bf = lambda *shape: pltpu.VMEM(shape, BF16)
    fl = lambda *shape: pltpu.VMEM(shape, F32)
    large = [
        jax.ShapeDtypeStruct(shape, kind)
        for shape, kind in (
            ((256, 1024), BF16), ((256, 1024), BF16), ((32, 3072), F32), ((32, 1024), F32),
            ((128, 1024), F32), ((128, 1024), F32), ((128, 1024), F32),
        )
    ]
    vector = lambda leaf: pltpu.VMEM(leaf.shape, leaf.dtype)
    scratch = [
        *[pltpu.VMEM(leaf.shape, leaf.dtype) for leaf in large], fl(8, 1024),
        pltpu.SMEM(bucket_start.shape, jnp.int32), vector(s_qk), vector(alpha_a), vector(alpha_m),
        vector(s_u), vector(s_v),
        bf(1024, 1024), bf(256, 1024), bf(2, 1024, 384), bf(8, 4, 32, 1024), bf(1024, 1024),
        bf(1024, 1024), bf(1024, 1024), bf(16, 128), bf(3, 16, 128), bf(16, 1024), fl(16, 1024),
        fl(2, 1024, 256), bf(2, 1024, 384), fl(1024, 256), bf(1024, 256), bf(4, 256, 256),
        fl(256, 1024), fl(256, 1024), bf(1024, 1024), bf(1024, 1024), bf(1024, 1024), bf(1024, 1024),
        bf(1024, 1024), bf(3, 256, 1024), bf(3, 256, 1024), bf(3, 256, 1024),
        fl(256, 1024), fl(256, 1024), fl(256, 1024), bf(1024, 1024), bf(256, 1024), bf(3, 256, 256),
        bf(1024, 256), bf(2, 1024, 384), fl(4, 8, 256),
        bf(1024, 1024), bf(128, 512), bf(4, 128, 512), bf(4, 128, 1024), bf(4, 128, 1024),
        bf(2, 4, 128, 384), bf(4, 32, 1024), bf(4, 256, 512), bf(4, 128, 512), bf(4, 128, 1024), bf(4, 128, 1024), bf(2, 4, 128, 384),
        bf(4, 32, 1024), bf(256, 1024), bf(256, 1024), bf(256, 1024), bf(256, 1024),
        fl(2, 128, 384), bf(2, 128, 384), bf(4, 2, 32, 384), fl(8, 1024), fl(3, 8, 1024), fl(2, 8, 1024), fl(4, 8, 1024),
        pltpu.SemaphoreType.DMA((COPIES,)), pltpu.SemaphoreType.DMA((COPIES,)),
        pltpu.SemaphoreType.DMA((32,)),
    ]
    *big, stats = pl.pallas_call(
        fused_kernel,
        out_shape=[*large, jax.ShapeDtypeStruct((8, 1024), F32)],
        in_specs=[hbm] * 13,
        out_specs=[hbm] * 8,
        scratch_shapes=scratch,
        compiler_params=pltpu.CompilerParams(
            collective_id=0, has_side_effects=True, vmem_limit_bytes=VMEM_BYTES
        ),
        cost_estimate=pl.CostEstimate(
            flops=27_000_000_000, bytes_accessed=8_000_000, transcendentals=10_000_000
        ),
    )(
        tokens, cotangent, bucket_start, w_qkv, w_out, s_qk, alpha_a, alpha_m,
        w_up, w_gate, w_down, s_u, s_v,
    )
    entries = n_rows * width * lax.axis_size("dp") * lax.axis_size("tensor")
    flat = [(piece,), (piece,), (piece,), (1024,), (1024,), (3,)]
    *big, g_qk, g_a, g_m, g_u, g_v, stream = pl.pallas_call(
        functools.partial(finish_kernel, float(entries)),
        out_shape=[*large, *[jax.ShapeDtypeStruct(shape, F32) for shape in flat]],
        in_specs=[hbm] * 8,
        out_specs=[hbm] * 13,
        scratch_shapes=[
            *[pltpu.VMEM(leaf.shape, leaf.dtype) for leaf in large],
            fl(8, 1024),
            *[fl(*shape) for shape in flat],
            pltpu.SemaphoreType.DMA((21,)),
        ],
    )(*big, stats)
    return (*big[:4], g_qk, g_a, g_m, *big[4:], g_u, g_v, stream)


def solution(mesh):
    body = fused if fits(mesh) else local
    return jax.shard_map(
        body,
        mesh=mesh,
        in_specs=(
            P(("dp", "tensor"), None),
            P(("dp", "tensor"), None),
            P(),
            P(("dp", "tensor"), None),
            P(("dp", "tensor"), None),
            P(("dp", "tensor")),
            P(("dp", "tensor")),
            P(("dp", "tensor")),
            P("dp", "tensor"),
            P("dp", "tensor"),
            P("dp", "tensor"),
            P("tensor"),
            P("tensor"),
        ),
        out_specs=(
            P(("dp", "tensor"), None),
            P(("dp", "tensor"), None),
            P(("dp", "tensor"), None),
            P(("dp", "tensor"), None),
            P(("dp", "tensor")),
            P(("dp", "tensor")),
            P(("dp", "tensor")),
            P("dp", "tensor"),
            P("dp", "tensor"),
            P("dp", "tensor"),
            P("tensor"),
            P("tensor"),
            P(),
        ),
        check_vma=False,
    )
```
